32 devices in a mesh: grp: 2 (over x), row: 8 (over z, y), col: 2 (over core).
Axes of the slice: x: 2, y: 2, z: 4, core: 2. Of those that a mesh axis runs over, the one named last changes fastest.
Arguments:
- queries: bfloat16 [8192, 2048], P(('grp', 'row'), 'col'), parts along dimension 0, may hold values from -34 to 34
- keys: bfloat16 [8192, 1024], P(('grp', 'row'), 'col'), parts along dimension 0, may hold values from -34 to 34
- values: bfloat16 [8192, 1024], P(('grp', 'row'), 'col'), parts along dimension 0, may hold values from -6 to 6
- out_proj: bfloat16 [2048, 5376], P(('col', 'row'))
- post_gain: float32 [5376], P('col'), may hold values from 0.1 to 1.9
- mean_vec: float32 [5376], P('col'), may hold values from -5 to 5
- erase_in: float32 [5376, 64], P('col'), may hold values from -0.078125 to 0.078125
- erase_out: float32 [5376, 64], P('col'), may hold values from -0.375 to 0.375
Outputs:
- erased: bfloat16 [8192, 5376], P(('grp', 'row'), 'col'), parts along dimension 0
The draws below stay inside these ranges and needn't reach their ends.
There are 2 independent parts, one for each index of `grp`. The reference program is written for one: setup_inputs(seed, part) draws one part's arguments, and reference() takes and returns one part's arrays. A program takes and returns all parts, laid end to end along the dimension named above; an argument that names none is the same for every part. Nothing has to cross between parts.
All inputs are finite; a program needn't handle non-finite values.
Results may differ from the reference program's by a relative error of at most 0.012.
The reference program's roundings to bfloat16 on the way (of `q_rot`, `k_rot`, `probs` and `attended`) count: a program that leaves them out, or rounds other values in their place, can miss the bound.
Values may be sent and summed in bfloat16 or wider, within the bound.
No kernel may reach another device: no remote copies, remote signals or barrier semaphores. Data moves between devices by JAX's collectives and lax.ppermute only.
A program may use at most 128 MiB of HBM per device.

```python
import jax
import jax.numpy as jnp
from jax import lax

D = 5376
HD = 128
HEADS = 16
KV = 8
WINDOW = 1024
RANK = 64
TOK_DEV = 512
TOKENS = 4096
N_ROW = 8


def base_field(key, shape):
    return jnp.clip(jax.random.normal(key, shape, jnp.float32), -4.0, 4.0)


def draw_queries(key, part):
    base_draw = base_field(jax.random.fold_in(key, 11), (TOKENS, HEADS, HD))
    return base_draw.reshape(TOKENS, HEADS * HD).astype(jnp.bfloat16)


def draw_keys(key, part):
    base_draw = base_field(jax.random.fold_in(key, 13), (TOKENS, KV, HD))
    return base_draw.reshape(TOKENS, KV * HD).astype(jnp.bfloat16)


def draw_out_proj(key, part):
    columns = jnp.arange(D).astype(jnp.float32)
    ramp = jnp.exp(jnp.log(3.0) * columns / D)
    base_draw = jnp.clip(jax.random.normal(jax.random.fold_in(key, 5), (HEADS * HD, D), jnp.float32), -5.0, 5.0)
    scaled = base_draw * ramp[None, :] * float(HEADS * HD) ** (-0.5) / 1.8
    return scaled.astype(jnp.bfloat16)


def shard_levels(key, extent, pieces, smallest, top_value):
    level = 1.0
    for axis_at, shards_of in pieces:
        steps = jax.random.uniform(jax.random.fold_in(jax.random.fold_in(key, 6), axis_at), (shards_of,), jnp.float32, smallest / len(pieces), top_value / len(pieces))
        level = level * jnp.repeat(jnp.exp(steps), extent[axis_at] // shards_of).reshape((-1,) + (1,) * (len(extent) - 1 - axis_at))
    return level


def centred(rng, shape, scale, reach, shards=(), kind=jnp.bfloat16):
    values = scale * jax.random.normal(rng, shape, jnp.float32)
    if shards:
        values = values * shard_levels(rng, shape, shards, -0.22, 0.18)
    return jnp.clip(values, -reach, reach).astype(kind)


def setup_inputs(seed: int = 0, part: int = 0) -> dict:
    splits = jax.random.split(jax.random.key(seed), 9)
    part_keys = jax.random.split(jax.random.fold_in(splits[8], part), 9)
    return {
        "queries": draw_queries(jax.random.fold_in(jax.random.fold_in(splits[8], part), 71), part),
        "keys": draw_keys(jax.random.fold_in(jax.random.fold_in(splits[8], part), 71), part),
        "values": centred(part_keys[2], (TOKENS, KV * HD), 1.0, 6.0, ((0, 8), (1, 2))),
        "out_proj": draw_out_proj(jax.random.fold_in(splits[8], 71), part),
        "post_gain": jnp.clip(1.0 + 0.18 * jax.random.normal(splits[4], (D,), jnp.float32), 0.1, 1.9),
        "mean_vec": centred(splits[5], (D,), 1.0, 5.0, ((0, 2),), jnp.float32),
        "erase_in": centred(splits[6], (D, RANK), D ** -0.5, 0.078125, ((0, 2),), jnp.float32),
        "erase_out": centred(splits[7], (D, RANK), (4 * RANK) ** -0.5, 0.375, ((0, 2),), jnp.float32),
    }


query_scale = 168.0 ** (-0.5)
norm_eps = 1e-06
rope_base = 10000.0

def rotate(field, positions):
    half_dim = HD // 2
    inverse = jnp.exp(-(2.0 * jnp.arange(half_dim, dtype=jnp.float32) / HD) * jnp.log(jnp.float32(rope_base)))
    angles = positions[:, None] * inverse[None, :]
    cosine = jnp.cos(angles)[:, None, :]
    sine = jnp.sin(angles)[:, None, :]
    wide = field.astype(jnp.float32)
    first = wide[..., :half_dim]
    second = wide[..., half_dim:]
    return jnp.concatenate([first * cosine - second * sine, second * cosine + first * sine], -1).astype(jnp.bfloat16)

def reference(queries, keys, values, out_proj, post_gain, mean_vec, erase_in, erase_out):
    group = HEADS // KV
    positions = jnp.arange(TOKENS).astype(jnp.float32)
    q_rot = rotate(queries.reshape(TOKENS, HEADS, HD), positions)
    k_rot = rotate(keys.reshape(TOKENS, KV, HD), positions)
    val_heads = values.reshape(TOKENS, KV, HD)
    key_padded = jnp.pad(k_rot, ((WINDOW, 0), (0, 0), (0, 0)))
    val_padded = jnp.pad(val_heads, ((WINDOW, 0), (0, 0), (0, 0)))

    def block(block_index):
        first_row = (block_index * TOK_DEV).astype(jnp.int32)
        query_block = lax.dynamic_slice_in_dim(q_rot, first_row, TOK_DEV, 0).reshape(TOK_DEV, KV, group, HD)
        key_block = lax.dynamic_slice_in_dim(key_padded, first_row, WINDOW + TOK_DEV, 0)
        val_block = lax.dynamic_slice_in_dim(val_padded, first_row, WINDOW + TOK_DEV, 0)
        scores = jnp.einsum('tkgd,skd->kgts', query_block.astype(jnp.float32), key_block.astype(jnp.float32)) * query_scale
        query_pos = first_row + jnp.arange(TOK_DEV, dtype=jnp.int32)
        key_pos = first_row - WINDOW + jnp.arange(WINDOW + TOK_DEV, dtype=jnp.int32)
        offsets = query_pos[:, None] - key_pos[None, :]
        allowed = ((key_pos >= 0)[None, :] & (offsets >= 0) & (offsets < WINDOW))[None, None]
        scores = jnp.where(allowed, scores, -1e+30)
        row_max = lax.optimization_barrier(jnp.max(scores, axis=-1, keepdims=True))
        weights = jnp.where(allowed, jnp.exp(scores - row_max), 0.0)
        probs = (weights / lax.optimization_barrier(jnp.sum(weights, axis=-1, keepdims=True))).astype(jnp.bfloat16)
        attended = jnp.einsum('kgts,skd->tkgd', probs.astype(jnp.float32), val_block.astype(jnp.float32)).astype(jnp.bfloat16)
        attended = attended.reshape(TOK_DEV, HEADS * HD)
        hidden = jnp.dot(attended, out_proj, preferred_element_type=jnp.float32)
        inv_rms = lax.rsqrt(lax.optimization_barrier(jnp.mean(hidden * hidden, axis=-1, keepdims=True)) + norm_eps)
        normed = hidden * inv_rms * post_gain[None, :]
        erase_code = jnp.dot(normed - mean_vec[None, :], erase_in, precision=lax.Precision.HIGHEST)
        return (normed - jnp.dot(erase_code, erase_out.T, precision=lax.Precision.HIGHEST)).astype(jnp.bfloat16)
    blocks = lax.map(block, jnp.arange(N_ROW, dtype=jnp.int32))
    return blocks.reshape(TOKENS, D)
```

```python
import functools

import jax
import jax.numpy as jnp
from jax import lax
from jax.experimental import pallas as pl
from jax.experimental.pallas import tpu as pltpu
from jax.sharding import Mesh
from jax.sharding import PartitionSpec as P

HD = 128
WINDOW = 1024
RANK = 64

query_scale = 168.0 ** (-0.5)
norm_eps = 1e-06
rope_base = 10000.0
log2_e = 1.4426950408889634

CHUNKS = ((2, "B"), (3, "D"), (2, "B"))
TILE = 384

NT = (((1,), (1,)), ((), ()))


def split_high_low(value):
    high = lax.reduce_precision(value, 8, 7)
    return high.astype(jnp.bfloat16), (value - high).astype(jnp.bfloat16)


def rope_tables(first_position, count):
    half_dim = HD // 2
    inverse = jnp.exp(
        -(2.0 * jnp.arange(half_dim, dtype=jnp.float32) / HD) * jnp.log(jnp.float32(rope_base))
    )
    positions = (first_position + jnp.arange(count, dtype=jnp.int32)).astype(jnp.float32)
    angles = positions[:, None] * inverse[None, :]
    cosine, sine = jnp.cos(angles), jnp.sin(angles)
    return jnp.concatenate([cosine, cosine], 1), jnp.concatenate([-sine, sine], 1)


def attend_kernel(tok, group, direct, row_ref, q_ref, k0, k1, k2, v0, v1, v2, cos_ref, sin_ref, out_ref):
    tile = 256

    def turned(field, at):
        wide = field.astype(jnp.float32)
        cos, sin = cos_ref[at : at + tok, :], sin_ref[at : at + tok, :]
        return (wide * cos + pltpu.roll(wide, HD // 2, 1) * sin).astype(jnp.bfloat16)

    row = row_ref[0]
    bias0 = jnp.where(row >= 2, 0.0, -1e30).astype(jnp.float32)
    bias1 = jnp.where(row >= 1, 0.0, -1e30).astype(jnp.float32)
    key0, key1, key2 = turned(k0[...], 0), turned(k1[...], tok), turned(k2[...], 2 * tok)
    heads = [turned(q_ref[:, h * HD : (h + 1) * HD], 2 * tok) for h in range(group)]
    scale = query_scale * log2_e
    stacked = group * tile
    inner = lax.rem(lax.broadcasted_iota(jnp.int32, (stacked, tile), 0), tile)
    newer = lax.broadcasted_iota(jnp.int32, (stacked, tile), 1) > inner

    def dot_nt(a, b):
        return lax.dot_general(a, b, NT, preferred_element_type=jnp.float32)

    def dot(a, b):
        return jnp.dot(a, b, preferred_element_type=jnp.float32)

    for t in range(tok // tile):
        lo, hi = t * tile, (t + 1) * tile
        query = jnp.concatenate([h[lo:hi] for h in heads], 0)
        parts = [(dot_nt(query, key1) + bias1, v1[...])]
        if hi < tok:
            parts.append((dot_nt(query, key0[hi:]) + bias0, v0[hi:, :]))
        if lo > 0:
            parts.append((dot_nt(query, key2[:lo]), v2[:lo, :]))
        mixed = jnp.where(newer, dot_nt(query, key0[lo:hi]) + bias0, dot_nt(query, key2[lo:hi]))
        top = jnp.max(mixed, axis=1, keepdims=True)
        for part, _ in parts:
            top = jnp.maximum(top, jnp.max(part, axis=1, keepdims=True))
        top = top * scale
        weights = jnp.exp2(mixed * scale - top)
        total = jnp.sum(weights, axis=1, keepdims=True)
        older = jnp.where(newer, weights, 0.0)
        result = dot(older.astype(jnp.bfloat16), v0[lo:hi, :])
        result += dot((weights - older).astype(jnp.bfloat16), v2[lo:hi, :])
        for part, value in parts:
            weights = jnp.exp2(part * scale - top)
            total += jnp.sum(weights, axis=1, keepdims=True)
            result += dot(weights.astype(jnp.bfloat16), value)
        result = (result / total).astype(jnp.bfloat16)
        for h in range(group):
            block = result[h * tile : (h + 1) * tile]
            if direct:
                out_ref[h, lo:hi, :] = block
            else:
                out_ref[lo:hi, h * HD : (h + 1) * HD] = block


def attend(row, queries, key_blocks, val_blocks, cos, sin, direct):
    tok, kv_local = queries.shape[0], key_blocks[0].shape[1] // HD
    group = queries.shape[1] // HD // kv_local
    head_block = pl.BlockSpec((tok, HD), lambda g, r: (0, g))
    table = pl.BlockSpec((3 * tok, HD), lambda g, r: (0, 0))
    if direct:
        out_shape = (group, tok, kv_local * HD)
        out_spec = pl.BlockSpec((group, tok, HD), lambda g, r: (0, 0, g))
    else:
        out_shape = queries.shape
        out_spec = pl.BlockSpec((tok, group * HD), lambda g, r: (0, g))
    heads = kv_local * group
    return pl.pallas_call(
        functools.partial(attend_kernel, tok, group, direct),
        grid_spec=pltpu.PrefetchScalarGridSpec(
            num_scalar_prefetch=1,
            grid=(kv_local,),
            in_specs=[pl.BlockSpec((tok, group * HD), lambda g, r: (0, g))] + [head_block] * 6 + [table] * 2,
            out_specs=out_spec,
        ),
        out_shape=jax.ShapeDtypeStruct(out_shape, jnp.bfloat16),
        compiler_params=pltpu.CompilerParams(vmem_limit_bytes=48 * 2**20),
        cost_estimate=pl.CostEstimate(
            flops=heads * tok * 10 * tok * HD, bytes_accessed=6 * 2**20, transcendentals=heads * tok * 2 * tok
        ),
    )(row, queries, *key_blocks, *val_blocks, cos, sin)


def project_kernel(pick_ref, att_ref, w0, w1, w2, w3, gain_ref, in_a, in_b, hidden_ref, stat_ref):
    step = pl.program_id(0)
    total = None
    for n, piece in enumerate((w0, w1, w2, w3)):
        part = jnp.dot(
            att_ref[pick_ref[2 * n], pick_ref[2 * n + 1]], piece[...], preferred_element_type=jnp.float32
        )
        total = part if total is None else total + part
    hidden_ref[...] = total
    gained = total * gain_ref[...]
    high = gained.astype(jnp.bfloat16)
    low = (gained - high.astype(jnp.float32)).astype(jnp.bfloat16)
    code = jnp.dot(high, in_a[...], preferred_element_type=jnp.float32)
    code += jnp.dot(low, in_b[...], preferred_element_type=jnp.float32)
    code = code + pltpu.roll(code, RANK, 1)
    square = jnp.sum(total * total, axis=1, keepdims=True)
    lane = lax.broadcasted_iota(jnp.int32, code.shape, 1)
    stat = jnp.where(lane < RANK, code, square)

    @pl.when(step == 0)
    def _():
        stat_ref[...] = stat

    @pl.when(step > 0)
    def _():
        stat_ref[...] += stat


def project(pick, att, pieces, gain, in_a, in_b):
    tok, depth = att.shape[2], att.shape[3]
    count = pieces[0].shape[1]
    return pl.pallas_call(
        project_kernel,
        grid_spec=pltpu.PrefetchScalarGridSpec(
            num_scalar_prefetch=1,
            grid=(count // TILE,),
            in_specs=[pl.BlockSpec(att.shape, lambda j, r: (0, 0, 0, 0))]
            + [pl.BlockSpec((depth, TILE), lambda j, r: (0, j))] * 4
            + [pl.BlockSpec((1, TILE), lambda j, r: (0, j))]
            + [pl.BlockSpec((TILE, 2 * RANK), lambda j, r: (j, 0))] * 2,
            out_specs=[
                pl.BlockSpec((tok, TILE), lambda j, r: (0, j)),
                pl.BlockSpec((tok, 2 * RANK), lambda j, r: (0, 0)),
            ],
        ),
        out_shape=[
            jax.ShapeDtypeStruct((tok, count), jnp.float32),
            jax.ShapeDtypeStruct((tok, 2 * RANK), jnp.float32),
        ],
        compiler_params=pltpu.CompilerParams(vmem_limit_bytes=48 * 2**20),
        cost_estimate=pl.CostEstimate(
            flops=2 * tok * 4 * depth * count, bytes_accessed=8 * depth * count, transcendentals=0
        ),
    )(pick, att, *pieces, gain, in_a, in_b)


def finish_kernel(model_width, counts, stat_ref, mean_ref, gain_ref, out_w_ref, *refs):
    hidden_refs, erased_ref = refs[:-1], refs[-1]
    stat = stat_ref[...]
    inv_rms = lax.rsqrt(stat[:, RANK : RANK + 1] / model_width + norm_eps)
    lane = lax.broadcasted_iota(jnp.int32, stat.shape, 1)
    code = jnp.where(lane < RANK, stat * inv_rms - mean_ref[...], 0.0)
    high = code.astype(jnp.bfloat16).astype(jnp.float32)
    low = code - high
    packed = jnp.concatenate([high + pltpu.roll(low, RANK, 1), high], 1).astype(jnp.bfloat16)
    at = 0
    for count, hidden in zip(counts, hidden_refs):
        for j in range(0, count, TILE):
            here = slice(at + j, at + j + TILE)
            removed = lax.dot_general(packed, out_w_ref[here, :], NT, preferred_element_type=jnp.float32)
            normed = hidden[:, j : j + TILE] * inv_rms * gain_ref[:, here]
            erased_ref[:, here] = (normed - removed).astype(jnp.bfloat16)
        at += count


def finish(model_width, stat, mean_code, gain, out_w, hiddens):
    tok, width = stat.shape[0], gain.shape[1]
    counts = [h.shape[1] for h in hiddens]
    rows = 128
    whole = lambda shape: pl.BlockSpec(shape, lambda i: (0, 0))
    return pl.pallas_call(
        functools.partial(finish_kernel, model_width, counts),
        grid=(tok // rows,),
        in_specs=[
            pl.BlockSpec((rows, 2 * RANK), lambda i: (i, 0)),
            whole(mean_code.shape),
            whole(gain.shape),
            whole(out_w.shape),
        ]
        + [pl.BlockSpec((rows, count), lambda i: (i, 0)) for count in counts],
        out_specs=pl.BlockSpec((rows, width), lambda i: (i, 0)),
        out_shape=jax.ShapeDtypeStruct((tok, width), jnp.bfloat16),
        compiler_params=pltpu.CompilerParams(vmem_limit_bytes=48 * 2**20),
        cost_estimate=pl.CostEstimate(
            flops=2 * tok * 256 * width, bytes_accessed=6 * tok * width, transcendentals=0
        ),
    )(stat, mean_code, gain, out_w, *hiddens)


def swapped(block, axis):
    return lax.ppermute(block, axis, [(0, 1), (1, 0)])


def on_device(queries, keys, values, out_proj, post_gain, mean_vec, erase_in, erase_out):
    tok = queries.shape[0]
    outer, inner = lax.axis_size("far"), lax.axis_size("near")
    grp, far, near, col = (lax.axis_index(a) for a in ("grp", "far", "near", "col"))
    row = far * inner + near
    depth, model_width = out_proj.shape
    width = model_width // 2

    mine = lax.dynamic_slice_in_dim(out_proj, col * width, width, 1)
    theirs = swapped(lax.dynamic_slice_in_dim(out_proj, (1 - col) * width, width, 1), "col")
    share = jnp.where(grp == col, mine, theirs)

    ahead = [(i, i + 1) for i in range(outer - 1)]
    blocks = []
    for own in (keys, values):
        second = lax.ppermute(own, "far", ahead)
        first = swapped(jnp.where(near == 0, own, second), "near")
        blocks.append((second, first, own))

    pieces = []
    at = 0
    bounds = []
    for tiles, order in CHUNKS:
        count = tiles * TILE
        along_far = lax.all_gather(share[:, at : at + count], "far", axis=0, tiled=True)
        along_near = swapped(along_far, "near")
        other = swapped(along_far, "grp")
        last = swapped(along_near, "grp") if order == "B" else swapped(other, "near")
        pieces.append((along_far, along_near, other, last))
        bounds.append((at, at + count))
        at += count

    mean_code = jnp.dot(mean_vec[None, :], erase_in, precision=lax.Precision.HIGHEST)
    mean_code = jnp.pad(mean_code, ((0, 7), (0, RANK)))
    mean_code = (mean_code + swapped(mean_code, "col"))[:1]

    cos, sin = rope_tables((row - 2) * tok, 3 * tok)
    kv_local = keys.shape[1] // HD
    group = queries.shape[1] // HD // kv_local
    direct = depth == HD and group == inner
    attended = attend(row[None], queries, *blocks_of(blocks), cos, sin, direct)
    if not direct:
        attended = attended.reshape(tok, outer, inner, depth).transpose(2, 0, 1, 3)
        attended = attended.reshape(inner, tok, outer * depth)
    att = jnp.stack([attended, swapped(attended, "col")])

    in_high, in_low = split_high_low(erase_in)
    in_a = jnp.concatenate([in_high, in_low], 1)
    in_b = jnp.concatenate([in_high, jnp.zeros_like(in_low)], 1)
    out_high, out_low = split_high_low(erase_out)
    out_w = jnp.concatenate([out_high, out_high, out_low, jnp.zeros_like(out_low)], 1)
    gain = post_gain[None, :]

    here = jnp.where(grp == col, 0, 1)
    pick = jnp.stack([here, near, here, 1 - near, 1 - here, near, 1 - here, 1 - near]).astype(jnp.int32)
    hiddens, stats = [], None
    for (lo, hi), piece in zip(bounds, pieces):
        hidden, stat = project(pick, att, piece, gain[:, lo:hi], in_a[lo:hi], in_b[lo:hi])
        hiddens.append(hidden)
        stats = stat if stats is None else stats + stat
    stats = stats + swapped(stats, "col")
    return finish(model_width, stats, mean_code, gain, out_w, hiddens)


def blocks_of(blocks):
    return blocks[0], blocks[1]


def solution(mesh):
    grp, row, col = (mesh.shape[a] for a in ("grp", "row", "col"))
    fine = Mesh(mesh.devices.reshape(grp, row // 2, 2, col), ("grp", "far", "near", "col"))
    tokens = P(("grp", "far", "near"), "col")
    placed = (tokens, tokens, tokens, P(("col", "far", "near"), None), P("col"), P("col"), P("col", None), P("col", None))
    return jax.shard_map(on_device, mesh=fine, in_specs=placed, out_specs=tokens, check_vma=False)
```

```python
import functools

import jax
import jax.numpy as jnp
from jax import lax
from jax.experimental import pallas as pl
from jax.experimental.pallas import tpu as pltpu
from jax.sharding import Mesh
from jax.sharding import PartitionSpec as P

HD = 128
WINDOW = 1024
RANK = 64

query_scale = 168.0 ** (-0.5)
norm_eps = 1e-06
rope_base = 10000.0
log2_e = 1.4426950408889634

TILE = 384
VMEM_LIMIT = 60 * 2**20

NT = (((1,), (1,)), ((), ()))


def split_high_low(value):
    high = lax.reduce_precision(value, 8, 7)
    return high.astype(jnp.bfloat16), (value - high).astype(jnp.bfloat16)


def rope_tables(first_position, count):
    half_dim = HD // 2
    inverse = jnp.exp(
        -(2.0 * jnp.arange(half_dim, dtype=jnp.float32) / HD) * jnp.log(jnp.float32(rope_base))
    )
    positions = (first_position + jnp.arange(count, dtype=jnp.int32)).astype(jnp.float32)
    angles = positions[:, None] * inverse[None, :]
    cosine, sine = jnp.cos(angles), jnp.sin(angles)
    return jnp.concatenate([cosine, cosine], 1), jnp.concatenate([-sine, sine], 1)


def attend_kernel(tok, group, direct, row_ref, q_ref, k0, k1, k2, v0, v1, v2, cos_ref, sin_ref, out_ref):
    tile = 256

    def turned(field, at):
        wide = field.astype(jnp.float32)
        cos, sin = cos_ref[at : at + tok, :], sin_ref[at : at + tok, :]
        return (wide * cos + pltpu.roll(wide, HD // 2, 1) * sin).astype(jnp.bfloat16)

    row = row_ref[0]
    bias0 = jnp.where(row >= 2, 0.0, -1e30).astype(jnp.float32)
    bias1 = jnp.where(row >= 1, 0.0, -1e30).astype(jnp.float32)
    key0, key1, key2 = turned(k0[...], 0), turned(k1[...], tok), turned(k2[...], 2 * tok)
    heads = [turned(q_ref[:, h * HD : (h + 1) * HD], 2 * tok) for h in range(group)]
    scale = query_scale * log2_e
    stacked = group * tile
    inner = lax.rem(lax.broadcasted_iota(jnp.int32, (stacked, tile), 0), tile)
    newer = lax.broadcasted_iota(jnp.int32, (stacked, tile), 1) > inner

    def dot_nt(a, b):
        return lax.dot_general(a, b, NT, preferred_element_type=jnp.float32)

    def dot(a, b):
        return jnp.dot(a, b, preferred_element_type=jnp.float32)

    for t in range(tok // tile):
        lo, hi = t * tile, (t + 1) * tile
        query = jnp.concatenate([h[lo:hi] for h in heads], 0)
        parts = [(dot_nt(query, key1) + bias1, v1[...])]
        if hi < tok:
            parts.append((dot_nt(query, key0[hi:]) + bias0, v0[hi:, :]))
        if lo > 0:
            parts.append((dot_nt(query, key2[:lo]), v2[:lo, :]))
        mixed = jnp.where(newer, dot_nt(query, key0[lo:hi]) + bias0, dot_nt(query, key2[lo:hi]))
        top = jnp.max(mixed, axis=1, keepdims=True)
        for part, _ in parts:
            top = jnp.maximum(top, jnp.max(part, axis=1, keepdims=True))
        top = top * scale
        weights = jnp.exp2(mixed * scale - top)
        total = jnp.sum(weights, axis=1, keepdims=True)
        older = jnp.where(newer, weights, 0.0)
        result = dot(older.astype(jnp.bfloat16), v0[lo:hi, :])
        result += dot((weights - older).astype(jnp.bfloat16), v2[lo:hi, :])
        for part, value in parts:
            weights = jnp.exp2(part * scale - top)
            total += jnp.sum(weights, axis=1, keepdims=True)
            result += dot(weights.astype(jnp.bfloat16), value)
        result = (result / total).astype(jnp.bfloat16)
        for h in range(group):
            block = result[h * tile : (h + 1) * tile]
            if direct:
                out_ref[h, lo:hi, :] = block
            else:
                out_ref[lo:hi, h * HD : (h + 1) * HD] = block


def attend(row, queries, key_blocks, val_blocks, cos, sin, direct):
    tok, kv_local = queries.shape[0], key_blocks[0].shape[1] // HD
    group = queries.shape[1] // HD // kv_local
    head_block = pl.BlockSpec((tok, HD), lambda g, r: (0, g))
    table = pl.BlockSpec((3 * tok, HD), lambda g, r: (0, 0))
    if direct:
        out_shape = (kv_local * group, tok, HD)
        out_spec = pl.BlockSpec((group, tok, HD), lambda g, r: (g, 0, 0))
    else:
        out_shape = queries.shape
        out_spec = pl.BlockSpec((tok, group * HD), lambda g, r: (0, g))
    heads = kv_local * group
    return pl.pallas_call(
        functools.partial(attend_kernel, tok, group, direct),
        grid_spec=pltpu.PrefetchScalarGridSpec(
            num_scalar_prefetch=1,
            grid=(kv_local,),
            in_specs=[pl.BlockSpec((tok, group * HD), lambda g, r: (0, g))] + [head_block] * 6 + [table] * 2,
            out_specs=out_spec,
        ),
        out_shape=jax.ShapeDtypeStruct(out_shape, jnp.bfloat16),
        compiler_params=pltpu.CompilerParams(vmem_limit_bytes=VMEM_LIMIT),
        cost_estimate=pl.CostEstimate(
            flops=heads * tok * 10 * tok * HD, bytes_accessed=6 * 2**20, transcendentals=heads * tok * 2 * tok
        ),
    )(row, queries, *key_blocks, *val_blocks, cos, sin)


def project_kernel(count, first, last, pick_ref, own_ref, other_ref, *refs):
    weights, refs = refs[:count], refs[count:]
    if not first:
        partial_ref, refs = refs[0], refs[1:]
    if last:
        gain_ref, in_ref, mean_ref, refs = *refs[:3], refs[3:]
    hidden_ref, refs = refs[0], refs[1:]
    if last:
        stat_ref, refs = refs[0], refs[1:]
    heads, sems = refs
    step = pl.program_id(0)
    depth = weights[0].shape[0]
    slots = own_ref.shape[0]

    @pl.when(step == 0)
    def _():
        for n in range(count):
            slot = pick_ref[n]
            place = heads.at[:, n * depth : (n + 1) * depth]

            @pl.when(slot < slots)
            def _():
                pltpu.make_async_copy(own_ref.at[slot], place, sems.at[n]).start()

            @pl.when(slot >= slots)
            def _():
                pltpu.make_async_copy(other_ref.at[slot - slots], place, sems.at[n]).start()

        for n in range(count):
            place = heads.at[:, n * depth : (n + 1) * depth]
            pltpu.make_async_copy(own_ref.at[0], place, sems.at[n]).wait()

    weight = jnp.concatenate([w[...] for w in weights], 0)
    total = jnp.dot(heads[...], weight, preferred_element_type=jnp.float32)
    if not first:
        total += partial_ref[...]
    hidden_ref[...] = total
    if last:
        wide = jnp.concatenate([in_ref[...], jnp.zeros_like(in_ref)], 1)
        wide_high = wide.astype(jnp.bfloat16)
        wide_low = wide - wide_high.astype(jnp.float32)
        in_a = (wide_high.astype(jnp.float32) + pltpu.roll(wide_low, RANK, 1)).astype(jnp.bfloat16)

        def coded(field):
            high = field.astype(jnp.bfloat16)
            low = (field - high.astype(jnp.float32)).astype(jnp.bfloat16)
            code = jnp.dot(high, in_a, preferred_element_type=jnp.float32)
            code += jnp.dot(low, wide_high, preferred_element_type=jnp.float32)
            return code + pltpu.roll(code, RANK, 1)

        code = coded(total * gain_ref[...])
        square = jnp.sum(total * total, axis=1, keepdims=True)
        lane = lax.broadcasted_iota(jnp.int32, code.shape, 1)
        stat = jnp.where(lane < RANK, code, square)
        tok = stat.shape[0]
        mean_code = coded(jnp.broadcast_to(mean_ref[...], (8, mean_ref.shape[1])))

        @pl.when(step == 0)
        def _():
            stat_ref[:tok, :] = stat
            stat_ref[tok:, :] = mean_code

        @pl.when(step > 0)
        def _():
            stat_ref[:tok, :] += stat
            stat_ref[tok:, :] += mean_code


def project(pick, own, other, weights, partial=None, last_terms=None):
    tok = own.shape[1]
    depth, width = weights[0].shape
    count = len(weights)
    first, last = partial is None, last_terms is not None
    columns = lambda rows: pl.BlockSpec((rows, TILE), lambda j, r: (0, j))
    anywhere = pl.BlockSpec(memory_space=pl.ANY)
    in_specs = [anywhere] * 2 + [columns(depth)] * count
    operands = [pick, own, other, *weights]
    out_specs = [columns(tok)]
    out_shape = [jax.ShapeDtypeStruct((tok, width), jnp.float32)]
    if not first:
        in_specs.append(columns(tok))
        operands.append(partial)
    if last:
        gain, erase_in, mean = last_terms
        in_specs += [columns(1), pl.BlockSpec((TILE, RANK), lambda j, r: (j, 0)), columns(1)]
        operands += [gain, erase_in, mean]
        out_specs.append(pl.BlockSpec((tok + 8, 2 * RANK), lambda j, r: (0, 0)))
        out_shape.append(jax.ShapeDtypeStruct((tok + 8, 2 * RANK), jnp.float32))
    return pl.pallas_call(
        functools.partial(project_kernel, count, first, last),
        grid_spec=pltpu.PrefetchScalarGridSpec(
            num_scalar_prefetch=1,
            grid=(width // TILE,),
            in_specs=in_specs,
            out_specs=out_specs,
            scratch_shapes=[
                pltpu.VMEM((tok, count * depth), jnp.bfloat16),
                pltpu.SemaphoreType.DMA((count,)),
            ],
        ),
        out_shape=out_shape,
        compiler_params=pltpu.CompilerParams(vmem_limit_bytes=VMEM_LIMIT),
        cost_estimate=pl.CostEstimate(
            flops=2 * tok * count * depth * width, bytes_accessed=2 * count * depth * width, transcendentals=0
        ),
    )(*operands)


def finish_kernel(model_width, own_ref, other_ref, own_mean, other_mean, gain_ref, out_w_ref, hidden_ref, erased_ref):
    stat = own_ref[...] + other_ref[...]
    mean_code = own_mean[0:1, :] + other_mean[0:1, :]
    inv_rms = lax.rsqrt(stat[:, RANK : RANK + 1] / model_width + norm_eps)
    lane = lax.broadcasted_iota(jnp.int32, stat.shape, 1)
    code = jnp.where(lane < RANK, stat * inv_rms - mean_code, 0.0)
    high = code.astype(jnp.bfloat16).astype(jnp.float32)
    low = code - high
    packed = jnp.concatenate([high + pltpu.roll(low, RANK, 1), high], 1).astype(jnp.bfloat16)
    for at in range(0, hidden_ref.shape[1], TILE):
        here = slice(at, at + TILE)
        removed = lax.dot_general(packed, out_w_ref[here, :], NT, preferred_element_type=jnp.float32)
        normed = hidden_ref[:, here] * inv_rms * gain_ref[:, here]
        erased_ref[:, here] = (normed - removed).astype(jnp.bfloat16)


def finish(model_width, stat, stat_other, gain, out_w, hidden):
    tok, width = hidden.shape
    rows = 128
    whole = lambda shape: pl.BlockSpec(shape, lambda i: (0, 0))
    stats = pl.BlockSpec((rows, 2 * RANK), lambda i: (i, 0))
    mean = pl.BlockSpec((8, 2 * RANK), lambda i: (tok // 8, 0))
    return pl.pallas_call(
        functools.partial(finish_kernel, model_width),
        grid=(tok // rows,),
        in_specs=[
            stats,
            stats,
            mean,
            mean,
            whole(gain.shape),
            whole(out_w.shape),
            pl.BlockSpec((rows, width), lambda i: (i, 0)),
        ],
        out_specs=pl.BlockSpec((rows, width), lambda i: (i, 0)),
        out_shape=jax.ShapeDtypeStruct((tok, width), jnp.bfloat16),
        compiler_params=pltpu.CompilerParams(vmem_limit_bytes=VMEM_LIMIT),
        cost_estimate=pl.CostEstimate(
            flops=2 * tok * 256 * width, bytes_accessed=6 * tok * width, transcendentals=0
        ),
    )(stat, stat_other, stat, stat_other, gain, out_w, hidden)


def swapped(block, axis):
    return lax.ppermute(block, axis, [(0, 1), (1, 0)])


def ring_order(size):
    return list(range(0, 1)) + list(range(1, size, 2)) + [i for i in range(size - 1, 0, -1) if i % 2 == 0]


def on_device(queries, keys, values, out_proj, post_gain, mean_vec, erase_in, erase_out):
    tok = queries.shape[0]
    outer, inner = lax.axis_size("far"), lax.axis_size("near")
    grp, far, near, col = (lax.axis_index(a) for a in ("grp", "far", "near", "col"))
    row = far * inner + near
    depth, model_width = out_proj.shape
    width = model_width // 2
    kv_local = keys.shape[1] // HD
    heads = queries.shape[1] // HD
    direct = depth == HD and outer * inner == heads

    mine = lax.dynamic_slice_in_dim(out_proj, col * width, width, 1)
    theirs = swapped(lax.dynamic_slice_in_dim(out_proj, (1 - col) * width, width, 1), "col")

    ahead = [(i, i + 1) for i in range(outer - 1)]
    blocks = []
    for own in (keys, values):
        second = lax.ppermute(own, "far", ahead)
        first = swapped(jnp.where(near == 0, own, second), "near")
        blocks.append((second, first, own))

    if direct:
        order = ring_order(outer)
        places = jnp.array(order, jnp.int32)
        position = jnp.argmax(places == far).astype(jnp.int32)
        hops = [(order[i], order[(i + 1) % outer]) for i in range(outer)]
        ring = lambda block: lax.ppermute(block, "far", hops)
        is_mine = grp == col
        main = [jnp.where(is_mine, mine, theirs)]
        across = [jnp.where(is_mine, theirs, mine)]
        beside = [swapped(main[0], "near")]
        corner = [swapped(beside[0], "grp")]
        for k in range(1, outer):
            main.append(ring(main[-1]))
            across.append(swapped(main[-1], "grp") if k % 2 else ring(across[-1]))
            beside.append(swapped(main[-1], "near"))
            corner.append(swapped(beside[-1], "grp"))
        here = jnp.where(is_mine, 0, heads)
        there = heads - here
        weights, pick = [], []
        for k in range(outer):
            far_k = places[lax.rem(position - k + outer, outer)]
            for piece, base, side in (
                (main[k], here, near),
                (beside[k], here, 1 - near),
                (across[k], there, near),
                (corner[k], there, 1 - near),
            ):
                weights.append(piece)
                pick.append(base + far_k * inner + side)
    else:
        weights = [lax.all_gather(w, ("far", "near"), axis=0, tiled=True) for w in (mine, theirs)]
        pick = [jnp.int32(0), jnp.int32(1)]
    pick = jnp.stack(pick).astype(jnp.int32)

    cos, sin = rope_tables((row - 2) * tok, 3 * tok)
    attended = attend(row[None], queries, blocks[0], blocks[1], cos, sin, direct)
    if not direct:
        attended = attended[None]
    att_other = swapped(attended, "col")

    out_high, out_low = split_high_low(erase_out)
    out_w = jnp.concatenate([out_high, out_high, out_low, jnp.zeros_like(out_low)], 1)
    gain = post_gain[None, :]

    half = len(weights) // 2
    (partial,) = project(pick[:half], attended, att_other, weights[:half])
    hidden, stat = project(
        pick[half:], attended, att_other, weights[half:], partial, (gain, erase_in, mean_vec[None, :])
    )
    return finish(model_width, stat, swapped(stat, "col"), gain, out_w, hidden)


def solution(mesh):
    grp, row, col = (mesh.shape[a] for a in ("grp", "row", "col"))
    fine = Mesh(mesh.devices.reshape(grp, row // 2, 2, col), ("grp", "far", "near", "col"))
    tokens = P(("grp", "far", "near"), "col")
    placed = (tokens, tokens, tokens, P(("col", "far", "near"), None), P("col"), P("col"), P("col", None), P("col", None))
    return jax.shard_map(on_device, mesh=fine, in_specs=placed, out_specs=tokens, check_vma=False)
```

```python
import functools

import jax
import jax.numpy as jnp
from jax import lax
from jax.experimental import pallas as pl
from jax.experimental.pallas import tpu as pltpu
from jax.sharding import Mesh
from jax.sharding import PartitionSpec as P

HD = 128
WINDOW = 1024
RANK = 64

query_scale = 168.0 ** (-0.5)
norm_eps = 1e-06
rope_base = 10000.0
log2_e = 1.4426950408889634

TILE = 384
VMEM_LIMIT = 60 * 2**20

NT = (((1,), (1,)), ((), ()))


def split_high_low(value):
    high = lax.reduce_precision(value, 8, 7)
    return high.astype(jnp.bfloat16), (value - high).astype(jnp.bfloat16)


def rope_tables(first_position, count):
    half_dim = HD // 2
    inverse = jnp.exp(
        -(2.0 * jnp.arange(half_dim, dtype=jnp.float32) / HD) * jnp.log(jnp.float32(rope_base))
    )
    positions = (first_position + jnp.arange(count, dtype=jnp.int32)).astype(jnp.float32)
    angles = positions[:, None] * inverse[None, :]
    cosine, sine = jnp.cos(angles), jnp.sin(angles)
    return jnp.concatenate([cosine, cosine], 1), jnp.concatenate([-sine, sine], 1)


def attend_kernel(tok, group, direct, row_ref, q_ref, k0, k1, k2, v0, v1, v2, cos_ref, sin_ref, out_ref):
    tile = 256

    def turned(field, at):
        wide = field.astype(jnp.float32)
        cos, sin = cos_ref[at : at + tok, :], sin_ref[at : at + tok, :]
        return (wide * cos + pltpu.roll(wide, HD // 2, 1) * sin).astype(jnp.bfloat16)

    row = row_ref[0]
    bias0 = jnp.where(row >= 2, 0.0, -1e30).astype(jnp.float32)
    bias1 = jnp.where(row >= 1, 0.0, -1e30).astype(jnp.float32)
    key0, key1, key2 = turned(k0[...], 0), turned(k1[...], tok), turned(k2[...], 2 * tok)
    heads = [turned(q_ref[:, h * HD : (h + 1) * HD], 2 * tok) for h in range(group)]
    scale = query_scale * log2_e
    stacked = group * tile
    inner = lax.rem(lax.broadcasted_iota(jnp.int32, (stacked, tile), 0), tile)
    newer = lax.broadcasted_iota(jnp.int32, (stacked, tile), 1) > inner

    def dot_nt(a, b):
        return lax.dot_general(a, b, NT, preferred_element_type=jnp.float32)

    def dot(a, b):
        return jnp.dot(a, b, preferred_element_type=jnp.float32)

    for t in range(tok // tile):
        lo, hi = t * tile, (t + 1) * tile
        query = jnp.concatenate([h[lo:hi] for h in heads], 0)
        parts = [(dot_nt(query, key1) + bias1, v1[...])]
        if hi < tok:
            parts.append((dot_nt(query, key0[hi:]) + bias0, v0[hi:, :]))
        if lo > 0:
            parts.append((dot_nt(query, key2[:lo]), v2[:lo, :]))
        mixed = jnp.where(newer, dot_nt(query, key0[lo:hi]) + bias0, dot_nt(query, key2[lo:hi]))
        top = jnp.max(mixed, axis=1, keepdims=True)
        for part, _ in parts:
            top = jnp.maximum(top, jnp.max(part, axis=1, keepdims=True))
        top = top * scale
        weights = jnp.exp2(mixed * scale - top)
        total = jnp.sum(weights, axis=1, keepdims=True)
        older = jnp.where(newer, weights, 0.0)
        result = dot(older.astype(jnp.bfloat16), v0[lo:hi, :])
        result += dot((weights - older).astype(jnp.bfloat16), v2[lo:hi, :])
        for part, value in parts:
            weights = jnp.exp2(part * scale - top)
            total += jnp.sum(weights, axis=1, keepdims=True)
            result += dot(weights.astype(jnp.bfloat16), value)
        result = (result / total).astype(jnp.bfloat16)
        for h in range(group):
            block = result[h * tile : (h + 1) * tile]
            if direct:
                out_ref[h, lo:hi, :] = block
            else:
                out_ref[lo:hi, h * HD : (h + 1) * HD] = block


def attend(row, queries, key_blocks, val_blocks, cos, sin, direct):
    tok, kv_local = queries.shape[0], key_blocks[0].shape[1] // HD
    group = queries.shape[1] // HD // kv_local
    head_block = pl.BlockSpec((tok, HD), lambda g, r: (0, g))
    table = pl.BlockSpec((3 * tok, HD), lambda g, r: (0, 0))
    if direct:
        out_shape = (kv_local * group, tok, HD)
        out_spec = pl.BlockSpec((group, tok, HD), lambda g, r: (g, 0, 0))
    else:
        out_shape = queries.shape
        out_spec = pl.BlockSpec((tok, group * HD), lambda g, r: (0, g))
    heads = kv_local * group
    return pl.pallas_call(
        functools.partial(attend_kernel, tok, group, direct),
        grid_spec=pltpu.PrefetchScalarGridSpec(
            num_scalar_prefetch=1,
            grid=(kv_local,),
            in_specs=[pl.BlockSpec((tok, group * HD), lambda g, r: (0, g))] + [head_block] * 6 + [table] * 2,
            out_specs=out_spec,
        ),
        out_shape=jax.ShapeDtypeStruct(out_shape, jnp.bfloat16),
        compiler_params=pltpu.CompilerParams(vmem_limit_bytes=VMEM_LIMIT),
        cost_estimate=pl.CostEstimate(
            flops=heads * tok * 10 * tok * HD, bytes_accessed=6 * 2**20, transcendentals=heads * tok * 2 * tok
        ),
    )(row, queries, *key_blocks, *val_blocks, cos, sin)


def project_kernel(count, first, last, pick_ref, own_ref, other_ref, *refs):
    weights, refs = refs[:count], refs[count:]
    if not first:
        partial_ref, refs = refs[0], refs[1:]
    if last:
        gain_ref, in_ref, mean_ref, refs = *refs[:3], refs[3:]
    hidden_ref, refs = refs[0], refs[1:]
    if last:
        stat_ref, refs = refs[0], refs[1:]
    heads, sems = refs
    step = pl.program_id(0)
    depth = weights[0].shape[0]
    slots = own_ref.shape[0]

    @pl.when(step == 0)
    def _():
        for n in range(count):
            slot = pick_ref[n]
            place = heads.at[:, n * depth : (n + 1) * depth]

            @pl.when(slot < slots)
            def _():
                pltpu.make_async_copy(own_ref.at[slot], place, sems.at[n]).start()

            @pl.when(slot >= slots)
            def _():
                pltpu.make_async_copy(other_ref.at[slot - slots], place, sems.at[n]).start()

        for n in range(count):
            place = heads.at[:, n * depth : (n + 1) * depth]
            pltpu.make_async_copy(own_ref.at[0], place, sems.at[n]).wait()

    weight = jnp.concatenate([w[...] for w in weights], 0)
    total = jnp.dot(heads[...], weight, preferred_element_type=jnp.float32)
    if not first:
        total += partial_ref[...]
    hidden_ref[...] = total
    if last:
        wide = jnp.concatenate([in_ref[...], jnp.zeros_like(in_ref)], 1)
        wide_high = wide.astype(jnp.bfloat16)
        wide_low = wide - wide_high.astype(jnp.float32)
        in_a = (wide_high.astype(jnp.float32) + pltpu.roll(wide_low, RANK, 1)).astype(jnp.bfloat16)

        def coded(field):
            high = field.astype(jnp.bfloat16)
            low = (field - high.astype(jnp.float32)).astype(jnp.bfloat16)
            code = jnp.dot(high, in_a, preferred_element_type=jnp.float32)
            code += jnp.dot(low, wide_high, preferred_element_type=jnp.float32)
            return code + pltpu.roll(code, RANK, 1)

        code = coded(total * gain_ref[...])
        square = jnp.sum(total * total, axis=1, keepdims=True)
        lane = lax.broadcasted_iota(jnp.int32, code.shape, 1)
        stat = jnp.where(lane < RANK, code, square)
        tok = stat.shape[0]
        mean_code = coded(jnp.broadcast_to(mean_ref[...], (8, mean_ref.shape[1])))

        @pl.when(step == 0)
        def _():
            stat_ref[:tok, :] = stat
            stat_ref[tok:, :] = mean_code

        @pl.when(step > 0)
        def _():
            stat_ref[:tok, :] += stat
            stat_ref[tok:, :] += mean_code


def project(pick, own, other, weights, partial=None, last_terms=None):
    tok = own.shape[1]
    depth, width = weights[0].shape
    count = len(weights)
    first, last = partial is None, last_terms is not None
    columns = lambda rows: pl.BlockSpec((rows, TILE), lambda j, r: (0, j))
    anywhere = pl.BlockSpec(memory_space=pl.ANY)
    in_specs = [anywhere] * 2 + [columns(depth)] * count
    operands = [pick, own, other, *weights]
    out_specs = [columns(tok)]
    out_shape = [jax.ShapeDtypeStruct((tok, width), jnp.float32)]
    if not first:
        in_specs.append(columns(tok))
        operands.append(partial)
    if last:
        gain, erase_in, mean = last_terms
        in_specs += [columns(1), pl.BlockSpec((TILE, RANK), lambda j, r: (j, 0)), columns(1)]
        operands += [gain, erase_in, mean]
        out_specs.append(pl.BlockSpec((tok + 8, 2 * RANK), lambda j, r: (0, 0)))
        out_shape.append(jax.ShapeDtypeStruct((tok + 8, 2 * RANK), jnp.float32))
    return pl.pallas_call(
        functools.partial(project_kernel, count, first, last),
        grid_spec=pltpu.PrefetchScalarGridSpec(
            num_scalar_prefetch=1,
            grid=(width // TILE,),
            in_specs=in_specs,
            out_specs=out_specs,
            scratch_shapes=[
                pltpu.VMEM((tok, count * depth), jnp.bfloat16),
                pltpu.SemaphoreType.DMA((count,)),
            ],
        ),
        out_shape=out_shape,
        compiler_params=pltpu.CompilerParams(vmem_limit_bytes=VMEM_LIMIT),
        cost_estimate=pl.CostEstimate(
            flops=2 * tok * count * depth * width, bytes_accessed=2 * count * depth * width, transcendentals=0
        ),
    )(*operands)


def finish_kernel(model_width, own_ref, other_ref, own_mean, other_mean, gain_ref, out_w_ref, hidden_ref, erased_ref):
    stat = own_ref[...] + other_ref[...]
    mean_code = own_mean[0:1, :] + other_mean[0:1, :]
    inv_rms = lax.rsqrt(stat[:, RANK : RANK + 1] / model_width + norm_eps)
    lane = lax.broadcasted_iota(jnp.int32, stat.shape, 1)
    code = jnp.where(lane < RANK, stat * inv_rms - mean_code, 0.0)
    high = code.astype(jnp.bfloat16).astype(jnp.float32)
    low = code - high
    packed = jnp.concatenate([high + pltpu.roll(low, RANK, 1), high], 1).astype(jnp.bfloat16)
    for at in range(0, hidden_ref.shape[1], TILE):
        here = slice(at, at + TILE)
        removed = lax.dot_general(packed, out_w_ref[here, :], NT, preferred_element_type=jnp.float32)
        normed = hidden_ref[:, here] * inv_rms * gain_ref[:, here]
        erased_ref[:, here] = (normed - removed).astype(jnp.bfloat16)


def finish(model_width, stat, stat_other, gain, out_w, hidden):
    tok, width = hidden.shape
    rows = 128
    whole = lambda shape: pl.BlockSpec(shape, lambda i: (0, 0))
    stats = pl.BlockSpec((rows, 2 * RANK), lambda i: (i, 0))
    mean = pl.BlockSpec((8, 2 * RANK), lambda i: (tok // 8, 0))
    return pl.pallas_call(
        functools.partial(finish_kernel, model_width),
        grid=(tok // rows,),
        in_specs=[
            stats,
            stats,
            mean,
            mean,
            whole(gain.shape),
            whole(out_w.shape),
            pl.BlockSpec((rows, width), lambda i: (i, 0)),
        ],
        out_specs=pl.BlockSpec((rows, width), lambda i: (i, 0)),
        out_shape=jax.ShapeDtypeStruct((tok, width), jnp.bfloat16),
        compiler_params=pltpu.CompilerParams(vmem_limit_bytes=VMEM_LIMIT),
        cost_estimate=pl.CostEstimate(
            flops=2 * tok * 256 * width, bytes_accessed=6 * tok * width, transcendentals=0
        ),
    )(stat, stat_other, stat, stat_other, gain, out_w, hidden)


def swapped(block, axis):
    return lax.ppermute(block, axis, [(0, 1), (1, 0)])


def ring_order(size):
    return list(range(0, 1)) + list(range(1, size, 2)) + [i for i in range(size - 1, 0, -1) if i % 2 == 0]


def on_device(queries, keys, values, out_proj, post_gain, mean_vec, erase_in, erase_out):
    tok = queries.shape[0]
    outer, inner = lax.axis_size("far"), lax.axis_size("near")
    grp, far, near, col = (lax.axis_index(a) for a in ("grp", "far", "near", "col"))
    row = far * inner + near
    depth, model_width = out_proj.shape
    width = model_width // 2
    kv_local = keys.shape[1] // HD
    heads = queries.shape[1] // HD
    direct = depth == HD and outer * inner == heads

    mine = lax.dynamic_slice_in_dim(out_proj, col * width, width, 1)
    theirs = swapped(lax.dynamic_slice_in_dim(out_proj, (1 - col) * width, width, 1), "col")

    ahead = [(i, i + 1) for i in range(outer - 1)]
    from_behind = lambda block: lax.ppermute(block, "far", ahead)
    hold = lax.optimization_barrier
    cos, sin = rope_tables((row - 2) * tok, 3 * tok)
    out_high, out_low = split_high_low(erase_out)
    out_w = jnp.concatenate([out_high, out_high, out_low, jnp.zeros_like(out_low)], 1)

    def for_next(second):
        return [swapped(jnp.where(near == 0, own, old), "near") for own, old in zip((keys, values), second)]

    if direct:
        order = ring_order(outer)
        places = jnp.array(order, jnp.int32)
        position = jnp.argmax(places == far).astype(jnp.int32)
        hops = [(order[i], order[(i + 1) % outer]) for i in range(outer)]
        ring = lambda block: lax.ppermute(block, "far", hops)
        beyond = lambda block: swapped(block, "near")
        facing = lambda block: swapped(block, "grp")
        is_mine = grp == col
        main, beside, across, corner = ([None] * outer for _ in range(4))
        main[0] = jnp.where(is_mine, mine, theirs)
        across[0] = jnp.where(is_mine, theirs, mine)
        main[1], beside[0] = ring(main[0]), beyond(main[0])
        main[1], beside[0], keys, values, cos, sin, out_w = hold((main[1], beside[0], keys, values, cos, sin, out_w))
        second = [from_behind(keys), from_behind(values)]
        beside[1], across[1] = beyond(main[1]), facing(main[1])
        second, beside[1], across[1], main[1] = hold((second, beside[1], across[1], main[1]))
        first = for_next(second)
        main[2], corner[1] = ring(main[1]), facing(beside[1])
        first, main[2], corner[1] = hold((first, main[2], corner[1]))
        main[3], beside[2], across[2] = ring(main[2]), beyond(main[2]), facing(main[2])
        attended = attend(row[None], queries, (second[0], first[0], keys), (second[1], first[1], values), cos, sin, True)
        main[3], beside[2], across[2], attended = hold((main[3], beside[2], across[2], attended))
        across[3], beside[3], corner[2] = ring(across[2]), beyond(main[3]), facing(beside[2])
        att_other = swapped(attended, "col")
        across[3], beside[3], corner[2], att_other, across[0] = hold(
            (across[3], beside[3], corner[2], att_other, across[0])
        )
        corner[0], corner[3] = beyond(across[0]), facing(beside[3])
        here = jnp.where(is_mine, 0, heads)
        there = heads - here
        weights, pick, late, late_pick = [], [], [], []
        for k in range(outer):
            far_k = places[lax.rem(position - k + outer, outer)]
            for piece, base, side in (
                (main[k], here, near),
                (beside[k], here, 1 - near),
                (across[k], there, near),
                (corner[k], there, 1 - near),
            ):
                is_late = piece is corner[0] or piece is corner[3]
                (late if is_late else weights).append(piece)
                (late_pick if is_late else pick).append(base + far_k * inner + side)
    else:
        second = [from_behind(keys), from_behind(values)]
        first = for_next(second)
        attended = attend(row[None], queries, (second[0], first[0], keys), (second[1], first[1], values), cos, sin, False)
        attended = attended[None]
        att_other = swapped(attended, "col")
        weights, late = ([lax.all_gather(w, ("far", "near"), axis=0, tiled=True)] for w in (mine, theirs))
        pick, late_pick = [jnp.int32(0)], [jnp.int32(1)]

    gain = post_gain[None, :]
    (partial,) = project(jnp.stack(pick).astype(jnp.int32), attended, att_other, weights)
    hidden, stat = project(
        jnp.stack(late_pick).astype(jnp.int32), attended, att_other, late, partial, (gain, erase_in, mean_vec[None, :])
    )
    return finish(model_width, stat, swapped(stat, "col"), gain, out_w, hidden)


def solution(mesh):
    grp, row, col = (mesh.shape[a] for a in ("grp", "row", "col"))
    fine = Mesh(mesh.devices.reshape(grp, row // 2, 2, col), ("grp", "far", "near", "col"))
    tokens = P(("grp", "far", "near"), "col")
    placed = (tokens, tokens, tokens, P(("col", "far", "near"), None), P("col"), P("col"), P("col", None), P("col", None))
    return jax.shard_map(on_device, mesh=fine, in_specs=placed, out_specs=tokens, check_vma=False)
```

```python
import functools

import jax
import jax.numpy as jnp
from jax import lax
from jax.experimental import pallas as pl
from jax.experimental.pallas import tpu as pltpu
from jax.sharding import Mesh
from jax.sharding import PartitionSpec as P

HD = 128
WINDOW = 1024
RANK = 64

query_scale = 168.0 ** (-0.5)
norm_eps = 1e-06
rope_base = 10000.0
log2_e = 1.4426950408889634

TILE = 896
VMEM_LIMIT = 32 * 2**20

NT = (((1,), (1,)), ((), ()))


def split_high_low(value):
    high = lax.reduce_precision(value, 8, 7)
    return high.astype(jnp.bfloat16), (value - high).astype(jnp.bfloat16)


def rope_tables(first_position, count):
    half_dim = HD // 2
    inverse = jnp.exp(
        -(2.0 * jnp.arange(half_dim, dtype=jnp.float32) / HD) * jnp.log(jnp.float32(rope_base))
    )
    positions = (first_position + jnp.arange(count, dtype=jnp.int32)).astype(jnp.float32)
    angles = positions[:, None] * inverse[None, :]
    cosine, sine = jnp.cos(angles), jnp.sin(angles)
    return jnp.concatenate([cosine, cosine], 1), jnp.concatenate([-sine, sine], 1)


def attend_kernel(tok, group, direct, row_ref, q_ref, k0, k1, k2, v0, v1, v2, cos_ref, sin_ref, out_ref):
    tile = 256

    def turned(field, at):
        wide = field.astype(jnp.float32)
        cos, sin = cos_ref[at : at + tok, :], sin_ref[at : at + tok, :]
        return (wide * cos + pltpu.roll(wide, HD // 2, 1) * sin).astype(jnp.bfloat16)

    row = row_ref[0]
    bias0 = jnp.where(row >= 2, 0.0, -1e30).astype(jnp.float32)
    bias1 = jnp.where(row >= 1, 0.0, -1e30).astype(jnp.float32)
    key0, key1, key2 = turned(k0[...], 0), turned(k1[...], tok), turned(k2[...], 2 * tok)
    heads = [turned(q_ref[:, h * HD : (h + 1) * HD], 2 * tok) for h in range(group)]
    scale = query_scale * log2_e
    stacked = group * tile
    inner = lax.rem(lax.broadcasted_iota(jnp.int32, (stacked, tile), 0), tile)
    newer = lax.broadcasted_iota(jnp.int32, (stacked, tile), 1) > inner

    def dot_nt(a, b):
        return lax.dot_general(a, b, NT, preferred_element_type=jnp.float32)

    def dot(a, b):
        return jnp.dot(a, b, preferred_element_type=jnp.float32)

    for t in range(tok // tile):
        lo, hi = t * tile, (t + 1) * tile
        query = jnp.concatenate([h[lo:hi] for h in heads], 0)
        parts = [(dot_nt(query, key1) + bias1, v1[...])]
        if hi < tok:
            parts.append((dot_nt(query, key0[hi:]) + bias0, v0[hi:, :]))
        if lo > 0:
            parts.append((dot_nt(query, key2[:lo]), v2[:lo, :]))
        mixed = jnp.where(newer, dot_nt(query, key0[lo:hi]) + bias0, dot_nt(query, key2[lo:hi]))
        top = jnp.max(mixed, axis=1, keepdims=True)
        for part, _ in parts:
            top = jnp.maximum(top, jnp.max(part, axis=1, keepdims=True))
        top = top * scale
        weights = jnp.exp2(mixed * scale - top)
        total = jnp.sum(weights, axis=1, keepdims=True)
        older = jnp.where(newer, weights, 0.0)
        result = dot(older.astype(jnp.bfloat16), v0[lo:hi, :])
        result += dot((weights - older).astype(jnp.bfloat16), v2[lo:hi, :])
        for part, value in parts:
            weights = jnp.exp2(part * scale - top)
            total += jnp.sum(weights, axis=1, keepdims=True)
            result += dot(weights.astype(jnp.bfloat16), value)
        result = (result / total).astype(jnp.bfloat16)
        for h in range(group):
            block = result[h * tile : (h + 1) * tile]
            if direct:
                out_ref[h, lo:hi, :] = block
            else:
                out_ref[lo:hi, h * HD : (h + 1) * HD] = block


def attend(row, queries, key_blocks, val_blocks, cos, sin, direct):
    tok, kv_local = queries.shape[0], key_blocks[0].shape[1] // HD
    group = queries.shape[1] // HD // kv_local
    head_block = pl.BlockSpec((tok, HD), lambda g, r: (0, g))
    table = pl.BlockSpec((3 * tok, HD), lambda g, r: (0, 0))
    if direct:
        out_shape = (kv_local * group, tok, HD)
        out_spec = pl.BlockSpec((group, tok, HD), lambda g, r: (g, 0, 0))
    else:
        out_shape = queries.shape
        out_spec = pl.BlockSpec((tok, group * HD), lambda g, r: (0, g))
    heads = kv_local * group
    return pl.pallas_call(
        functools.partial(attend_kernel, tok, group, direct),
        grid_spec=pltpu.PrefetchScalarGridSpec(
            num_scalar_prefetch=1,
            grid=(kv_local,),
            in_specs=[pl.BlockSpec((tok, group * HD), lambda g, r: (0, g))] + [head_block] * 6 + [table] * 2,
            out_specs=out_spec,
        ),
        out_shape=jax.ShapeDtypeStruct(out_shape, jnp.bfloat16),
        compiler_params=pltpu.CompilerParams(vmem_limit_bytes=VMEM_LIMIT),
        cost_estimate=pl.CostEstimate(
            flops=heads * tok * 10 * tok * HD, bytes_accessed=6 * 2**20, transcendentals=heads * tok * 2 * tok
        ),
    )(row, queries, *key_blocks, *val_blocks, cos, sin)


def ring_place(position, size):
    return jnp.where(position <= size // 2, jnp.maximum(2 * position - 1, 0), 2 * (size - position))


def ring_position(place, size):
    return jnp.where(place % 2 == 1, (place + 1) // 2, (size - place // 2) % size)


def slot_of(kind, step, where_ref, slots):
    if kind is None:
        return step * slots
    is_mine, far, near, outer = where_ref[0], where_ref[1], where_ref[2], where_ref[3]
    from_far = ring_place((ring_position(far, outer) - step + outer) % outer, outer)
    side = near if kind in ("main", "across") else 1 - near
    other = 1 - is_mine if kind in ("main", "beside") else is_mine
    return other * slots + from_far * 2 + side


def project_kernel(kinds, first, last, where_ref, own_ref, other_ref, *refs):
    count = len(kinds)
    weights, refs = refs[:count], refs[count:]
    if not first:
        partial_ref, refs = refs[0], refs[1:]
    if last:
        gain_ref, in_ref, mean_ref, refs = *refs[:3], refs[3:]
    hidden_ref, refs = refs[0], refs[1:]
    if last:
        stat_ref, refs = refs[0], refs[1:]
    heads, sems = refs
    step = pl.program_id(0)
    depth = weights[0].shape[0]
    slots = own_ref.shape[0]

    @pl.when(step == 0)
    def _():
        for n, (kind, k) in enumerate(kinds):
            slot = slot_of(kind, k, where_ref, slots)
            place = heads.at[:, n * depth : (n + 1) * depth]

            @pl.when(slot < slots)
            def _():
                pltpu.make_async_copy(own_ref.at[slot], place, sems.at[n]).start()

            @pl.when(slot >= slots)
            def _():
                pltpu.make_async_copy(other_ref.at[slot - slots], place, sems.at[n]).start()

        for n in range(count):
            place = heads.at[:, n * depth : (n + 1) * depth]
            pltpu.make_async_copy(own_ref.at[0], place, sems.at[n]).wait()

    weight = jnp.concatenate([w[...] for w in weights], 0)
    total = jnp.dot(heads[...], weight, preferred_element_type=jnp.float32)
    if not first:
        total += partial_ref[...]
    hidden_ref[...] = total
    if last:
        wide = jnp.concatenate([in_ref[...], jnp.zeros_like(in_ref)], 1)
        wide_high = wide.astype(jnp.bfloat16)
        wide_low = wide - wide_high.astype(jnp.float32)
        in_a = (wide_high.astype(jnp.float32) + pltpu.roll(wide_low, RANK, 1)).astype(jnp.bfloat16)

        def coded(field):
            code = jnp.dot(field.astype(jnp.bfloat16), in_a, preferred_element_type=jnp.float32)
            return code + pltpu.roll(code, RANK, 1)

        code = coded(total * gain_ref[...])
        square = jnp.sum(total * total, axis=1, keepdims=True)
        lane = lax.broadcasted_iota(jnp.int32, code.shape, 1)
        stat = jnp.where(lane < RANK, code, square)
        tok = stat.shape[0]
        mean = jnp.broadcast_to(mean_ref[...], (8, mean_ref.shape[1]))
        mean_high = mean.astype(jnp.bfloat16).astype(jnp.float32)
        mean_code = coded(mean_high) + coded(mean - mean_high)

        @pl.when(step == 0)
        def _():
            stat_ref[:tok, :] = stat
            stat_ref[tok:, :] = mean_code

        @pl.when(step > 0)
        def _():
            stat_ref[:tok, :] += stat
            stat_ref[tok:, :] += mean_code


def project(where, kinds, own, other, weights, partial=None, last_terms=None):
    tok = own.shape[1]
    depth, width = weights[0].shape
    count = len(weights)
    first, last = partial is None, last_terms is not None
    columns = lambda rows: pl.BlockSpec((rows, TILE), lambda j, r: (0, j))
    anywhere = pl.BlockSpec(memory_space=pl.ANY)
    in_specs = [anywhere] * 2 + [columns(depth)] * count
    operands = [where, own, other, *weights]
    out_specs = [columns(tok)]
    out_shape = [jax.ShapeDtypeStruct((tok, width), jnp.float32)]
    if not first:
        in_specs.append(columns(tok))
        operands.append(partial)
    if last:
        gain, erase_in, mean = last_terms
        in_specs += [columns(1), pl.BlockSpec((TILE, RANK), lambda j, r: (j, 0)), columns(1)]
        operands += [gain, erase_in, mean]
        out_specs.append(pl.BlockSpec((tok + 8, 2 * RANK), lambda j, r: (0, 0)))
        out_shape.append(jax.ShapeDtypeStruct((tok + 8, 2 * RANK), jnp.float32))
    return pl.pallas_call(
        functools.partial(project_kernel, kinds, first, last),
        grid_spec=pltpu.PrefetchScalarGridSpec(
            num_scalar_prefetch=1,
            grid=(width // TILE,),
            in_specs=in_specs,
            out_specs=out_specs,
            scratch_shapes=[
                pltpu.VMEM((tok, count * depth), jnp.bfloat16),
                pltpu.SemaphoreType.DMA((count,)),
            ],
        ),
        out_shape=out_shape,
        compiler_params=pltpu.CompilerParams(vmem_limit_bytes=VMEM_LIMIT),
        cost_estimate=pl.CostEstimate(
            flops=2 * tok * count * depth * width, bytes_accessed=2 * count * depth * width, transcendentals=0
        ),
    )(*operands)


def finish_kernel(model_width, own_ref, other_ref, gain_ref, out_w_ref, hidden_ref, erased_ref, packed_ref, inv_ref):
    tok = hidden_ref.shape[0]

    @pl.when(pl.program_id(0) == 0)
    def _():
        stat = own_ref[:tok, :] + other_ref[:tok, :]
        mean_code = own_ref[tok : tok + 1, :] + other_ref[tok : tok + 1, :]
        inv_rms = lax.rsqrt(stat[:, RANK : RANK + 1] / model_width + norm_eps)
        lane = lax.broadcasted_iota(jnp.int32, stat.shape, 1)
        code = jnp.where(lane < RANK, stat * inv_rms - mean_code, 0.0)
        high = code.astype(jnp.bfloat16).astype(jnp.float32)
        low = code - high
        packed_ref[...] = jnp.concatenate([high + pltpu.roll(low, RANK, 1), high], 1).astype(jnp.bfloat16)
        inv_ref[...] = jnp.broadcast_to(inv_rms, inv_ref.shape)

    removed = lax.dot_general(packed_ref[...], out_w_ref[...], NT, preferred_element_type=jnp.float32)
    normed = hidden_ref[...] * inv_ref[:, :1] * gain_ref[...]
    erased_ref[...] = (normed - removed).astype(jnp.bfloat16)


def finish(model_width, stat, stat_other, gain, out_w, hidden):
    tok, width = hidden.shape
    whole = pl.BlockSpec(stat.shape, lambda j: (0, 0))
    return pl.pallas_call(
        functools.partial(finish_kernel, model_width),
        grid=(width // TILE,),
        in_specs=[
            whole,
            whole,
            pl.BlockSpec((1, TILE), lambda j: (0, j)),
            pl.BlockSpec((TILE, 4 * RANK), lambda j: (j, 0)),
            pl.BlockSpec((tok, TILE), lambda j: (0, j)),
        ],
        out_specs=pl.BlockSpec((tok, TILE), lambda j: (0, j)),
        out_shape=jax.ShapeDtypeStruct((tok, width), jnp.bfloat16),
        scratch_shapes=[pltpu.VMEM((tok, 4 * RANK), jnp.bfloat16), pltpu.VMEM((tok, 2 * RANK), jnp.float32)],
        compiler_params=pltpu.CompilerParams(vmem_limit_bytes=VMEM_LIMIT),
        cost_estimate=pl.CostEstimate(
            flops=2 * tok * 256 * width, bytes_accessed=6 * tok * width, transcendentals=0
        ),
    )(stat, stat_other, gain, out_w, hidden)


def swapped(block, axis):
    return lax.ppermute(block, axis, [(0, 1), (1, 0)])


def ring_order(size):
    return list(range(0, 1)) + list(range(1, size, 2)) + [i for i in range(size - 1, 0, -1) if i % 2 == 0]


def on_device(queries, keys, values, out_proj, post_gain, mean_vec, erase_in, erase_out):
    tok = queries.shape[0]
    outer, inner = lax.axis_size("far"), lax.axis_size("near")
    grp, far, near, col = (lax.axis_index(a) for a in ("grp", "far", "near", "col"))
    row = far * inner + near
    depth, model_width = out_proj.shape
    width = model_width // 2
    kv_local = keys.shape[1] // HD
    heads = queries.shape[1] // HD
    direct = depth == HD and outer * inner == heads and outer == 4

    ahead = [(i, i + 1) for i in range(outer - 1)]
    from_behind = lambda block: lax.ppermute(block, "far", ahead)
    hold = lax.optimization_barrier

    def for_next(second):
        return [swapped(jnp.where(near == 0, own, old), "near") for own, old in zip((keys, values), second)]

    second = [from_behind(keys), from_behind(values)]
    theirs = swapped(lax.dynamic_slice_in_dim(out_proj, (1 - col) * width, width, 1), "col")
    mine = lax.dynamic_slice_in_dim(out_proj, col * width, width, 1)
    cos, sin = rope_tables((row - 2) * tok, 3 * tok)
    out_high, out_low = split_high_low(erase_out)
    out_w = jnp.concatenate([out_high, out_high, out_low, jnp.zeros_like(out_low)], 1)
    gain, mean = post_gain[None, :], mean_vec[None, :]
    is_mine = grp == col
    where = jnp.stack([is_mine.astype(jnp.int32), far, near, jnp.int32(outer)])

    if direct:
        order = ring_order(outer)
        hops = [(order[i], order[(i + 1) % outer]) for i in range(outer)]
        ring = lambda block: lax.ppermute(block, "far", hops)
        beyond = lambda block: swapped(block, "near")
        facing = lambda block: swapped(block, "grp")
        main, beside, across, corner = ({} for _ in range(4))
        main[0] = jnp.where(is_mine, mine, theirs)
        across[0] = jnp.where(is_mine, theirs, mine)
        beside[0] = beyond(main[0])
        second, beside[0], main[0], keys, values, cos, sin, out_w, where, gain, mean, erase_in = hold(
            (second, beside[0], main[0], keys, values, cos, sin, out_w, where, gain, mean, erase_in)
        )
        main[1], first, corner[0] = ring(main[0]), for_next(second), facing(beside[0])
        main[1], first, corner[0] = hold((main[1], first, corner[0]))
        main[2], beside[1], across[1] = ring(main[1]), beyond(main[1]), facing(main[1])
        attended = attend(row[None], queries, (second[0], first[0], keys), (second[1], first[1], values), cos, sin, True)
        main[2], beside[1], across[1], attended = hold((main[2], beside[1], across[1], attended))
        main[3], beside[2], corner[1] = ring(main[2]), beyond(main[2]), facing(beside[1])
        att_other = swapped(attended, "col")
        main[3], beside[2], corner[1], att_other = hold((main[3], beside[2], corner[1], att_other))
        across[2], beside[3], corner[2] = ring(across[1]), beyond(main[3]), facing(beside[2])
        across[2], beside[3], corner[2] = hold((across[2], beside[3], corner[2]))
        across[3], corner[3] = ring(across[2]), facing(beside[3])
        weights, kinds, late, late_kinds = [], [], [], []
        for name, pieces in (("main", main), ("beside", beside), ("across", across), ("corner", corner)):
            for k in range(outer):
                is_late = k == 3 and name in ("across", "corner")
                (late if is_late else weights).append(pieces[k])
                (late_kinds if is_late else kinds).append((name, k))
    else:
        first = for_next(second)
        attended = attend(row[None], queries, (second[0], first[0], keys), (second[1], first[1], values), cos, sin, False)
        attended = attended[None]
        att_other = swapped(attended, "col")
        weights, late = ([lax.all_gather(w, ("far", "near"), axis=0, tiled=True)] for w in (mine, theirs))
        kinds, late_kinds = [(None, 0)], [(None, 1)]

    (partial,) = project(where, kinds, attended, att_other, weights)
    hidden, stat = project(where, late_kinds, attended, att_other, late, partial, (gain, erase_in, mean))
    return finish(model_width, stat, swapped(stat, "col"), gain, out_w, hidden)


def solution(mesh):
    grp, row, col = (mesh.shape[a] for a in ("grp", "row", "col"))
    fine = Mesh(mesh.devices.reshape(grp, row // 2, 2, col), ("grp", "far", "near", "col"))
    tokens = P(("grp", "far", "near"), "col")
    placed = (tokens, tokens, tokens, P(("col", "far", "near"), None), P("col"), P("col"), P("col", None), P("col", None))
    return jax.shard_map(on_device, mesh=fine, in_specs=placed, out_specs=tokens, check_vma=False)
```

```python
import functools

import jax
import jax.numpy as jnp
from jax import lax
from jax.experimental import pallas as pl
from jax.experimental.pallas import tpu as pltpu
from jax.sharding import Mesh
from jax.sharding import PartitionSpec as P

HD = 128
WINDOW = 1024
RANK = 64

query_scale = 168.0 ** (-0.5)
norm_eps = 1e-06
rope_base = 10000.0
log2_e = 1.4426950408889634

TILE = 896
VMEM_LIMIT = 32 * 2**20

NT = (((1,), (1,)), ((), ()))


def rope_tables(first_position, count):
    half_dim = HD // 2
    inverse = jnp.exp(
        -(2.0 * jnp.arange(half_dim, dtype=jnp.float32) / HD) * jnp.log(jnp.float32(rope_base))
    )
    positions = (first_position + jnp.arange(count, dtype=jnp.int32)).astype(jnp.float32)
    angles = positions[:, None] * inverse[None, :]
    cosine, sine = jnp.cos(angles), jnp.sin(angles)
    return jnp.concatenate([cosine, cosine], 1), jnp.concatenate([-sine, sine], 1)


def attend_kernel(tok, group, direct, row_ref, q_ref, k0, k1, k2, v0, v1, v2, cos_ref, sin_ref, out_ref):
    tile = 256

    def turned(field, at):
        wide = field.astype(jnp.float32)
        cos, sin = cos_ref[at : at + tok, :], sin_ref[at : at + tok, :]
        return (wide * cos + pltpu.roll(wide, HD // 2, 1) * sin).astype(jnp.bfloat16)

    row = row_ref[0]
    bias0 = jnp.where(row >= 2, 0.0, -1e30).astype(jnp.float32)
    bias1 = jnp.where(row >= 1, 0.0, -1e30).astype(jnp.float32)
    key0, key1, key2 = turned(k0[...], 0), turned(k1[...], tok), turned(k2[...], 2 * tok)
    heads = [turned(q_ref[:, h * HD : (h + 1) * HD], 2 * tok) for h in range(group)]
    scale = query_scale * log2_e
    stacked = group * tile
    inner = lax.rem(lax.broadcasted_iota(jnp.int32, (stacked, tile), 0), tile)
    newer = lax.broadcasted_iota(jnp.int32, (stacked, tile), 1) > inner

    def dot_nt(a, b):
        return lax.dot_general(a, b, NT, preferred_element_type=jnp.float32)

    def dot(a, b):
        return jnp.dot(a, b, preferred_element_type=jnp.float32)

    for t in range(tok // tile):
        lo, hi = t * tile, (t + 1) * tile
        query = jnp.concatenate([h[lo:hi] for h in heads], 0)
        parts = [(dot_nt(query, key1) + bias1, v1[...])]
        if hi < tok:
            parts.append((dot_nt(query, key0[hi:]) + bias0, v0[hi:, :]))
        if lo > 0:
            parts.append((dot_nt(query, key2[:lo]), v2[:lo, :]))
        mixed = jnp.where(newer, dot_nt(query, key0[lo:hi]) + bias0, dot_nt(query, key2[lo:hi]))
        top = jnp.max(mixed, axis=1, keepdims=True)
        for part, _ in parts:
            top = jnp.maximum(top, jnp.max(part, axis=1, keepdims=True))
        top = top * scale
        weights = jnp.exp2(mixed * scale - top)
        total = jnp.sum(weights, axis=1, keepdims=True)
        older = jnp.where(newer, weights, 0.0)
        result = dot(older.astype(jnp.bfloat16), v0[lo:hi, :])
        result += dot((weights - older).astype(jnp.bfloat16), v2[lo:hi, :])
        for part, value in parts:
            weights = jnp.exp2(part * scale - top)
            total += jnp.sum(weights, axis=1, keepdims=True)
            result += dot(weights.astype(jnp.bfloat16), value)
        result = (result / total).astype(jnp.bfloat16)
        for h in range(group):
            block = result[h * tile : (h + 1) * tile]
            if direct:
                out_ref[h, lo:hi, :] = block
            else:
                out_ref[lo:hi, h * HD : (h + 1) * HD] = block


def attend(row, queries, blocks, cos, sin, direct):
    tok, kv_local = queries.shape[0], blocks[0].shape[1] // HD // 2
    group = queries.shape[1] // HD // kv_local
    key_block = pl.BlockSpec((tok, HD), lambda g, r: (0, g))
    val_block = pl.BlockSpec((tok, HD), lambda g, r: (0, g + kv_local))
    table = pl.BlockSpec((3 * tok, HD), lambda g, r: (0, 0))
    if direct:
        out_shape = (kv_local * group, tok, HD)
        out_spec = pl.BlockSpec((group, tok, HD), lambda g, r: (g, 0, 0))
    else:
        out_shape = queries.shape
        out_spec = pl.BlockSpec((tok, group * HD), lambda g, r: (0, g))
    heads = kv_local * group
    return pl.pallas_call(
        functools.partial(attend_kernel, tok, group, direct),
        grid_spec=pltpu.PrefetchScalarGridSpec(
            num_scalar_prefetch=1,
            grid=(kv_local,),
            in_specs=[pl.BlockSpec((tok, group * HD), lambda g, r: (0, g))] + [key_block] * 3 + [val_block] * 3 + [table] * 2,
            out_specs=out_spec,
        ),
        out_shape=jax.ShapeDtypeStruct(out_shape, jnp.bfloat16),
        compiler_params=pltpu.CompilerParams(vmem_limit_bytes=VMEM_LIMIT),
        cost_estimate=pl.CostEstimate(
            flops=heads * tok * 10 * tok * HD, bytes_accessed=6 * 2**20, transcendentals=heads * tok * 2 * tok
        ),
    )(row, queries, *blocks, *blocks, cos, sin)


def ring_place(position, size):
    return jnp.where(position <= size // 2, jnp.maximum(2 * position - 1, 0), 2 * (size - position))


def ring_position(place, size):
    return jnp.where(place % 2 == 1, (place + 1) // 2, (size - place // 2) % size)


def slot_of(kind, step, where_ref, slots):
    if kind is None:
        return step * slots
    is_mine, far, near, outer = where_ref[0], where_ref[1], where_ref[2], where_ref[3]
    from_far = ring_place((ring_position(far, outer) - step + outer) % outer, outer)
    side = near if kind in ("main", "across") else 1 - near
    other = 1 - is_mine if kind in ("main", "beside") else is_mine
    return other * slots + from_far * 2 + side


def project_kernel(kinds, first, last, where_ref, own_ref, other_ref, *refs):
    count = len(kinds)
    weights, refs = refs[:count], refs[count:]
    if not first:
        partial_ref, refs = refs[0], refs[1:]
    if last:
        gain_ref, in_ref, mean_ref, refs = *refs[:3], refs[3:]
    hidden_ref, refs = refs[0], refs[1:]
    if last:
        stat_ref, refs = refs[0], refs[1:]
    heads, sems = refs[:2]
    step = pl.program_id(0)
    depth = weights[0].shape[0]
    if not last:
        blocks, block_sems = refs[2:]
        steps = pl.num_programs(0)

        def columns_of(at, act):
            slot = lax.rem(at, 2)
            for n, piece in enumerate(weights):
                source = piece.at[:, pl.ds(pl.multiple_of(at * TILE, TILE), TILE)]
                act(pltpu.make_async_copy(source, blocks.at[slot, n * depth : (n + 1) * depth], block_sems.at[slot, n]))

        @pl.when(step == 0)
        def _():
            columns_of(step, lambda copy: copy.start())

        @pl.when(step + 1 < steps)
        def _():
            columns_of(step + 1, lambda copy: copy.start())

    slots = own_ref.shape[0]

    @pl.when(step == 0)
    def _():
        for n, (kind, k) in enumerate(kinds):
            slot = slot_of(kind, k, where_ref, slots)
            place = heads.at[:, n * depth : (n + 1) * depth]

            @pl.when(slot < slots)
            def _():
                pltpu.make_async_copy(own_ref.at[slot], place, sems.at[n]).start()

            @pl.when(slot >= slots)
            def _():
                pltpu.make_async_copy(other_ref.at[slot - slots], place, sems.at[n]).start()

        for n in range(count):
            place = heads.at[:, n * depth : (n + 1) * depth]
            pltpu.make_async_copy(own_ref.at[0], place, sems.at[n]).wait()

    if last:
        weight = jnp.concatenate([w[...] for w in weights], 0)
    else:
        columns_of(step, lambda copy: copy.wait())
        weight = blocks[lax.rem(step, 2)]
    total = jnp.dot(heads[...], weight, preferred_element_type=jnp.float32)
    if not first:
        total += partial_ref[...]
    hidden_ref[...] = total
    if last:
        in_high = in_ref[...].astype(jnp.bfloat16)
        in_low = (in_ref[...] - in_high.astype(jnp.float32)).astype(jnp.bfloat16)
        in_parts = jnp.concatenate([in_high, in_low], 0)

        def coded(field):
            code = lax.dot_general(field.astype(jnp.bfloat16), in_parts, NT, preferred_element_type=jnp.float32)
            return code + pltpu.roll(code, RANK, 1)

        code = coded(total * gain_ref[...])
        square = jnp.sum(total * total, axis=1, keepdims=True)
        lane = lax.broadcasted_iota(jnp.int32, code.shape, 1)
        stat = jnp.where(lane < RANK, code, square)
        tok = stat.shape[0]
        mean = jnp.broadcast_to(mean_ref[...], (8, mean_ref.shape[1]))
        mean_high = mean.astype(jnp.bfloat16).astype(jnp.float32)
        mean_code = coded(mean_high) + coded(mean - mean_high)

        @pl.when(step == 0)
        def _():
            stat_ref[:tok, :] = stat
            stat_ref[tok:, :] = mean_code

        @pl.when(step > 0)
        def _():
            stat_ref[:tok, :] += stat
            stat_ref[tok:, :] += mean_code


def project(where, kinds, own, other, weights, partial=None, last_terms=None):
    tok = own.shape[1]
    depth, width = weights[0].shape
    count = len(weights)
    first, last = partial is None, last_terms is not None
    columns = lambda rows: pl.BlockSpec((rows, TILE), lambda j, r: (0, j))
    in_hbm = pl.BlockSpec(memory_space=pltpu.HBM)
    in_specs = [in_hbm] * 2 + [columns(depth) if last else in_hbm] * count
    scratch = [pltpu.VMEM((tok, count * depth), jnp.bfloat16), pltpu.SemaphoreType.DMA((count,))]
    if not last:
        scratch += [pltpu.VMEM((2, count * depth, TILE), jnp.bfloat16), pltpu.SemaphoreType.DMA((2, count))]
    operands = [where, own, other, *weights]
    out_specs = [columns(tok)]
    out_shape = [jax.ShapeDtypeStruct((tok, width), jnp.float32)]
    if not first:
        in_specs.append(columns(tok))
        operands.append(partial)
    if last:
        gain, erase_in, mean = last_terms
        in_specs += [columns(1), columns(RANK), columns(1)]
        operands += [gain, erase_in, mean]
        out_specs.append(pl.BlockSpec((tok + 8, 2 * RANK), lambda j, r: (0, 0)))
        out_shape.append(jax.ShapeDtypeStruct((tok + 8, 2 * RANK), jnp.float32))
    return pl.pallas_call(
        functools.partial(project_kernel, kinds, first, last),
        grid_spec=pltpu.PrefetchScalarGridSpec(
            num_scalar_prefetch=1,
            grid=(width // TILE,),
            in_specs=in_specs,
            out_specs=out_specs,
            scratch_shapes=scratch,
        ),
        out_shape=out_shape,
        compiler_params=pltpu.CompilerParams(vmem_limit_bytes=VMEM_LIMIT),
        cost_estimate=pl.CostEstimate(
            flops=2 * tok * count * depth * width, bytes_accessed=2 * count * depth * width, transcendentals=0
        ),
    )(*operands)


def finish_kernel(model_width, own_ref, other_ref, gain_ref, out_ref, hidden_ref, erased_ref, packed_ref, inv_ref):
    tok = hidden_ref.shape[0]

    @pl.when(pl.program_id(0) == 0)
    def _():
        stat = own_ref[:tok, :] + other_ref[:tok, :]
        mean_code = own_ref[tok : tok + 1, :] + other_ref[tok : tok + 1, :]
        inv_rms = lax.rsqrt(stat[:, RANK : RANK + 1] / model_width + norm_eps)
        lane = lax.broadcasted_iota(jnp.int32, stat.shape, 1)
        code = jnp.where(lane < RANK, stat * inv_rms - mean_code, 0.0)
        high = code.astype(jnp.bfloat16).astype(jnp.float32)
        low = code - high
        packed_ref[...] = jnp.concatenate([high + pltpu.roll(low, RANK, 1), high], 1).astype(jnp.bfloat16)
        inv_ref[...] = jnp.broadcast_to(inv_rms, inv_ref.shape)

    out_high = out_ref[...].astype(jnp.bfloat16)
    out_low = (out_ref[...] - out_high.astype(jnp.float32)).astype(jnp.bfloat16)
    out_parts = jnp.concatenate([out_high, out_high, out_low, jnp.zeros_like(out_low)], 0)
    removed = jnp.dot(packed_ref[...], out_parts, preferred_element_type=jnp.float32)
    normed = hidden_ref[...] * inv_ref[:, :1] * gain_ref[...]
    erased_ref[...] = (normed - removed).astype(jnp.bfloat16)


def finish(model_width, stat, stat_other, gain, erase_out, hidden):
    tok, width = hidden.shape
    whole = pl.BlockSpec(stat.shape, lambda j: (0, 0))
    return pl.pallas_call(
        functools.partial(finish_kernel, model_width),
        grid=(width // TILE,),
        in_specs=[
            whole,
            whole,
            pl.BlockSpec((1, TILE), lambda j: (0, j)),
            pl.BlockSpec((RANK, TILE), lambda j: (0, j)),
            pl.BlockSpec((tok, TILE), lambda j: (0, j)),
        ],
        out_specs=pl.BlockSpec((tok, TILE), lambda j: (0, j)),
        out_shape=jax.ShapeDtypeStruct((tok, width), jnp.bfloat16),
        scratch_shapes=[pltpu.VMEM((tok, 4 * RANK), jnp.bfloat16), pltpu.VMEM((tok, 2 * RANK), jnp.float32)],
        compiler_params=pltpu.CompilerParams(vmem_limit_bytes=VMEM_LIMIT),
        cost_estimate=pl.CostEstimate(
            flops=2 * tok * 256 * width, bytes_accessed=6 * tok * width, transcendentals=0
        ),
    )(stat, stat_other, gain, erase_out, hidden)


def swapped(block, axis):
    return lax.ppermute(block, axis, [(0, 1), (1, 0)])


def ring_order(size):
    return list(range(0, 1)) + list(range(1, size, 2)) + [i for i in range(size - 1, 0, -1) if i % 2 == 0]


def on_device(queries, keys, values, out_proj, post_gain, mean_vec, erase_in, erase_out):
    tok = queries.shape[0]
    outer, inner = lax.axis_size("far"), lax.axis_size("near")
    grp, far, near, col = (lax.axis_index(a) for a in ("grp", "far", "near", "col"))
    row = far * inner + near
    depth, model_width = out_proj.shape
    width = model_width // 2
    kv_local = keys.shape[1] // HD
    heads = queries.shape[1] // HD
    direct = depth == HD and outer * inner == heads and outer == 4

    ahead = [(i, i + 1) for i in range(outer - 1)]
    from_behind = lambda block: lax.ppermute(block, "far", ahead)
    hold = lax.optimization_barrier

    def for_next(second):
        return swapped(jnp.where(near == 0, both, second), "near")

    both = jnp.concatenate([keys, values], 1)
    second = from_behind(both)
    theirs = swapped(lax.dynamic_slice_in_dim(out_proj, (1 - col) * width, width, 1), "col")
    mine = lax.dynamic_slice_in_dim(out_proj, col * width, width, 1)
    gain, mean = post_gain[None, :], mean_vec[None, :]
    erase_in, erase_out = erase_in.T, erase_out.T
    is_mine = grp == col
    where = jnp.stack([is_mine.astype(jnp.int32), far, near, jnp.int32(outer)])

    if direct:
        order = ring_order(outer)
        hops = [(order[i], order[(i + 1) % outer]) for i in range(outer)]
        ring = lambda block: lax.ppermute(block, "far", hops)
        beyond = lambda block: swapped(block, "near")
        facing = lambda block: swapped(block, "grp")
        main, beside, across, corner = ({} for _ in range(4))
        main[0] = jnp.where(is_mine, mine, theirs)
        across[0] = jnp.where(is_mine, theirs, mine)
        beside[0] = beyond(main[0])
        second, beside[0], main[0], row, where = hold((second, beside[0], main[0], row, where))
        main[1], first, corner[0] = ring(main[0]), for_next(second), facing(beside[0])
        cos, sin = rope_tables((row - 2) * tok, 3 * tok)
        main[1], first, corner[0], cos, sin = hold((main[1], first, corner[0], cos, sin))
        main[2], beside[1], across[1] = ring(main[1]), beyond(main[1]), facing(main[1])
        attended = attend(row[None], queries, (second, first, both), cos, sin, True)
        main[2], beside[1], across[1], attended = hold((main[2], beside[1], across[1], attended))
        main[3], beside[2], corner[1] = ring(main[2]), beyond(main[2]), facing(beside[1])
        att_other = swapped(attended, "col")
        main[3], beside[2], corner[1], att_other = hold((main[3], beside[2], corner[1], att_other))
        across[2], beside[3], corner[2] = ring(across[1]), beyond(main[3]), facing(beside[2])
        across[2], beside[3], corner[2] = hold((across[2], beside[3], corner[2]))
        across[3], corner[3] = ring(across[2]), facing(beside[3])
        weights, kinds, late, late_kinds = [], [], [], []
        for name, pieces in (("main", main), ("beside", beside), ("across", across), ("corner", corner)):
            for k in range(outer):
                is_late = k == 3 and name in ("across", "corner")
                (late if is_late else weights).append(pieces[k])
                (late_kinds if is_late else kinds).append((name, k))
    else:
        first = for_next(second)
        cos, sin = rope_tables((row - 2) * tok, 3 * tok)
        attended = attend(row[None], queries, (second, first, both), cos, sin, False)
        attended = attended[None]
        att_other = swapped(attended, "col")
        weights, late = ([lax.all_gather(w, ("far", "near"), axis=0, tiled=True)] for w in (mine, theirs))
        kinds, late_kinds = [(None, 0)], [(None, 1)]

    (partial,) = project(where, kinds, attended, att_other, weights)
    hidden, stat = project(where, late_kinds, attended, att_other, late, partial, (gain, erase_in, mean))
    return finish(model_width, stat, swapped(stat, "col"), gain, erase_out, hidden)


def solution(mesh):
    grp, row, col = (mesh.shape[a] for a in ("grp", "row", "col"))
    fine = Mesh(mesh.devices.reshape(grp, row // 2, 2, col), ("grp", "far", "near", "col"))
    tokens = P(("grp", "far", "near"), "col")
    placed = (tokens, tokens, tokens, P(("col", "far", "near"), None), P("col"), P("col"), P("col", None), P("col", None))
    return jax.shard_map(on_device, mesh=fine, in_specs=placed, out_specs=tokens, check_vma=False)
```

```python
import functools

import jax
import jax.numpy as jnp
from jax import lax
from jax.experimental import pallas as pl
from jax.experimental.pallas import tpu as pltpu
from jax.sharding import Mesh
from jax.sharding import PartitionSpec as P

HD = 128
WINDOW = 1024
RANK = 64

query_scale = 168.0 ** (-0.5)
norm_eps = 1e-06
rope_base = 10000.0
log2_e = 1.4426950408889634

TILE = 896
VMEM_LIMIT = 32 * 2**20

NT = (((1,), (1,)), ((), ()))


def rope_tables(first_position, count):
    half_dim = HD // 2
    inverse = jnp.exp(
        -(2.0 * jnp.arange(half_dim, dtype=jnp.float32) / HD) * jnp.log(jnp.float32(rope_base))
    )
    positions = (first_position + jnp.arange(count, dtype=jnp.int32)).astype(jnp.float32)
    angles = positions[:, None] * inverse[None, :]
    cosine, sine = jnp.cos(angles), jnp.sin(angles)
    return jnp.concatenate([cosine, cosine], 1), jnp.concatenate([-sine, sine], 1)


def attend_kernel(tok, group, direct, row_ref, q_ref, k0, k1, k2, v0, v1, v2, cos_ref, sin_ref, out_ref):
    tile = 256

    def turned(field, at):
        wide = field.astype(jnp.float32)
        cos, sin = cos_ref[at : at + tok, :], sin_ref[at : at + tok, :]
        return (wide * cos + pltpu.roll(wide, HD // 2, 1) * sin).astype(jnp.bfloat16)

    row = row_ref[0]
    bias0 = jnp.where(row >= 2, 0.0, -1e30).astype(jnp.float32)
    bias1 = jnp.where(row >= 1, 0.0, -1e30).astype(jnp.float32)
    key0, key1, key2 = turned(k0[...], 0), turned(k1[...], tok), turned(k2[...], 2 * tok)
    heads = [turned(q_ref[:, h * HD : (h + 1) * HD], 2 * tok) for h in range(group)]
    scale = query_scale * log2_e
    stacked = group * tile
    inner = lax.rem(lax.broadcasted_iota(jnp.int32, (stacked, tile), 0), tile)
    newer = lax.broadcasted_iota(jnp.int32, (stacked, tile), 1) > inner

    def dot_nt(a, b):
        return lax.dot_general(a, b, NT, preferred_element_type=jnp.float32)

    def dot(a, b):
        return jnp.dot(a, b, preferred_element_type=jnp.float32)

    for t in range(tok // tile):
        lo, hi = t * tile, (t + 1) * tile
        query = jnp.concatenate([h[lo:hi] for h in heads], 0)
        parts = [(dot_nt(query, key1) + bias1, v1[...])]
        if hi < tok:
            parts.append((dot_nt(query, key0[hi:]) + bias0, v0[hi:, :]))
        if lo > 0:
            parts.append((dot_nt(query, key2[:lo]), v2[:lo, :]))
        mixed = jnp.where(newer, dot_nt(query, key0[lo:hi]) + bias0, dot_nt(query, key2[lo:hi]))
        top = jnp.max(mixed, axis=1, keepdims=True)
        for part, _ in parts:
            top = jnp.maximum(top, jnp.max(part, axis=1, keepdims=True))
        top = top * scale
        weights = jnp.exp2(mixed * scale - top)
        total = jnp.sum(weights, axis=1, keepdims=True)
        older = jnp.where(newer, weights, 0.0)
        result = dot(older.astype(jnp.bfloat16), v0[lo:hi, :])
        result += dot((weights - older).astype(jnp.bfloat16), v2[lo:hi, :])
        for part, value in parts:
            weights = jnp.exp2(part * scale - top)
            total += jnp.sum(weights, axis=1, keepdims=True)
            result += dot(weights.astype(jnp.bfloat16), value)
        result = (result / total).astype(jnp.bfloat16)
        for h in range(group):
            block = result[h * tile : (h + 1) * tile]
            if direct:
                out_ref[h, lo:hi, :] = block
            else:
                out_ref[lo:hi, h * HD : (h + 1) * HD] = block


def attend(row, queries, key_blocks, val_blocks, cos, sin, direct):
    tok, kv_local = queries.shape[0], key_blocks[0].shape[1] // HD
    group = queries.shape[1] // HD // kv_local
    head_block = pl.BlockSpec((tok, HD), lambda g, r: (0, g))
    table = pl.BlockSpec((3 * tok, HD), lambda g, r: (0, 0))
    if direct:
        out_shape = (kv_local * group, tok, HD)
        out_spec = pl.BlockSpec((group, tok, HD), lambda g, r: (g, 0, 0))
    else:
        out_shape = queries.shape
        out_spec = pl.BlockSpec((tok, group * HD), lambda g, r: (0, g))
    heads = kv_local * group
    return pl.pallas_call(
        functools.partial(attend_kernel, tok, group, direct),
        grid_spec=pltpu.PrefetchScalarGridSpec(
            num_scalar_prefetch=1,
            grid=(kv_local,),
            in_specs=[pl.BlockSpec((tok, group * HD), lambda g, r: (0, g))] + [head_block] * 6 + [table] * 2,
            out_specs=out_spec,
        ),
        out_shape=jax.ShapeDtypeStruct(out_shape, jnp.bfloat16),
        compiler_params=pltpu.CompilerParams(vmem_limit_bytes=VMEM_LIMIT),
        cost_estimate=pl.CostEstimate(
            flops=heads * tok * 10 * tok * HD, bytes_accessed=6 * 2**20, transcendentals=heads * tok * 2 * tok
        ),
    )(row, queries, *key_blocks, *val_blocks, cos, sin)


def ring_place(position, size):
    return jnp.where(position <= size // 2, jnp.maximum(2 * position - 1, 0), 2 * (size - position))


def ring_position(place, size):
    return jnp.where(place % 2 == 1, (place + 1) // 2, (size - place // 2) % size)


def slot_of(kind, step, where_ref, slots):
    if kind is None:
        return step * slots
    is_mine, far, near, outer = where_ref[0], where_ref[1], where_ref[2], where_ref[3]
    from_far = ring_place((ring_position(far, outer) - step + outer) % outer, outer)
    side = near if kind in ("main", "across") else 1 - near
    other = 1 - is_mine if kind in ("main", "beside") else is_mine
    return other * slots + from_far * 2 + side


def project_kernel(kinds, first, last, where_ref, own_ref, other_ref, *refs):
    count = len(kinds)
    weights, refs = refs[:count], refs[count:]
    if not first:
        partial_ref, refs = refs[0], refs[1:]
    if last:
        gain_ref, in_ref, mean_ref, refs = *refs[:3], refs[3:]
    hidden_ref, refs = refs[0], refs[1:]
    if last:
        stat_ref, refs = refs[0], refs[1:]
    heads, sems = refs[:2]
    step = pl.program_id(0)
    depth = weights[0].shape[0]
    if not last:
        blocks, block_sems = refs[2:]
        steps = pl.num_programs(0)

        def columns_of(at, act):
            slot = lax.rem(at, 2)
            for n, piece in enumerate(weights):
                source = piece.at[:, pl.ds(pl.multiple_of(at * TILE, TILE), TILE)]
                act(pltpu.make_async_copy(source, blocks.at[slot, n * depth : (n + 1) * depth], block_sems.at[slot, n]))

        @pl.when(step == 0)
        def _():
            columns_of(step, lambda copy: copy.start())

        @pl.when(step + 1 < steps)
        def _():
            columns_of(step + 1, lambda copy: copy.start())

    slots = own_ref.shape[0]

    @pl.when(step == 0)
    def _():
        for n, (kind, k) in enumerate(kinds):
            slot = slot_of(kind, k, where_ref, slots)
            place = heads.at[:, n * depth : (n + 1) * depth]

            @pl.when(slot < slots)
            def _():
                pltpu.make_async_copy(own_ref.at[slot], place, sems.at[n]).start()

            @pl.when(slot >= slots)
            def _():
                pltpu.make_async_copy(other_ref.at[slot - slots], place, sems.at[n]).start()

        for n in range(count):
            place = heads.at[:, n * depth : (n + 1) * depth]
            pltpu.make_async_copy(own_ref.at[0], place, sems.at[n]).wait()

    if last:
        weight = jnp.concatenate([w[...] for w in weights], 0)
    else:
        columns_of(step, lambda copy: copy.wait())
        weight = blocks[lax.rem(step, 2)]
    total = jnp.dot(heads[...], weight, preferred_element_type=jnp.float32)
    if not first:
        total += partial_ref[...]
    hidden_ref[...] = total
    if last:
        in_high = in_ref[...].astype(jnp.bfloat16)
        in_low = (in_ref[...] - in_high.astype(jnp.float32)).astype(jnp.bfloat16)
        in_parts = jnp.concatenate([in_high, in_low], 0)

        def coded(field):
            code = lax.dot_general(field.astype(jnp.bfloat16), in_parts, NT, preferred_element_type=jnp.float32)
            return code + pltpu.roll(code, RANK, 1)

        code = coded(total * gain_ref[...])
        square = jnp.sum(total * total, axis=1, keepdims=True)
        lane = lax.broadcasted_iota(jnp.int32, code.shape, 1)
        stat = jnp.where(lane < RANK, code, square)
        tok = stat.shape[0]
        mean = jnp.broadcast_to(mean_ref[...], (8, mean_ref.shape[1]))
        mean_high = mean.astype(jnp.bfloat16).astype(jnp.float32)
        mean_code = coded(mean_high) + coded(mean - mean_high)

        @pl.when(step == 0)
        def _():
            stat_ref[:tok, :] = stat
            stat_ref[tok:, :] = mean_code

        @pl.when(step > 0)
        def _():
            stat_ref[:tok, :] += stat
            stat_ref[tok:, :] += mean_code


def project(where, kinds, own, other, weights, partial=None, last_terms=None):
    tok = own.shape[1]
    depth, width = weights[0].shape
    count = len(weights)
    first, last = partial is None, last_terms is not None
    columns = lambda rows: pl.BlockSpec((rows, TILE), lambda j, r: (0, j))
    in_hbm = pl.BlockSpec(memory_space=pltpu.HBM)
    in_specs = [in_hbm] * 2 + [columns(depth) if last else in_hbm] * count
    scratch = [pltpu.VMEM((tok, count * depth), jnp.bfloat16), pltpu.SemaphoreType.DMA((count,))]
    if not last:
        scratch += [pltpu.VMEM((2, count * depth, TILE), jnp.bfloat16), pltpu.SemaphoreType.DMA((2, count))]
    operands = [where, own, other, *weights]
    out_specs = [columns(tok)]
    out_shape = [jax.ShapeDtypeStruct((tok, width), jnp.float32)]
    if not first:
        in_specs.append(columns(tok))
        operands.append(partial)
    if last:
        gain, erase_in, mean = last_terms
        in_specs += [columns(1), columns(RANK), columns(1)]
        operands += [gain, erase_in, mean]
        out_specs.append(pl.BlockSpec((tok + 8, 2 * RANK), lambda j, r: (0, 0)))
        out_shape.append(jax.ShapeDtypeStruct((tok + 8, 2 * RANK), jnp.float32))
    return pl.pallas_call(
        functools.partial(project_kernel, kinds, first, last),
        grid_spec=pltpu.PrefetchScalarGridSpec(
            num_scalar_prefetch=1,
            grid=(width // TILE,),
            in_specs=in_specs,
            out_specs=out_specs,
            scratch_shapes=scratch,
        ),
        out_shape=out_shape,
        compiler_params=pltpu.CompilerParams(vmem_limit_bytes=VMEM_LIMIT),
        cost_estimate=pl.CostEstimate(
            flops=2 * tok * count * depth * width, bytes_accessed=2 * count * depth * width, transcendentals=0
        ),
    )(*operands)


def finish_kernel(model_width, own_ref, other_ref, gain_ref, out_ref, hidden_ref, erased_ref, packed_ref, inv_ref):
    tok = hidden_ref.shape[0]

    @pl.when(pl.program_id(0) == 0)
    def _():
        stat = own_ref[:tok, :] + other_ref[:tok, :]
        mean_code = own_ref[tok : tok + 1, :] + other_ref[tok : tok + 1, :]
        inv_rms = lax.rsqrt(stat[:, RANK : RANK + 1] / model_width + norm_eps)
        lane = lax.broadcasted_iota(jnp.int32, stat.shape, 1)
        code = jnp.where(lane < RANK, stat * inv_rms - mean_code, 0.0)
        high = code.astype(jnp.bfloat16).astype(jnp.float32)
        low = code - high
        packed_ref[...] = jnp.concatenate([high + pltpu.roll(low, RANK, 1), high], 1).astype(jnp.bfloat16)
        inv_ref[...] = jnp.broadcast_to(inv_rms, inv_ref.shape)

    out_high = out_ref[...].astype(jnp.bfloat16)
    out_low = (out_ref[...] - out_high.astype(jnp.float32)).astype(jnp.bfloat16)
    out_parts = jnp.concatenate([out_high, out_high, out_low, jnp.zeros_like(out_low)], 0)
    removed = jnp.dot(packed_ref[...], out_parts, preferred_element_type=jnp.float32)
    normed = hidden_ref[...] * inv_ref[:, :1] * gain_ref[...]
    erased_ref[...] = (normed - removed).astype(jnp.bfloat16)


def finish(model_width, stat, stat_other, gain, erase_out, hidden):
    tok, width = hidden.shape
    whole = pl.BlockSpec(stat.shape, lambda j: (0, 0))
    return pl.pallas_call(
        functools.partial(finish_kernel, model_width),
        grid=(width // TILE,),
        in_specs=[
            whole,
            whole,
            pl.BlockSpec((1, TILE), lambda j: (0, j)),
            pl.BlockSpec((RANK, TILE), lambda j: (0, j)),
            pl.BlockSpec((tok, TILE), lambda j: (0, j)),
        ],
        out_specs=pl.BlockSpec((tok, TILE), lambda j: (0, j)),
        out_shape=jax.ShapeDtypeStruct((tok, width), jnp.bfloat16),
        scratch_shapes=[pltpu.VMEM((tok, 4 * RANK), jnp.bfloat16), pltpu.VMEM((tok, 2 * RANK), jnp.float32)],
        compiler_params=pltpu.CompilerParams(vmem_limit_bytes=VMEM_LIMIT),
        cost_estimate=pl.CostEstimate(
            flops=2 * tok * 256 * width, bytes_accessed=6 * tok * width, transcendentals=0
        ),
    )(stat, stat_other, gain, erase_out, hidden)


def swapped(block, axis):
    return lax.ppermute(block, axis, [(0, 1), (1, 0)])


def ring_order(size):
    return list(range(0, 1)) + list(range(1, size, 2)) + [i for i in range(size - 1, 0, -1) if i % 2 == 0]


def on_device(queries, keys, values, out_proj, post_gain, mean_vec, erase_in, erase_out):
    tok = queries.shape[0]
    outer, inner = lax.axis_size("far"), lax.axis_size("near")
    grp, far, near, col = (lax.axis_index(a) for a in ("grp", "far", "near", "col"))
    row = far * inner + near
    depth, model_width = out_proj.shape
    width = model_width // 2
    kv_local = keys.shape[1] // HD
    heads = queries.shape[1] // HD
    direct = depth == HD and outer * inner == heads and outer == 4

    ahead = [(i, i + 1) for i in range(outer - 1)]
    from_behind = lambda block: lax.ppermute(block, "far", ahead)
    hold = lax.optimization_barrier

    def for_next(own, second):
        return swapped(jnp.where(near == 0, own, second), "near")

    def after(block, *earlier):
        return hold((block, earlier))[0]

    theirs = swapped(lax.dynamic_slice_in_dim(out_proj, (1 - col) * width, width, 1), "col")
    mine = lax.dynamic_slice_in_dim(out_proj, col * width, width, 1)
    gain, mean = post_gain[None, :], mean_vec[None, :]
    erase_in, erase_out = erase_in.T, erase_out.T
    is_mine = grp == col
    where = jnp.stack([is_mine.astype(jnp.int32), far, near, jnp.int32(outer)])

    if direct:
        order = ring_order(outer)
        hops = [(order[i], order[(i + 1) % outer]) for i in range(outer)]
        ring = lambda block: lax.ppermute(block, "far", hops)
        beyond = lambda block: swapped(block, "near")
        facing = lambda block: swapped(block, "grp")
        main, beside, across, corner = ({} for _ in range(4))
        main[0] = jnp.where(is_mine, mine, theirs)
        across[0] = jnp.where(is_mine, theirs, mine)
        beside[0] = beyond(main[0])
        second_keys = from_behind(after(keys, main[0]))
        second_values = from_behind(after(values, second_keys))
        first_keys = for_next(keys, after(second_keys, beside[0]))
        corner[0] = facing(beside[0])
        main[1] = ring(after(main[0], second_values))
        first_values = for_next(values, after(second_values, first_keys))
        cos, sin = rope_tables((after(row, beside[0]) - 2) * tok, 3 * tok)
        main[1], first_keys, first_values, corner[0], cos, sin, where = hold(
            (main[1], first_keys, first_values, corner[0], cos, sin, where)
        )
        main[2], beside[1], across[1] = ring(main[1]), beyond(main[1]), facing(main[1])
        attended = attend(
            row[None], queries, (second_keys, first_keys, keys), (second_values, first_values, values), cos, sin, True
        )
        main[2], beside[1], across[1], attended = hold((main[2], beside[1], across[1], attended))
        main[3], beside[2], corner[1] = ring(main[2]), beyond(main[2]), facing(beside[1])
        att_other = swapped(attended, "col")
        main[3], beside[2], corner[1], att_other, across[1] = hold(
            (main[3], beside[2], corner[1], att_other, across[1])
        )
        across[2], beside[3], corner[2] = ring(across[1]), beyond(main[3]), facing(beside[2])
        across[2], beside[3], corner[2] = hold((across[2], beside[3], corner[2]))
        across[3], corner[3] = ring(across[2]), facing(beside[3])
        weights, kinds, late, late_kinds = [], [], [], []
        for name, pieces in (("main", main), ("beside", beside), ("across", across), ("corner", corner)):
            for k in range(outer):
                is_late = k == 3 and name in ("across", "corner")
                (late if is_late else weights).append(pieces[k])
                (late_kinds if is_late else kinds).append((name, k))
    else:
        second_keys, second_values = from_behind(keys), from_behind(values)
        first_keys, first_values = for_next(keys, second_keys), for_next(values, second_values)
        cos, sin = rope_tables((row - 2) * tok, 3 * tok)
        attended = attend(
            row[None], queries, (second_keys, first_keys, keys), (second_values, first_values, values), cos, sin, False
        )
        attended = attended[None]
        att_other = swapped(attended, "col")
        weights, late = ([lax.all_gather(w, ("far", "near"), axis=0, tiled=True)] for w in (mine, theirs))
        kinds, late_kinds = [(None, 0)], [(None, 1)]

    (partial,) = project(where, kinds, attended, att_other, weights)
    hidden, stat = project(where, late_kinds, attended, att_other, late, partial, (gain, erase_in, mean))
    return finish(model_width, stat, swapped(stat, "col"), gain, erase_out, hidden)


def solution(mesh):
    grp, row, col = (mesh.shape[a] for a in ("grp", "row", "col"))
    fine = Mesh(mesh.devices.reshape(grp, row // 2, 2, col), ("grp", "far", "near", "col"))
    tokens = P(("grp", "far", "near"), "col")
    placed = (tokens, tokens, tokens, P(("col", "far", "near"), None), P("col"), P("col"), P("col", None), P("col", None))
    return jax.shard_map(on_device, mesh=fine, in_specs=placed, out_specs=tokens, check_vma=False)
```

```python
import functools

import jax
import jax.numpy as jnp
from jax import lax
from jax.experimental import pallas as pl
from jax.experimental.pallas import tpu as pltpu
from jax.sharding import Mesh
from jax.sharding import PartitionSpec as P

HD = 128
WINDOW = 1024
RANK = 64

query_scale = 168.0 ** (-0.5)
norm_eps = 1e-06
rope_base = 10000.0
log2_e = 1.4426950408889634

TILE = 896
VMEM_LIMIT = 32 * 2**20

NT = (((1,), (1,)), ((), ()))


def rope_tables(first_position, count):
    half_dim = HD // 2
    inverse = jnp.exp(
        -(2.0 * jnp.arange(half_dim, dtype=jnp.float32) / HD) * jnp.log(jnp.float32(rope_base))
    )
    positions = (first_position + jnp.arange(count, dtype=jnp.int32)).astype(jnp.float32)
    angles = positions[:, None] * inverse[None, :]
    cosine, sine = jnp.cos(angles), jnp.sin(angles)
    return jnp.concatenate([cosine, cosine], 1), jnp.concatenate([-sine, sine], 1)


def attend_kernel(tok, group, direct, row_ref, q_ref, k0, k1, k2, v0, v1, v2, cos_ref, sin_ref, out_ref):
    tile = 256

    def turned(field, at):
        wide = field.astype(jnp.float32)
        cos, sin = cos_ref[at : at + tok, :], sin_ref[at : at + tok, :]
        return (wide * cos + pltpu.roll(wide, HD // 2, 1) * sin).astype(jnp.bfloat16)

    row = row_ref[0]
    bias0 = jnp.where(row >= 2, 0.0, -1e30).astype(jnp.float32)
    bias1 = jnp.where(row >= 1, 0.0, -1e30).astype(jnp.float32)
    key0, key1, key2 = turned(k0[...], 0), turned(k1[...], tok), turned(k2[...], 2 * tok)
    heads = [turned(q_ref[:, h * HD : (h + 1) * HD], 2 * tok) for h in range(group)]
    scale = query_scale * log2_e
    stacked = group * tile
    inner = lax.rem(lax.broadcasted_iota(jnp.int32, (stacked, tile), 0), tile)
    newer = lax.broadcasted_iota(jnp.int32, (stacked, tile), 1) > inner

    def dot_nt(a, b):
        return lax.dot_general(a, b, NT, preferred_element_type=jnp.float32)

    def dot(a, b):
        return jnp.dot(a, b, preferred_element_type=jnp.float32)

    for t in range(tok // tile):
        lo, hi = t * tile, (t + 1) * tile
        query = jnp.concatenate([h[lo:hi] for h in heads], 0)
        parts = [(dot_nt(query, key1) + bias1, v1[...])]
        if hi < tok:
            parts.append((dot_nt(query, key0[hi:]) + bias0, v0[hi:, :]))
        if lo > 0:
            parts.append((dot_nt(query, key2[:lo]), v2[:lo, :]))
        mixed = jnp.where(newer, dot_nt(query, key0[lo:hi]) + bias0, dot_nt(query, key2[lo:hi]))
        top = jnp.max(mixed, axis=1, keepdims=True)
        for part, _ in parts:
            top = jnp.maximum(top, jnp.max(part, axis=1, keepdims=True))
        top = top * scale
        weights = jnp.exp2(mixed * scale - top)
        total = jnp.sum(weights, axis=1, keepdims=True)
        older = jnp.where(newer, weights, 0.0)
        result = dot(older.astype(jnp.bfloat16), v0[lo:hi, :])
        result += dot((weights - older).astype(jnp.bfloat16), v2[lo:hi, :])
        for part, value in parts:
            weights = jnp.exp2(part * scale - top)
            total += jnp.sum(weights, axis=1, keepdims=True)
            result += dot(weights.astype(jnp.bfloat16), value)
        result = (result / total).astype(jnp.bfloat16)
        for h in range(group):
            block = result[h * tile : (h + 1) * tile]
            if direct:
                out_ref[h, lo:hi, :] = block
            else:
                out_ref[lo:hi, h * HD : (h + 1) * HD] = block


def attend(row, queries, key_blocks, val_blocks, cos, sin, direct):
    tok, kv_local = queries.shape[0], key_blocks[0].shape[1] // HD
    group = queries.shape[1] // HD // kv_local
    head_block = pl.BlockSpec((tok, HD), lambda g, r: (0, g))
    table = pl.BlockSpec((3 * tok, HD), lambda g, r: (0, 0))
    if direct:
        out_shape = (kv_local * group, tok, HD)
        out_spec = pl.BlockSpec((group, tok, HD), lambda g, r: (g, 0, 0))
    else:
        out_shape = queries.shape
        out_spec = pl.BlockSpec((tok, group * HD), lambda g, r: (0, g))
    heads = kv_local * group
    return pl.pallas_call(
        functools.partial(attend_kernel, tok, group, direct),
        grid_spec=pltpu.PrefetchScalarGridSpec(
            num_scalar_prefetch=1,
            grid=(kv_local,),
            in_specs=[pl.BlockSpec((tok, group * HD), lambda g, r: (0, g))] + [head_block] * 6 + [table] * 2,
            out_specs=out_spec,
        ),
        out_shape=jax.ShapeDtypeStruct(out_shape, jnp.bfloat16),
        compiler_params=pltpu.CompilerParams(vmem_limit_bytes=VMEM_LIMIT),
        cost_estimate=pl.CostEstimate(
            flops=4 * heads * tok * 10 * tok * HD, bytes_accessed=6 * 2**20, transcendentals=heads * tok * 2 * tok
        ),
    )(row, queries, *key_blocks, *val_blocks, cos, sin)


def ring_place(position, size):
    return jnp.where(position <= size // 2, jnp.maximum(2 * position - 1, 0), 2 * (size - position))


def ring_position(place, size):
    return jnp.where(place % 2 == 1, (place + 1) // 2, (size - place // 2) % size)


def slot_of(kind, step, where_ref, slots):
    if kind is None:
        return step * slots
    is_mine, far, near, outer = where_ref[0], where_ref[1], where_ref[2], where_ref[3]
    from_far = ring_place((ring_position(far, outer) - step + outer) % outer, outer)
    side = near if kind in ("main", "across") else 1 - near
    other = 1 - is_mine if kind in ("main", "beside") else is_mine
    return other * slots + from_far * 2 + side


def parts_of(kinds):
    return sum(1 if kind is None else 2 for kind, _ in kinds)


def project_kernel(kinds, first, last, where_ref, own_ref, other_ref, *refs):
    count, parts = len(kinds), parts_of(kinds)
    weights, refs = refs[:parts], refs[parts:]
    if not first:
        partial_ref, refs = refs[0], refs[1:]
    if last:
        gain_ref, in_ref, mean_ref, refs = *refs[:3], refs[3:]
    hidden_ref, refs = refs[0], refs[1:]
    if last:
        stat_ref, refs = refs[0], refs[1:]
    heads, sems = refs[:2]
    step = pl.program_id(0)
    share = weights[0].shape[0]
    depth = parts // count * share
    if not last:
        blocks, block_sems = refs[2:]
        steps = pl.num_programs(0)

        def columns_of(at, act):
            slot = lax.rem(at, 2)
            for n, piece in enumerate(weights):
                source = piece.at[:, pl.ds(pl.multiple_of(at * TILE, TILE), TILE)]
                act(pltpu.make_async_copy(source, blocks.at[slot, n * share : (n + 1) * share], block_sems.at[slot, n]))

        @pl.when(step == 0)
        def _():
            columns_of(step, lambda copy: copy.start())

        @pl.when(step + 1 < steps)
        def _():
            columns_of(step + 1, lambda copy: copy.start())

    slots = own_ref.shape[0]

    @pl.when(step == 0)
    def _():
        for n, (kind, k) in enumerate(kinds):
            slot = slot_of(kind, k, where_ref, slots)
            place = heads.at[:, n * depth : (n + 1) * depth]

            @pl.when(slot < slots)
            def _():
                pltpu.make_async_copy(own_ref.at[slot], place, sems.at[n]).start()

            @pl.when(slot >= slots)
            def _():
                pltpu.make_async_copy(other_ref.at[slot - slots], place, sems.at[n]).start()

        for n in range(count):
            place = heads.at[:, n * depth : (n + 1) * depth]
            pltpu.make_async_copy(own_ref.at[0], place, sems.at[n]).wait()

    if last:
        weight = jnp.concatenate([w[...] for w in weights], 0)
    else:
        columns_of(step, lambda copy: copy.wait())
        weight = blocks[lax.rem(step, 2)]
    total = jnp.dot(heads[...], weight, preferred_element_type=jnp.float32)
    if not first:
        total += partial_ref[...]
    hidden_ref[...] = total
    if last:
        in_high = in_ref[...].astype(jnp.bfloat16)
        in_low = (in_ref[...] - in_high.astype(jnp.float32)).astype(jnp.bfloat16)
        in_parts = jnp.concatenate([in_high, in_low], 0)

        def coded(field):
            code = lax.dot_general(field.astype(jnp.bfloat16), in_parts, NT, preferred_element_type=jnp.float32)
            return code + pltpu.roll(code, RANK, 1)

        code = coded(total * gain_ref[...])
        square = jnp.sum(total * total, axis=1, keepdims=True)
        lane = lax.broadcasted_iota(jnp.int32, code.shape, 1)
        stat = jnp.where(lane < RANK, code, square)
        tok = stat.shape[0]
        mean = jnp.broadcast_to(mean_ref[...], (8, mean_ref.shape[1]))
        mean_high = mean.astype(jnp.bfloat16).astype(jnp.float32)
        mean_code = coded(mean_high) + coded(mean - mean_high)

        @pl.when(step == 0)
        def _():
            stat_ref[:tok, :] = stat
            stat_ref[tok:, :] = mean_code

        @pl.when(step > 0)
        def _():
            stat_ref[:tok, :] += stat
            stat_ref[tok:, :] += mean_code


def project(where, kinds, own, other, weights, partial=None, last_terms=None):
    tok = own.shape[1]
    share, width = weights[0].shape
    parts, count = len(weights), len(kinds)
    depth = parts // count * share
    first, last = partial is None, last_terms is not None
    columns = lambda rows: pl.BlockSpec((rows, TILE), lambda j, r: (0, j))
    in_hbm = pl.BlockSpec(memory_space=pltpu.HBM)
    in_specs = [in_hbm] * 2 + [columns(share) if last else in_hbm] * parts
    scratch = [pltpu.VMEM((tok, count * depth), jnp.bfloat16), pltpu.SemaphoreType.DMA((count,))]
    if not last:
        scratch += [pltpu.VMEM((2, count * depth, TILE), jnp.bfloat16), pltpu.SemaphoreType.DMA((2, parts))]
    operands = [where, own, other, *weights]
    out_specs = [columns(tok)]
    out_shape = [jax.ShapeDtypeStruct((tok, width), jnp.float32)]
    if not first:
        in_specs.append(columns(tok))
        operands.append(partial)
    if last:
        gain, erase_in, mean = last_terms
        in_specs += [columns(1), columns(RANK), columns(1)]
        operands += [gain, erase_in, mean]
        out_specs.append(pl.BlockSpec((tok + 8, 2 * RANK), lambda j, r: (0, 0)))
        out_shape.append(jax.ShapeDtypeStruct((tok + 8, 2 * RANK), jnp.float32))
    return pl.pallas_call(
        functools.partial(project_kernel, kinds, first, last),
        grid_spec=pltpu.PrefetchScalarGridSpec(
            num_scalar_prefetch=1,
            grid=(width // TILE,),
            in_specs=in_specs,
            out_specs=out_specs,
            scratch_shapes=scratch,
        ),
        out_shape=out_shape,
        compiler_params=pltpu.CompilerParams(vmem_limit_bytes=VMEM_LIMIT),
        cost_estimate=pl.CostEstimate(
            flops=2 * tok * count * depth * width, bytes_accessed=2 * count * depth * width, transcendentals=0
        ),
    )(*operands)


def finish_kernel(model_width, own_ref, other_ref, gain_ref, out_ref, hidden_ref, erased_ref, packed_ref, inv_ref):
    tok = hidden_ref.shape[0]

    @pl.when(pl.program_id(0) == 0)
    def _():
        stat = own_ref[:tok, :] + other_ref[:tok, :]
        mean_code = own_ref[tok : tok + 1, :] + other_ref[tok : tok + 1, :]
        inv_rms = lax.rsqrt(stat[:, RANK : RANK + 1] / model_width + norm_eps)
        lane = lax.broadcasted_iota(jnp.int32, stat.shape, 1)
        code = jnp.where(lane < RANK, stat * inv_rms - mean_code, 0.0)
        high = code.astype(jnp.bfloat16).astype(jnp.float32)
        low = code - high
        packed_ref[...] = jnp.concatenate([high + pltpu.roll(low, RANK, 1), high], 1).astype(jnp.bfloat16)
        inv_ref[...] = jnp.broadcast_to(inv_rms, inv_ref.shape)

    out_high = out_ref[...].astype(jnp.bfloat16)
    out_low = (out_ref[...] - out_high.astype(jnp.float32)).astype(jnp.bfloat16)
    out_parts = jnp.concatenate([out_high, out_high, out_low, jnp.zeros_like(out_low)], 0)
    removed = jnp.dot(packed_ref[...], out_parts, preferred_element_type=jnp.float32)
    normed = hidden_ref[...] * inv_ref[:, :1] * gain_ref[...]
    erased_ref[...] = (normed - removed).astype(jnp.bfloat16)


def finish(model_width, stat, stat_other, gain, erase_out, hidden):
    tok, width = hidden.shape
    whole = pl.BlockSpec(stat.shape, lambda j: (0, 0))
    return pl.pallas_call(
        functools.partial(finish_kernel, model_width),
        grid=(width // TILE,),
        in_specs=[
            whole,
            whole,
            pl.BlockSpec((1, TILE), lambda j: (0, j)),
            pl.BlockSpec((RANK, TILE), lambda j: (0, j)),
            pl.BlockSpec((tok, TILE), lambda j: (0, j)),
        ],
        out_specs=pl.BlockSpec((tok, TILE), lambda j: (0, j)),
        out_shape=jax.ShapeDtypeStruct((tok, width), jnp.bfloat16),
        scratch_shapes=[pltpu.VMEM((tok, 4 * RANK), jnp.bfloat16), pltpu.VMEM((tok, 2 * RANK), jnp.float32)],
        compiler_params=pltpu.CompilerParams(vmem_limit_bytes=VMEM_LIMIT),
        cost_estimate=pl.CostEstimate(
            flops=2 * tok * 256 * width, bytes_accessed=6 * tok * width, transcendentals=0
        ),
    )(stat, stat_other, gain, erase_out, hidden)


def swapped(block, axis):
    return lax.ppermute(block, axis, [(0, 1), (1, 0)])


def ring_order(size):
    return list(range(0, 1)) + list(range(1, size, 2)) + [i for i in range(size - 1, 0, -1) if i % 2 == 0]


def on_device(queries, keys, values, out_proj, post_gain, mean_vec, erase_in, erase_out):
    tok = queries.shape[0]
    outer, inner = lax.axis_size("far"), lax.axis_size("near")
    grp, far, near, col = (lax.axis_index(a) for a in ("grp", "far", "near", "col"))
    row = far * inner + near
    depth, model_width = out_proj.shape
    width = model_width // 2
    kv_local = keys.shape[1] // HD
    heads = queries.shape[1] // HD
    direct = depth == HD and outer * inner == heads and outer == 4

    ahead = [(i, i + 1) for i in range(outer - 1)]
    from_behind = lambda block: lax.ppermute(block, "far", ahead)
    hold = lax.optimization_barrier

    def for_next(own, second):
        return swapped(jnp.where(near == 0, own, second), "near")

    def after(block, *earlier):
        return hold((block, earlier))[0]

    theirs = swapped(lax.dynamic_slice_in_dim(out_proj, (1 - col) * width, width, 1), "col")
    mine = lax.dynamic_slice_in_dim(out_proj, col * width, width, 1)
    gain, mean = post_gain[None, :], mean_vec[None, :]
    erase_in, erase_out = erase_in.T, erase_out.T
    is_mine = grp == col
    where = jnp.stack([is_mine.astype(jnp.int32), far, near, jnp.int32(outer)])

    if direct:
        order = ring_order(outer)
        hops = [(order[i], order[(i + 1) % outer]) for i in range(outer)]
        queues = {"far": [], "near": [], "grp": []}

        def send(axis, block, *earlier, route=((0, 1), (1, 0))):
            queue = queues[axis]
            waits = (*earlier, *queue[-2:-1])
            queue.append(lax.ppermute(after(block, *waits) if waits else block, axis, route))
            return queue[-1]

        ring = lambda block, *earlier: send("far", block, *earlier, route=hops)
        beyond = lambda block, *earlier: send("near", block, *earlier)
        facing = lambda block, *earlier: send("grp", block, *earlier)
        main, beside, across, corner = ({} for _ in range(4))
        rows = [slice(0, depth // 2), slice(depth // 2, depth)]
        main[0] = [jnp.where(is_mine, mine[r], theirs[r]) for r in rows]
        across[0] = [jnp.where(is_mine, theirs[r], mine[r]) for r in rows]
        beside[0] = [beyond(half) for half in main[0]]
        second_keys = send("far", keys, main[0], route=ahead)
        second_values = send("far", values, beside[0][0], route=ahead)
        cos, sin = rope_tables((after(row, beside[0], second_keys) - 2) * tok, 3 * tok)
        first_keys = beyond(jnp.where(near == 0, keys, after(second_keys, beside[0])))
        corner[0] = [facing(half) for half in beside[0]]
        main[1] = [ring(main[0][0], beside[0]), ring(main[0][1])]
        first_values = beyond(jnp.where(near == 0, values, second_values))
        beside[1] = [beyond(half) for half in main[1]]
        across[1] = [facing(half) for half in main[1]]
        main[2] = [ring(half) for half in main[1]]
        corner[1] = [facing(half) for half in beside[1]]
        attended = attend(
            row[None], queries, (second_keys, first_keys, keys), (second_values, first_values, values), cos, sin, True
        )
        main[3] = [ring(main[2][0], attended), ring(main[2][1])]
        beside[2] = [beyond(half) for half in main[2]]
        corner[2] = [facing(half) for half in beside[2]]
        att_other = swapped(attended, "col")
        beside[3] = [beyond(half) for half in main[3]]
        across[2] = [ring(half) for half in across[1]]
        across[3] = [ring(half) for half in across[2]]
        corner[3] = [facing(half) for half in beside[3]]
        weights, kinds, late, late_kinds = [], [], [], []
        for name, pieces in (("main", main), ("beside", beside), ("across", across), ("corner", corner)):
            for k in range(outer):
                is_late = k == 3 and name in ("across", "corner")
                (late if is_late else weights).extend(pieces[k])
                (late_kinds if is_late else kinds).append((name, k))
    else:
        second_keys, second_values = from_behind(keys), from_behind(values)
        first_keys, first_values = for_next(keys, second_keys), for_next(values, second_values)
        cos, sin = rope_tables((row - 2) * tok, 3 * tok)
        attended = attend(
            row[None], queries, (second_keys, first_keys, keys), (second_values, first_values, values), cos, sin, False
        )
        attended = attended[None]
        att_other = swapped(attended, "col")
        weights, late = ([lax.all_gather(w, ("far", "near"), axis=0, tiled=True)] for w in (mine, theirs))
        kinds, late_kinds = [(None, 0)], [(None, 1)]

    (partial,) = project(where, kinds, attended, att_other, weights)
    hidden, stat = project(where, late_kinds, attended, att_other, late, partial, (gain, erase_in, mean))
    return finish(model_width, stat, swapped(stat, "col"), gain, erase_out, hidden)


def solution(mesh):
    grp, row, col = (mesh.shape[a] for a in ("grp", "row", "col"))
    fine = Mesh(mesh.devices.reshape(grp, row // 2, 2, col), ("grp", "far", "near", "col"))
    tokens = P(("grp", "far", "near"), "col")
    placed = (tokens, tokens, tokens, P(("col", "far", "near"), None), P("col"), P("col"), P("col", None), P("col", None))
    return jax.shard_map(on_device, mesh=fine, in_specs=placed, out_specs=tokens, check_vma=False)
```

```python
import functools

import jax
import jax.numpy as jnp
from jax import lax
from jax.experimental import pallas as pl
from jax.experimental.pallas import tpu as pltpu
from jax.sharding import Mesh
from jax.sharding import PartitionSpec as P

HD = 128
WINDOW = 1024
RANK = 64

query_scale = 168.0 ** (-0.5)
norm_eps = 1e-06
rope_base = 10000.0
log2_e = 1.4426950408889634

TILE = 896
VMEM_LIMIT = 32 * 2**20

NT = (((1,), (1,)), ((), ()))


def rope_tables(first_position, count):
    half_dim = HD // 2
    inverse = jnp.exp(
        -(2.0 * jnp.arange(half_dim, dtype=jnp.float32) / HD) * jnp.log(jnp.float32(rope_base))
    )
    positions = (first_position + jnp.arange(count, dtype=jnp.int32)).astype(jnp.float32)
    angles = positions[:, None] * inverse[None, :]
    cosine, sine = jnp.cos(angles), jnp.sin(angles)
    return jnp.concatenate([cosine, cosine], 1), jnp.concatenate([-sine, sine], 1)


def attend_kernel(tok, group, direct, row_ref, q_ref, k0, k1, k2, v0, v1, v2, cos_ref, sin_ref, out_ref):
    tile = 256

    def turned(field, at):
        wide = field.astype(jnp.float32)
        cos, sin = cos_ref[at : at + tok, :], sin_ref[at : at + tok, :]
        return (wide * cos + pltpu.roll(wide, HD // 2, 1) * sin).astype(jnp.bfloat16)

    row = row_ref[0]
    bias0 = jnp.where(row >= 2, 0.0, -1e30).astype(jnp.float32)
    bias1 = jnp.where(row >= 1, 0.0, -1e30).astype(jnp.float32)
    key0, key1, key2 = turned(k0[...], 0), turned(k1[...], tok), turned(k2[...], 2 * tok)
    heads = [turned(q_ref[:, h * HD : (h + 1) * HD], 2 * tok) for h in range(group)]
    scale = query_scale * log2_e
    stacked = group * tile
    inner = lax.rem(lax.broadcasted_iota(jnp.int32, (stacked, tile), 0), tile)
    newer = lax.broadcasted_iota(jnp.int32, (stacked, tile), 1) > inner

    def dot_nt(a, b):
        return lax.dot_general(a, b, NT, preferred_element_type=jnp.float32)

    def dot(a, b):
        return jnp.dot(a, b, preferred_element_type=jnp.float32)

    for t in range(tok // tile):
        lo, hi = t * tile, (t + 1) * tile
        query = jnp.concatenate([h[lo:hi] for h in heads], 0)
        parts = [(dot_nt(query, key1) + bias1, v1[...])]
        if hi < tok:
            parts.append((dot_nt(query, key0[hi:]) + bias0, v0[hi:, :]))
        if lo > 0:
            parts.append((dot_nt(query, key2[:lo]), v2[:lo, :]))
        mixed = jnp.where(newer, dot_nt(query, key0[lo:hi]) + bias0, dot_nt(query, key2[lo:hi]))
        top = jnp.max(mixed, axis=1, keepdims=True)
        for part, _ in parts:
            top = jnp.maximum(top, jnp.max(part, axis=1, keepdims=True))
        top = top * scale
        weights = jnp.exp2(mixed * scale - top)
        total = jnp.sum(weights, axis=1, keepdims=True)
        older = jnp.where(newer, weights, 0.0)
        result = dot(older.astype(jnp.bfloat16), v0[lo:hi, :])
        result += dot((weights - older).astype(jnp.bfloat16), v2[lo:hi, :])
        for part, value in parts:
            weights = jnp.exp2(part * scale - top)
            total += jnp.sum(weights, axis=1, keepdims=True)
            result += dot(weights.astype(jnp.bfloat16), value)
        result = (result / total).astype(jnp.bfloat16)
        for h in range(group):
            block = result[h * tile : (h + 1) * tile]
            if direct:
                out_ref[h, lo:hi, :] = block
            else:
                out_ref[lo:hi, h * HD : (h + 1) * HD] = block


def attend(row, queries, key_blocks, val_blocks, cos, sin, direct, first=0, count=None):
    tok, kv_local = queries.shape[0], key_blocks[0].shape[1] // HD
    group = queries.shape[1] // HD // kv_local
    count = kv_local if count is None else count
    head_block = pl.BlockSpec((tok, HD), lambda g, r: (0, g + first))
    table = pl.BlockSpec((3 * tok, HD), lambda g, r: (0, 0))
    if direct:
        out_shape = (count * group, tok, HD)
        out_spec = pl.BlockSpec((group, tok, HD), lambda g, r: (g, 0, 0))
    else:
        out_shape = queries.shape
        out_spec = pl.BlockSpec((tok, group * HD), lambda g, r: (0, g))
    heads = count * group
    return pl.pallas_call(
        functools.partial(attend_kernel, tok, group, direct),
        grid_spec=pltpu.PrefetchScalarGridSpec(
            num_scalar_prefetch=1,
            grid=(count,),
            in_specs=[pl.BlockSpec((tok, group * HD), lambda g, r: (0, g + first))] + [head_block] * 6 + [table] * 2,
            out_specs=out_spec,
        ),
        out_shape=jax.ShapeDtypeStruct(out_shape, jnp.bfloat16),
        compiler_params=pltpu.CompilerParams(vmem_limit_bytes=VMEM_LIMIT),
        cost_estimate=pl.CostEstimate(
            flops=4 * heads * tok * 10 * tok * HD, bytes_accessed=6 * 2**20, transcendentals=heads * tok * 2 * tok
        ),
    )(row, queries, *key_blocks, *val_blocks, cos, sin)


def ring_place(position, size):
    return jnp.where(position <= size // 2, jnp.maximum(2 * position - 1, 0), 2 * (size - position))


def ring_position(place, size):
    return jnp.where(place % 2 == 1, (place + 1) // 2, (size - place // 2) % size)


def slot_of(kind, step, where_ref, slots):
    if kind is None:
        return step * slots
    is_mine, far, near, outer = where_ref[0], where_ref[1], where_ref[2], where_ref[3]
    from_far = ring_place((ring_position(far, outer) - step + outer) % outer, outer)
    side = near if kind in ("main", "across") else 1 - near
    other = 1 - is_mine if kind in ("main", "beside") else is_mine
    return other * slots + from_far * 2 + side


def project_kernel(kinds, sources, parts, first, last, where_ref, *refs):
    count = len(kinds)
    sources, refs = refs[:sources], refs[sources:]
    weights, refs = refs[: len(parts)], refs[len(parts) :]
    if not first:
        partial_ref, refs = refs[0], refs[1:]
    if last:
        gain_ref, in_ref, mean_ref, refs = *refs[:3], refs[3:]
    hidden_ref, refs = refs[0], refs[1:]
    if last:
        stat_ref, refs = refs[0], refs[1:]
    heads, sems = refs[:2]
    step = pl.program_id(0)
    depth = sum(parts) // count
    if not last:
        blocks, block_sems = refs[2:]
        steps = pl.num_programs(0)

        def columns_of(at, act):
            slot = lax.rem(at, 2)
            for n, (piece, share) in enumerate(zip(weights, parts)):
                rows = slice(sum(parts[:n]), sum(parts[: n + 1]))
                source = piece.at[:, pl.ds(pl.multiple_of(at * TILE, TILE), TILE)]
                act(pltpu.make_async_copy(source, blocks.at[slot, rows], block_sems.at[slot, n]))

        @pl.when(step == 0)
        def _():
            columns_of(step, lambda copy: copy.start())

        @pl.when(step + 1 < steps)
        def _():
            columns_of(step + 1, lambda copy: copy.start())

    slots = sources[0].shape[0]

    @pl.when(step == 0)
    def _():
        for n, (kind, k) in enumerate(kinds):
            slot = slot_of(kind, k, where_ref, slots * len(sources) // 2)
            place = heads.at[:, n * depth : (n + 1) * depth]
            for i, source in enumerate(sources):

                @pl.when((slot >= i * slots) & (slot < (i + 1) * slots))
                def _():
                    pltpu.make_async_copy(source.at[slot - i * slots], place, sems.at[n]).start()

        for n in range(count):
            place = heads.at[:, n * depth : (n + 1) * depth]
            pltpu.make_async_copy(sources[0].at[0], place, sems.at[n]).wait()

    if last:
        weight = jnp.concatenate([w[...] for w in weights], 0)
    else:
        columns_of(step, lambda copy: copy.wait())
        weight = blocks[lax.rem(step, 2)]
    total = jnp.dot(heads[...], weight, preferred_element_type=jnp.float32)
    if not first:
        total += partial_ref[...]
    hidden_ref[...] = total
    if last:
        in_high = in_ref[...].astype(jnp.bfloat16)
        in_low = (in_ref[...] - in_high.astype(jnp.float32)).astype(jnp.bfloat16)
        in_parts = jnp.concatenate([in_high, in_low], 0)

        def coded(field):
            code = lax.dot_general(field.astype(jnp.bfloat16), in_parts, NT, preferred_element_type=jnp.float32)
            return code + pltpu.roll(code, RANK, 1)

        code = coded(total * gain_ref[...])
        square = jnp.sum(total * total, axis=1, keepdims=True)
        lane = lax.broadcasted_iota(jnp.int32, code.shape, 1)
        stat = jnp.where(lane < RANK, code, square)
        tok = stat.shape[0]
        mean = jnp.broadcast_to(mean_ref[...], (8, mean_ref.shape[1]))
        mean_high = mean.astype(jnp.bfloat16).astype(jnp.float32)
        mean_code = coded(mean_high) + coded(mean - mean_high)

        @pl.when(step == 0)
        def _():
            stat_ref[:tok, :] = stat
            stat_ref[tok:, :] = mean_code

        @pl.when(step > 0)
        def _():
            stat_ref[:tok, :] += stat
            stat_ref[tok:, :] += mean_code


def project(where, kinds, sources, weights, partial=None, last_terms=None):
    tok = sources[0].shape[1]
    width = weights[0].shape[1]
    parts = [w.shape[0] for w in weights]
    count, total = len(kinds), sum(parts)
    first, last = partial is None, last_terms is not None
    columns = lambda rows: pl.BlockSpec((rows, TILE), lambda j, r: (0, j))
    in_hbm = pl.BlockSpec(memory_space=pltpu.HBM)
    in_specs = [in_hbm] * len(sources) + [columns(rows) if last else in_hbm for rows in parts]
    scratch = [pltpu.VMEM((tok, total), jnp.bfloat16), pltpu.SemaphoreType.DMA((count,))]
    if not last:
        scratch += [pltpu.VMEM((2, total, TILE), jnp.bfloat16), pltpu.SemaphoreType.DMA((2, len(parts)))]
    operands = [where, *sources, *weights]
    out_specs = [columns(tok)]
    out_shape = [jax.ShapeDtypeStruct((tok, width), jnp.float32)]
    if not first:
        in_specs.append(columns(tok))
        operands.append(partial)
    if last:
        gain, erase_in, mean = last_terms
        in_specs += [columns(1), columns(RANK), columns(1)]
        operands += [gain, erase_in, mean]
        out_specs.append(pl.BlockSpec((tok + 8, 2 * RANK), lambda j, r: (0, 0)))
        out_shape.append(jax.ShapeDtypeStruct((tok + 8, 2 * RANK), jnp.float32))
    return pl.pallas_call(
        functools.partial(project_kernel, kinds, len(sources), parts, first, last),
        grid_spec=pltpu.PrefetchScalarGridSpec(
            num_scalar_prefetch=1,
            grid=(width // TILE,),
            in_specs=in_specs,
            out_specs=out_specs,
            scratch_shapes=scratch,
        ),
        out_shape=out_shape,
        compiler_params=pltpu.CompilerParams(vmem_limit_bytes=VMEM_LIMIT),
        cost_estimate=pl.CostEstimate(
            flops=4 * tok * total * width, bytes_accessed=2 * total * width, transcendentals=0
        ),
    )(*operands)


def finish_kernel(model_width, own_ref, other_ref, gain_ref, out_ref, hidden_ref, erased_ref, packed_ref, inv_ref):
    tok = hidden_ref.shape[0]

    @pl.when(pl.program_id(0) == 0)
    def _():
        stat = own_ref[:tok, :] + other_ref[:tok, :]
        mean_code = own_ref[tok : tok + 1, :] + other_ref[tok : tok + 1, :]
        inv_rms = lax.rsqrt(stat[:, RANK : RANK + 1] / model_width + norm_eps)
        lane = lax.broadcasted_iota(jnp.int32, stat.shape, 1)
        code = jnp.where(lane < RANK, stat * inv_rms - mean_code, 0.0)
        high = code.astype(jnp.bfloat16).astype(jnp.float32)
        low = code - high
        packed_ref[...] = jnp.concatenate([high + pltpu.roll(low, RANK, 1), high], 1).astype(jnp.bfloat16)
        inv_ref[...] = jnp.broadcast_to(inv_rms, inv_ref.shape)

    out_high = out_ref[...].astype(jnp.bfloat16)
    out_low = (out_ref[...] - out_high.astype(jnp.float32)).astype(jnp.bfloat16)
    out_parts = jnp.concatenate([out_high, out_high, out_low, jnp.zeros_like(out_low)], 0)
    removed = jnp.dot(packed_ref[...], out_parts, preferred_element_type=jnp.float32)
    normed = hidden_ref[...] * inv_ref[:, :1] * gain_ref[...]
    erased_ref[...] = (normed - removed).astype(jnp.bfloat16)


def finish(model_width, stat, stat_other, gain, erase_out, hidden):
    tok, width = hidden.shape
    whole = pl.BlockSpec(stat.shape, lambda j: (0, 0))
    return pl.pallas_call(
        functools.partial(finish_kernel, model_width),
        grid=(width // TILE,),
        in_specs=[
            whole,
            whole,
            pl.BlockSpec((1, TILE), lambda j: (0, j)),
            pl.BlockSpec((RANK, TILE), lambda j: (0, j)),
            pl.BlockSpec((tok, TILE), lambda j: (0, j)),
        ],
        out_specs=pl.BlockSpec((tok, TILE), lambda j: (0, j)),
        out_shape=jax.ShapeDtypeStruct((tok, width), jnp.bfloat16),
        scratch_shapes=[pltpu.VMEM((tok, 4 * RANK), jnp.bfloat16), pltpu.VMEM((tok, 2 * RANK), jnp.float32)],
        compiler_params=pltpu.CompilerParams(vmem_limit_bytes=VMEM_LIMIT),
        cost_estimate=pl.CostEstimate(
            flops=2 * tok * 256 * width, bytes_accessed=6 * tok * width, transcendentals=0
        ),
    )(stat, stat_other, gain, erase_out, hidden)


def swapped(block, axis):
    return lax.ppermute(block, axis, [(0, 1), (1, 0)])


def ring_order(size):
    return list(range(0, 1)) + list(range(1, size, 2)) + [i for i in range(size - 1, 0, -1) if i % 2 == 0]


def on_device(queries, keys, values, out_proj, post_gain, mean_vec, erase_in, erase_out):
    tok = queries.shape[0]
    outer, inner = lax.axis_size("far"), lax.axis_size("near")
    grp, far, near, col = (lax.axis_index(a) for a in ("grp", "far", "near", "col"))
    row = far * inner + near
    depth, model_width = out_proj.shape
    width = model_width // 2
    kv_local = keys.shape[1] // HD
    heads = queries.shape[1] // HD
    direct = depth == HD and outer * inner == heads and outer == 4

    ahead = [(i, i + 1) for i in range(outer - 1)]
    from_behind = lambda block: lax.ppermute(block, "far", ahead)
    hold = lax.optimization_barrier

    def for_next(own, second):
        return swapped(jnp.where(near == 0, own, second), "near")

    def after(block, *earlier):
        return hold((block, earlier))[0]

    theirs = swapped(lax.dynamic_slice_in_dim(out_proj, (1 - col) * width, width, 1), "col")
    mine = lax.dynamic_slice_in_dim(out_proj, col * width, width, 1)
    gain, mean = post_gain[None, :], mean_vec[None, :]
    erase_in, erase_out = erase_in.T, erase_out.T
    is_mine = grp == col
    where = jnp.stack([is_mine.astype(jnp.int32), far, near, jnp.int32(outer)])

    if direct:
        order = ring_order(outer)
        hops = [(order[i], order[(i + 1) % outer]) for i in range(outer)]
        ring = lambda block: lax.ppermute(block, "far", hops)
        beyond = lambda block: swapped(block, "near")
        facing = lambda block: swapped(block, "grp")
        main, beside, across, corner = ({} for _ in range(4))
        main[0] = jnp.where(is_mine, mine, theirs)
        across[0] = jnp.where(is_mine, theirs, mine)
        beside[0] = beyond(main[0])
        second_keys = from_behind(after(keys, main[0]))
        second_values = from_behind(after(values, second_keys))
        main[1] = ring(after(main[0], second_keys))
        first_keys = for_next(keys, after(second_keys, beside[0]))
        corner[0] = facing(beside[0])
        cos, sin = rope_tables((after(row, beside[0], second_keys) - 2) * tok, 3 * tok)
        first_values = for_next(values, after(second_values, first_keys))
        main[2] = ring(after(main[1], cos, sin))
        across[1] = facing(after(main[1], corner[0]))
        beside[1] = beyond(after(main[1], second_values))
        key_blocks, val_blocks = (second_keys, first_keys, keys), (second_values, first_values, values)
        some = kv_local // 2
        early = attend(row[None], queries, key_blocks, val_blocks, cos, sin, True, 0, some)
        main[3] = ring(after(main[2], early))
        across[2] = facing(after(main[2], across[1], early))
        beside[2] = beyond(after(main[2], beside[1], early))
        corner[1] = facing(after(beside[1], early))
        rest = attend(after(row, beside[1])[None], queries, key_blocks, val_blocks, cos, sin, True, some, kv_local - some)
        attended = [early, rest]
        att_other = [swapped(after(early, rest), "col"), swapped(rest, "col")]
        across[3] = ring(after(across[2], main[3]))
        beside[3] = beyond(after(main[3], beside[2], rest))
        corner[2] = facing(after(beside[2], corner[1]))
        weights, kinds, late, late_kinds = [], [], [], []
        last_ones = (("beside", 3), ("across", 3), ("corner", 2))
        for name, pieces in (("main", main), ("beside", beside), ("across", across), ("corner", corner)):
            for k in range(outer):
                if (name, k) == ("corner", 3):
                    continue
                is_late = (name, k) in last_ones
                (late if is_late else weights).append(pieces[k])
                (late_kinds if is_late else kinds).append((name, k))
        (partial,) = project(where, kinds, attended + att_other, weights)
        half = depth // 2
        late.append(facing(after(beside[3][:half], corner[2], partial)))
        late.append(beyond(after(across[3][half:], beside[3], partial)))
        late_kinds.append(("corner", 3))
    else:
        second_keys, second_values = from_behind(keys), from_behind(values)
        first_keys, first_values = for_next(keys, second_keys), for_next(values, second_values)
        cos, sin = rope_tables((row - 2) * tok, 3 * tok)
        attended = attend(
            row[None], queries, (second_keys, first_keys, keys), (second_values, first_values, values), cos, sin, False
        )
        attended = [attended[None]]
        att_other = [swapped(attended[0], "col")]
        weights, late = ([lax.all_gather(w, ("far", "near"), axis=0, tiled=True)] for w in (mine, theirs))
        kinds, late_kinds = [(None, 0)], [(None, 1)]
        (partial,) = project(where, kinds, attended + att_other, weights)

    hidden, stat = project(where, late_kinds, attended + att_other, late, partial, (gain, erase_in, mean))
    return finish(model_width, stat, swapped(stat, "col"), gain, erase_out, hidden)


def solution(mesh):
    grp, row, col = (mesh.shape[a] for a in ("grp", "row", "col"))
    fine = Mesh(mesh.devices.reshape(grp, row // 2, 2, col), ("grp", "far", "near", "col"))
    tokens = P(("grp", "far", "near"), "col")
    placed = (tokens, tokens, tokens, P(("col", "far", "near"), None), P("col"), P("col"), P("col", None), P("col", None))
    return jax.shard_map(on_device, mesh=fine, in_specs=placed, out_specs=tokens, check_vma=False)
```

```python
import functools

import jax
import jax.numpy as jnp
from jax import lax
from jax.experimental import pallas as pl
from jax.experimental.pallas import tpu as pltpu
from jax.sharding import Mesh
from jax.sharding import PartitionSpec as P

HD = 128
WINDOW = 1024
RANK = 64

query_scale = 168.0 ** (-0.5)
norm_eps = 1e-06
rope_base = 10000.0
log2_e = 1.4426950408889634

TILE = 896
VMEM_LIMIT = 20 * 2**20

NT = (((1,), (1,)), ((), ()))


def rope_tables(first_position, count):
    half_dim = HD // 2
    inverse = jnp.exp(
        -(2.0 * jnp.arange(half_dim, dtype=jnp.float32) / HD) * jnp.log(jnp.float32(rope_base))
    )
    positions = (first_position + jnp.arange(count, dtype=jnp.int32)).astype(jnp.float32)
    angles = positions[:, None] * inverse[None, :]
    cosine, sine = jnp.cos(angles), jnp.sin(angles)
    return jnp.concatenate([cosine, cosine], 1), jnp.concatenate([-sine, sine], 1)


def attend_kernel(tok, group, direct, row_ref, q_ref, k0, k1, k2, v0, v1, v2, cos_ref, sin_ref, out_ref):
    tile = 256

    def turned(field, at):
        wide = field.astype(jnp.float32)
        cos, sin = cos_ref[at : at + tok, :], sin_ref[at : at + tok, :]
        return (wide * cos + pltpu.roll(wide, HD // 2, 1) * sin).astype(jnp.bfloat16)

    row = row_ref[0]
    bias0 = jnp.where(row >= 2, 0.0, -1e30).astype(jnp.float32)
    bias1 = jnp.where(row >= 1, 0.0, -1e30).astype(jnp.float32)
    key0, key1, key2 = turned(k0[...], 0), turned(k1[...], tok), turned(k2[...], 2 * tok)
    heads = [turned(q_ref[:, h * HD : (h + 1) * HD], 2 * tok) for h in range(group)]
    scale = query_scale * log2_e
    stacked = group * tile
    inner = lax.rem(lax.broadcasted_iota(jnp.int32, (stacked, tile), 0), tile)
    newer = lax.broadcasted_iota(jnp.int32, (stacked, tile), 1) > inner

    def dot_nt(a, b):
        return lax.dot_general(a, b, NT, preferred_element_type=jnp.float32)

    def dot(a, b):
        return jnp.dot(a, b, preferred_element_type=jnp.float32)

    for t in range(tok // tile):
        lo, hi = t * tile, (t + 1) * tile
        query = jnp.concatenate([h[lo:hi] for h in heads], 0)
        parts = [(dot_nt(query, key1) + bias1, v1[...])]
        if hi < tok:
            parts.append((dot_nt(query, key0[hi:]) + bias0, v0[hi:, :]))
        if lo > 0:
            parts.append((dot_nt(query, key2[:lo]), v2[:lo, :]))
        mixed = jnp.where(newer, dot_nt(query, key0[lo:hi]) + bias0, dot_nt(query, key2[lo:hi]))
        top = jnp.max(mixed, axis=1, keepdims=True)
        for part, _ in parts:
            top = jnp.maximum(top, jnp.max(part, axis=1, keepdims=True))
        top = top * scale
        weights = jnp.exp2(mixed * scale - top)
        total = jnp.sum(weights, axis=1, keepdims=True)
        older = jnp.where(newer, weights, 0.0)
        result = dot(older.astype(jnp.bfloat16), v0[lo:hi, :])
        result += dot((weights - older).astype(jnp.bfloat16), v2[lo:hi, :])
        for part, value in parts:
            weights = jnp.exp2(part * scale - top)
            total += jnp.sum(weights, axis=1, keepdims=True)
            result += dot(weights.astype(jnp.bfloat16), value)
        result = (result / total).astype(jnp.bfloat16)
        for h in range(group):
            block = result[h * tile : (h + 1) * tile]
            if direct:
                out_ref[h, lo:hi, :] = block
            else:
                out_ref[lo:hi, h * HD : (h + 1) * HD] = block


def attend(row, queries, key_blocks, val_blocks, cos, sin, direct, first=0, count=None):
    tok, kv_local = queries.shape[0], key_blocks[0].shape[1] // HD
    group = queries.shape[1] // HD // kv_local
    count = kv_local if count is None else count
    head_block = pl.BlockSpec((tok, HD), lambda g, r: (0, g + first))
    table = pl.BlockSpec((3 * tok, HD), lambda g, r: (0, 0))
    if direct:
        out_shape = (count * group, tok, HD)
        out_spec = pl.BlockSpec((group, tok, HD), lambda g, r: (g, 0, 0))
    else:
        out_shape = queries.shape
        out_spec = pl.BlockSpec((tok, group * HD), lambda g, r: (0, g))
    heads = count * group
    return pl.pallas_call(
        functools.partial(attend_kernel, tok, group, direct),
        grid_spec=pltpu.PrefetchScalarGridSpec(
            num_scalar_prefetch=1,
            grid=(count,),
            in_specs=[pl.BlockSpec((tok, group * HD), lambda g, r: (0, g + first))] + [head_block] * 6 + [table] * 2,
            out_specs=out_spec,
        ),
        out_shape=jax.ShapeDtypeStruct(out_shape, jnp.bfloat16),
        compiler_params=pltpu.CompilerParams(vmem_limit_bytes=VMEM_LIMIT),
        cost_estimate=pl.CostEstimate(
            flops=4 * heads * tok * 10 * tok * HD, bytes_accessed=6 * 2**20, transcendentals=heads * tok * 2 * tok
        ),
    )(row, queries, *key_blocks, *val_blocks, cos, sin)


def ring_place(position, size):
    return jnp.where(position <= size // 2, jnp.maximum(2 * position - 1, 0), 2 * (size - position))


def ring_position(place, size):
    return jnp.where(place % 2 == 1, (place + 1) // 2, (size - place // 2) % size)


def slot_of(kind, step, where_ref, slots):
    if kind is None:
        return step * slots
    is_mine, far, near, outer = where_ref[0], where_ref[1], where_ref[2], where_ref[3]
    from_far = ring_place((ring_position(far, outer) - step + outer) % outer, outer)
    side = near if kind in ("main", "across") else 1 - near
    other = 1 - is_mine if kind in ("main", "beside") else is_mine
    return other * slots + from_far * 2 + side


def project_kernel(kinds, sources, parts, first, last, where_ref, *refs):
    count = len(kinds)
    sources, refs = refs[:sources], refs[sources:]
    weights, refs = refs[: len(parts)], refs[len(parts) :]
    if not first:
        partial_ref, refs = refs[0], refs[1:]
    if last:
        gain_ref, in_ref, mean_ref, refs = *refs[:3], refs[3:]
    hidden_ref, refs = refs[0], refs[1:]
    if last:
        stat_ref, refs = refs[0], refs[1:]
    heads, sems = refs[:2]
    step = pl.program_id(0)
    depth = sum(parts) // count
    if not last:
        blocks, block_sems = refs[2:]
        steps = pl.num_programs(0)

        def columns_of(at, act):
            slot = lax.rem(at, 2)
            for n, (piece, share) in enumerate(zip(weights, parts)):
                rows = slice(sum(parts[:n]), sum(parts[: n + 1]))
                source = piece.at[:, pl.ds(pl.multiple_of(at * TILE, TILE), TILE)]
                act(pltpu.make_async_copy(source, blocks.at[slot, rows], block_sems.at[slot, n]))

        @pl.when(step == 0)
        def _():
            columns_of(step, lambda copy: copy.start())

        @pl.when(step + 1 < steps)
        def _():
            columns_of(step + 1, lambda copy: copy.start())

    slots = sources[0].shape[0]

    @pl.when(step == 0)
    def _():
        for n, (kind, k) in enumerate(kinds):
            slot = slot_of(kind, k, where_ref, slots * len(sources) // 2)
            place = heads.at[:, n * depth : (n + 1) * depth]
            for i, source in enumerate(sources):

                @pl.when((slot >= i * slots) & (slot < (i + 1) * slots))
                def _():
                    pltpu.make_async_copy(source.at[slot - i * slots], place, sems.at[n]).start()

        for n in range(count):
            place = heads.at[:, n * depth : (n + 1) * depth]
            pltpu.make_async_copy(sources[0].at[0], place, sems.at[n]).wait()

    if last:
        weight = jnp.concatenate([w[...] for w in weights], 0)
    else:
        columns_of(step, lambda copy: copy.wait())
        weight = blocks[lax.rem(step, 2)]
    total = jnp.dot(heads[...], weight, preferred_element_type=jnp.float32)
    if not first:
        total += partial_ref[...]
    hidden_ref[...] = total
    if last:
        in_high = in_ref[...].astype(jnp.bfloat16)
        in_low = (in_ref[...] - in_high.astype(jnp.float32)).astype(jnp.bfloat16)
        in_parts = jnp.concatenate([in_high, in_low], 0)

        def coded(field):
            code = lax.dot_general(field.astype(jnp.bfloat16), in_parts, NT, preferred_element_type=jnp.float32)
            return code + pltpu.roll(code, RANK, 1)

        code = coded(total * gain_ref[...])
        square = jnp.sum(total * total, axis=1, keepdims=True)
        lane = lax.broadcasted_iota(jnp.int32, code.shape, 1)
        stat = jnp.where(lane < RANK, code, square)
        tok = stat.shape[0]
        mean = jnp.broadcast_to(mean_ref[...], (8, mean_ref.shape[1]))
        mean_high = mean.astype(jnp.bfloat16).astype(jnp.float32)
        mean_code = coded(mean_high) + coded(mean - mean_high)

        @pl.when(step == 0)
        def _():
            stat_ref[:tok, :] = stat
            stat_ref[tok:, :] = mean_code

        @pl.when(step > 0)
        def _():
            stat_ref[:tok, :] += stat
            stat_ref[tok:, :] += mean_code


def project(where, kinds, sources, weights, partial=None, last_terms=None):
    tok = sources[0].shape[1]
    width = weights[0].shape[1]
    parts = [w.shape[0] for w in weights]
    count, total = len(kinds), sum(parts)
    first, last = partial is None, last_terms is not None
    columns = lambda rows: pl.BlockSpec((rows, TILE), lambda j, r: (0, j))
    in_hbm = pl.BlockSpec(memory_space=pltpu.HBM)
    in_specs = [in_hbm] * len(sources) + [columns(rows) if last else in_hbm for rows in parts]
    scratch = [pltpu.VMEM((tok, total), jnp.bfloat16), pltpu.SemaphoreType.DMA((count,))]
    if not last:
        scratch += [pltpu.VMEM((2, total, TILE), jnp.bfloat16), pltpu.SemaphoreType.DMA((2, len(parts)))]
    operands = [where, *sources, *weights]
    out_specs = [columns(tok)]
    out_shape = [jax.ShapeDtypeStruct((tok, width), jnp.float32)]
    if not first:
        in_specs.append(columns(tok))
        operands.append(partial)
    if last:
        gain, erase_in, mean = last_terms
        in_specs += [columns(1), columns(RANK), columns(1)]
        operands += [gain, erase_in, mean]
        out_specs.append(pl.BlockSpec((tok + 8, 2 * RANK), lambda j, r: (0, 0)))
        out_shape.append(jax.ShapeDtypeStruct((tok + 8, 2 * RANK), jnp.float32))
    return pl.pallas_call(
        functools.partial(project_kernel, kinds, len(sources), parts, first, last),
        grid_spec=pltpu.PrefetchScalarGridSpec(
            num_scalar_prefetch=1,
            grid=(width // TILE,),
            in_specs=in_specs,
            out_specs=out_specs,
            scratch_shapes=scratch,
        ),
        out_shape=out_shape,
        compiler_params=pltpu.CompilerParams(vmem_limit_bytes=VMEM_LIMIT),
        cost_estimate=pl.CostEstimate(
            flops=4 * tok * total * width, bytes_accessed=2 * total * width, transcendentals=0
        ),
    )(*operands)


def finish_kernel(model_width, own_ref, other_ref, gain_ref, out_ref, hidden_ref, erased_ref, packed_ref, inv_ref):
    tok = hidden_ref.shape[0]

    @pl.when(pl.program_id(0) == 0)
    def _():
        stat = own_ref[:tok, :] + other_ref[:tok, :]
        mean_code = own_ref[tok : tok + 1, :] + other_ref[tok : tok + 1, :]
        inv_rms = lax.rsqrt(stat[:, RANK : RANK + 1] / model_width + norm_eps)
        lane = lax.broadcasted_iota(jnp.int32, stat.shape, 1)
        code = jnp.where(lane < RANK, stat * inv_rms - mean_code, 0.0)
        high = code.astype(jnp.bfloat16).astype(jnp.float32)
        low = code - high
        packed_ref[...] = jnp.concatenate([high + pltpu.roll(low, RANK, 1), high], 1).astype(jnp.bfloat16)
        inv_ref[...] = jnp.broadcast_to(inv_rms, inv_ref.shape)

    out_high = out_ref[...].astype(jnp.bfloat16)
    out_low = (out_ref[...] - out_high.astype(jnp.float32)).astype(jnp.bfloat16)
    out_parts = jnp.concatenate([out_high, out_high, out_low, jnp.zeros_like(out_low)], 0)
    removed = jnp.dot(packed_ref[...], out_parts, preferred_element_type=jnp.float32)
    normed = hidden_ref[...] * inv_ref[:, :1] * gain_ref[...]
    erased_ref[...] = (normed - removed).astype(jnp.bfloat16)


def finish(model_width, stat, stat_other, gain, erase_out, hidden):
    tok, width = hidden.shape
    whole = pl.BlockSpec(stat.shape, lambda j: (0, 0))
    return pl.pallas_call(
        functools.partial(finish_kernel, model_width),
        grid=(width // TILE,),
        in_specs=[
            whole,
            whole,
            pl.BlockSpec((1, TILE), lambda j: (0, j)),
            pl.BlockSpec((RANK, TILE), lambda j: (0, j)),
            pl.BlockSpec((tok, TILE), lambda j: (0, j)),
        ],
        out_specs=pl.BlockSpec((tok, TILE), lambda j: (0, j)),
        out_shape=jax.ShapeDtypeStruct((tok, width), jnp.bfloat16),
        scratch_shapes=[pltpu.VMEM((tok, 4 * RANK), jnp.bfloat16), pltpu.VMEM((tok, 2 * RANK), jnp.float32)],
        compiler_params=pltpu.CompilerParams(vmem_limit_bytes=VMEM_LIMIT),
        cost_estimate=pl.CostEstimate(
            flops=2 * tok * 256 * width, bytes_accessed=6 * tok * width, transcendentals=0
        ),
    )(stat, stat_other, gain, erase_out, hidden)


def swapped(block, axis):
    return lax.ppermute(block, axis, [(0, 1), (1, 0)])


def ring_order(size):
    return list(range(0, 1)) + list(range(1, size, 2)) + [i for i in range(size - 1, 0, -1) if i % 2 == 0]


def on_device(queries, keys, values, out_proj, post_gain, mean_vec, erase_in, erase_out):
    tok = queries.shape[0]
    outer, inner = lax.axis_size("far"), lax.axis_size("near")
    grp, far, near, col = (lax.axis_index(a) for a in ("grp", "far", "near", "col"))
    row = far * inner + near
    depth, model_width = out_proj.shape
    width = model_width // 2
    kv_local = keys.shape[1] // HD
    heads = queries.shape[1] // HD
    direct = depth == HD and outer * inner == heads and outer == 4

    ahead = [(i, i + 1) for i in range(outer - 1)]
    from_behind = lambda block: lax.ppermute(block, "far", ahead)
    hold = lax.optimization_barrier

    def for_next(own, second):
        return swapped(jnp.where(near == 0, own, second), "near")

    def after(block, *earlier):
        return hold((block, earlier))[0]

    theirs = swapped(lax.dynamic_slice_in_dim(out_proj, (1 - col) * width, width, 1), "col")
    mine = lax.dynamic_slice_in_dim(out_proj, col * width, width, 1)
    gain, mean = post_gain[None, :], mean_vec[None, :]
    erase_in, erase_out = erase_in.T, erase_out.T
    is_mine = grp == col
    where = jnp.stack([is_mine.astype(jnp.int32), far, near, jnp.int32(outer)])

    if direct:
        order = ring_order(outer)
        hops = [(order[i], order[(i + 1) % outer]) for i in range(outer)]
        queues = {"far": [], "near": [], "grp": []}

        def send(axis, block, *earlier, route=((0, 1), (1, 0))):
            queue = queues[axis]
            waits = (*earlier, *queue[-2:-1])
            queue.append(lax.ppermute(after(block, *waits) if waits else block, axis, route))
            return queue[-1]

        ring = lambda block, *earlier: send("far", block, *earlier, route=hops)
        beyond = lambda block, *earlier: send("near", block, *earlier)
        facing = lambda block, *earlier: send("grp", block, *earlier)
        main, beside, across, corner = ({} for _ in range(4))
        rows = [slice(0, depth // 2), slice(depth // 2, depth)]
        main[0] = [jnp.where(is_mine, mine[r], theirs[r]) for r in rows]
        across[0] = [jnp.where(is_mine, theirs[r], mine[r]) for r in rows]
        beside[0] = [beyond(half) for half in main[0]]
        second_keys = send("far", keys, main[0], route=ahead)
        second_values = send("far", values, beside[0][0], route=ahead)
        cos, sin = rope_tables((after(row, beside[0], second_keys) - 2) * tok, 3 * tok)
        first_keys = beyond(jnp.where(near == 0, keys, after(second_keys, beside[0])))
        corner[0] = [facing(half) for half in beside[0]]
        main[1] = [ring(main[0][0], beside[0]), ring(main[0][1])]
        first_values = beyond(jnp.where(near == 0, values, second_values))
        beside[1] = [beyond(half) for half in main[1]]
        across[1] = [facing(half) for half in main[1]]
        main[2] = [ring(half) for half in main[1]]
        corner[1] = [facing(half) for half in beside[1]]
        key_blocks, val_blocks = (second_keys, first_keys, keys), (second_values, first_values, values)
        some = kv_local // 2
        early = attend(row[None], queries, key_blocks, val_blocks, cos, sin, True, 0, some)
        main[3] = [ring(main[2][0], early), ring(main[2][1])]
        rest = attend(after(row, main[2][0])[None], queries, key_blocks, val_blocks, cos, sin, True, some, kv_local - some)
        beside[2] = [beyond(main[2][0], early), beyond(main[2][1], rest)]
        corner[2] = [facing(half) for half in beside[2]]
        attended = [early, rest]
        att_other = [swapped(after(early, rest), "col"), swapped(rest, "col")]
        beside[3] = [beyond(half) for half in main[3]]
        across[2] = [ring(half) for half in across[1]]
        across[3] = [ring(half) for half in across[2]]
        corner[3] = [facing(half) for half in beside[3]]
        weights, kinds, late, late_kinds = [], [], [], []
        for name, pieces in (("main", main), ("beside", beside), ("across", across), ("corner", corner)):
            for k in range(outer):
                is_late = k == 3 and name in ("across", "corner")
                (late if is_late else weights).extend(pieces[k])
                (late_kinds if is_late else kinds).append((name, k))
        (partial,) = project(where, kinds, attended + att_other, weights)
    else:
        second_keys, second_values = from_behind(keys), from_behind(values)
        first_keys, first_values = for_next(keys, second_keys), for_next(values, second_values)
        cos, sin = rope_tables((row - 2) * tok, 3 * tok)
        attended = attend(
            row[None], queries, (second_keys, first_keys, keys), (second_values, first_values, values), cos, sin, False
        )
        attended = [attended[None]]
        att_other = [swapped(attended[0], "col")]
        weights, late = ([lax.all_gather(w, ("far", "near"), axis=0, tiled=True)] for w in (mine, theirs))
        kinds, late_kinds = [(None, 0)], [(None, 1)]
        (partial,) = project(where, kinds, attended + att_other, weights)

    hidden, stat = project(where, late_kinds, attended + att_other, late, partial, (gain, erase_in, mean))
    return finish(model_width, stat, swapped(stat, "col"), gain, erase_out, hidden)


def solution(mesh):
    grp, row, col = (mesh.shape[a] for a in ("grp", "row", "col"))
    fine = Mesh(mesh.devices.reshape(grp, row // 2, 2, col), ("grp", "far", "near", "col"))
    tokens = P(("grp", "far", "near"), "col")
    placed = (tokens, tokens, tokens, P(("col", "far", "near"), None), P("col"), P("col"), P("col", None), P("col", None))
    return jax.shard_map(on_device, mesh=fine, in_specs=placed, out_specs=tokens, check_vma=False)
```

```python
import functools

import jax
import jax.numpy as jnp
from jax import lax
from jax.experimental import pallas as pl
from jax.experimental.pallas import tpu as pltpu
from jax.sharding import Mesh
from jax.sharding import PartitionSpec as P

HD = 128
WINDOW = 1024
RANK = 64

query_scale = 168.0 ** (-0.5)
norm_eps = 1e-06
rope_base = 10000.0
log2_e = 1.4426950408889634

TILE = 896
VMEM_LIMIT = 32 * 2**20

NT = (((1,), (1,)), ((), ()))


def rope_tables(first_position, count):
    half_dim = HD // 2
    inverse = jnp.exp(
        -(2.0 * jnp.arange(half_dim, dtype=jnp.float32) / HD) * jnp.log(jnp.float32(rope_base))
    )
    positions = (first_position + jnp.arange(count, dtype=jnp.int32)).astype(jnp.float32)
    angles = positions[:, None] * inverse[None, :]
    cosine, sine = jnp.cos(angles), jnp.sin(angles)
    return jnp.concatenate([cosine, cosine], 1), jnp.concatenate([-sine, sine], 1)


def attend_kernel(tok, group, direct, row_ref, q_ref, k0, k1, k2, v0, v1, v2, cos_ref, sin_ref, out_ref):
    tile = 256

    def turned(field, at):
        wide = field.astype(jnp.float32)
        cos, sin = cos_ref[at : at + tok, :], sin_ref[at : at + tok, :]
        return (wide * cos + pltpu.roll(wide, HD // 2, 1) * sin).astype(jnp.bfloat16)

    row = row_ref[0]
    bias0 = jnp.where(row >= 2, 0.0, -1e30).astype(jnp.float32)
    bias1 = jnp.where(row >= 1, 0.0, -1e30).astype(jnp.float32)
    key0, key1, key2 = turned(k0[...], 0), turned(k1[...], tok), turned(k2[...], 2 * tok)
    heads = [turned(q_ref[:, h * HD : (h + 1) * HD], 2 * tok) for h in range(group)]
    scale = query_scale * log2_e
    stacked = group * tile
    inner = lax.rem(lax.broadcasted_iota(jnp.int32, (stacked, tile), 0), tile)
    newer = lax.broadcasted_iota(jnp.int32, (stacked, tile), 1) > inner

    def dot_nt(a, b):
        return lax.dot_general(a, b, NT, preferred_element_type=jnp.float32)

    def dot(a, b):
        return jnp.dot(a, b, preferred_element_type=jnp.float32)

    for t in range(tok // tile):
        lo, hi = t * tile, (t + 1) * tile
        query = jnp.concatenate([h[lo:hi] for h in heads], 0)
        parts = [(dot_nt(query, key1) + bias1, v1[...])]
        if hi < tok:
            parts.append((dot_nt(query, key0[hi:]) + bias0, v0[hi:, :]))
        if lo > 0:
            parts.append((dot_nt(query, key2[:lo]), v2[:lo, :]))
        mixed = jnp.where(newer, dot_nt(query, key0[lo:hi]) + bias0, dot_nt(query, key2[lo:hi]))
        top = jnp.max(mixed, axis=1, keepdims=True)
        for part, _ in parts:
            top = jnp.maximum(top, jnp.max(part, axis=1, keepdims=True))
        top = top * scale
        weights = jnp.exp2(mixed * scale - top)
        total = jnp.sum(weights, axis=1, keepdims=True)
        older = jnp.where(newer, weights, 0.0)
        result = dot(older.astype(jnp.bfloat16), v0[lo:hi, :])
        result += dot((weights - older).astype(jnp.bfloat16), v2[lo:hi, :])
        for part, value in parts:
            weights = jnp.exp2(part * scale - top)
            total += jnp.sum(weights, axis=1, keepdims=True)
            result += dot(weights.astype(jnp.bfloat16), value)
        result = (result / total).astype(jnp.bfloat16)
        for h in range(group):
            block = result[h * tile : (h + 1) * tile]
            if direct:
                out_ref[h, lo:hi, :] = block
            else:
                out_ref[lo:hi, h * HD : (h + 1) * HD] = block


def attend(row, queries, key_blocks, val_blocks, cos, sin, direct, first=0, count=None):
    tok, kv_local = queries.shape[0], key_blocks[-1].shape[1] // HD
    group = queries.shape[1] // HD // kv_local
    count = kv_local if count is None else count
    head_block = pl.BlockSpec((tok, HD), lambda g, r: (0, g + first))
    table = pl.BlockSpec((3 * tok, HD), lambda g, r: (0, 0))
    if direct:
        out_shape = (count * group, tok, HD)
        out_spec = pl.BlockSpec((group, tok, HD), lambda g, r: (g, 0, 0))
    else:
        out_shape = queries.shape
        out_spec = pl.BlockSpec((tok, group * HD), lambda g, r: (0, g))
    heads = count * group
    return pl.pallas_call(
        functools.partial(attend_kernel, tok, group, direct),
        grid_spec=pltpu.PrefetchScalarGridSpec(
            num_scalar_prefetch=1,
            grid=(count,),
            in_specs=[pl.BlockSpec((tok, group * HD), lambda g, r: (0, g + first))] + [head_block] * 3
            + [
                pl.BlockSpec((tok, HD), lambda g, r, skip=v.shape[1] // HD - kv_local: (0, g + first + skip))
                for v in val_blocks
            ]
            + [table] * 2,
            out_specs=out_spec,
        ),
        out_shape=jax.ShapeDtypeStruct(out_shape, jnp.bfloat16),
        compiler_params=pltpu.CompilerParams(vmem_limit_bytes=VMEM_LIMIT),
        cost_estimate=pl.CostEstimate(
            flops=4 * heads * tok * 10 * tok * HD, bytes_accessed=6 * 2**20, transcendentals=heads * tok * 2 * tok
        ),
    )(row, queries, *key_blocks, *val_blocks, cos, sin)


def ring_place(position, size):
    return jnp.where(position <= size // 2, jnp.maximum(2 * position - 1, 0), 2 * (size - position))


def ring_position(place, size):
    return jnp.where(place % 2 == 1, (place + 1) // 2, (size - place // 2) % size)


def slot_of(kind, step, where_ref, slots):
    if kind is None:
        return step * slots
    is_mine, far, near, outer = where_ref[0], where_ref[1], where_ref[2], where_ref[3]
    from_far = ring_place((ring_position(far, outer) - step + outer) % outer, outer)
    side = near if kind in ("main", "across") else 1 - near
    other = 1 - is_mine if kind in ("main", "beside") else is_mine
    return other * slots + from_far * 2 + side


def gather_heads(kinds, where_ref, sources, heads, sems):
    slots = sources[0].shape[0]
    depth = sources[0].shape[2]
    places = [heads.at[:, n * depth : (n + 1) * depth] for n in range(len(kinds))]
    for n, (kind, k) in enumerate(kinds):
        slot = slot_of(kind, k, where_ref, slots * len(sources) // 2)
        for i, source in enumerate(sources):

            @pl.when((slot >= i * slots) & (slot < (i + 1) * slots))
            def _():
                pltpu.make_async_copy(source.at[slot - i * slots], places[n], sems.at[n]).start()

    for n, place in enumerate(places):
        pltpu.make_async_copy(sources[0].at[0], place, sems.at[n]).wait()


def project_kernel(kinds, sources, where_ref, *refs):
    sources, refs = refs[:sources], refs[sources:]
    weights, (partial_ref, heads, sems, blocks, block_sems) = refs[:-5], refs[-5:]
    step = pl.program_id(0)
    steps = pl.num_programs(0)
    depth = weights[0].shape[0]

    def columns_of(at, act):
        slot = lax.rem(at, 2)
        for n, piece in enumerate(weights):
            source = piece.at[:, pl.ds(pl.multiple_of(at * TILE, TILE), TILE)]
            act(pltpu.make_async_copy(source, blocks.at[slot, n * depth : (n + 1) * depth], block_sems.at[slot, n]))

    @pl.when(step == 0)
    def _():
        columns_of(step, lambda copy: copy.start())

    @pl.when(step + 1 < steps)
    def _():
        columns_of(step + 1, lambda copy: copy.start())

    @pl.when(step == 0)
    def _():
        gather_heads(kinds, where_ref, sources, heads, sems)

    columns_of(step, lambda copy: copy.wait())
    partial_ref[...] = jnp.dot(heads[...], blocks[lax.rem(step, 2)], preferred_element_type=jnp.float32)


def project(where, kinds, sources, weights):
    tok = sources[0].shape[1]
    depth, width = weights[0].shape
    count = len(kinds)
    in_hbm = pl.BlockSpec(memory_space=pltpu.HBM)
    return pl.pallas_call(
        functools.partial(project_kernel, kinds, len(sources)),
        grid_spec=pltpu.PrefetchScalarGridSpec(
            num_scalar_prefetch=1,
            grid=(width // TILE,),
            in_specs=[in_hbm] * (len(sources) + count),
            out_specs=pl.BlockSpec((tok, TILE), lambda j, r: (0, j)),
            scratch_shapes=[
                pltpu.VMEM((tok, count * depth), jnp.bfloat16),
                pltpu.SemaphoreType.DMA((count,)),
                pltpu.VMEM((2, count * depth, TILE), jnp.bfloat16),
                pltpu.SemaphoreType.DMA((2, count)),
            ],
        ),
        out_shape=jax.ShapeDtypeStruct((tok, width), jnp.float32),
        compiler_params=pltpu.CompilerParams(vmem_limit_bytes=VMEM_LIMIT),
        cost_estimate=pl.CostEstimate(
            flops=2 * tok * count * depth * width, bytes_accessed=2 * count * depth * width, transcendentals=0
        ),
    )(where, *sources, *weights)


def close_kernel(kinds, sources, where_ref, *refs):
    sources, refs = refs[:sources], refs[sources:]
    weights, (partial_ref, gain_ref, in_ref, mean_ref, hidden_ref, stat_ref, heads, sems) = refs[:-8], refs[-8:]
    gather_heads(kinds, where_ref, sources, heads, sems)
    tok, width = hidden_ref.shape
    code = square = mean_code = 0.0
    for at in range(0, width, TILE):
        here = slice(at, at + TILE)
        weight = jnp.concatenate([w[:, here] for w in weights], 0)
        total = partial_ref[:, here] + jnp.dot(heads[...], weight, preferred_element_type=jnp.float32)
        hidden_ref[:, here] = total
        in_high = in_ref[:, here].astype(jnp.bfloat16)
        in_low = (in_ref[:, here] - in_high.astype(jnp.float32)).astype(jnp.bfloat16)
        in_parts = jnp.concatenate([in_high, in_low], 0)

        def coded(field):
            return lax.dot_general(field.astype(jnp.bfloat16), in_parts, NT, preferred_element_type=jnp.float32)

        code += coded(total * gain_ref[:, here])
        square += jnp.sum(total * total, axis=1, keepdims=True)
        mean = jnp.broadcast_to(mean_ref[:, here], (8, TILE))
        mean_high = mean.astype(jnp.bfloat16).astype(jnp.float32)
        mean_code += coded(mean_high) + coded(mean - mean_high)
    lane = lax.broadcasted_iota(jnp.int32, code.shape, 1)
    stat_ref[:tok, :] = jnp.where(lane < RANK, code + pltpu.roll(code, RANK, 1), square)
    stat_ref[tok:, :] = mean_code + pltpu.roll(mean_code, RANK, 1)


def close(where, kinds, sources, weights, partial, gain, erase_in, mean):
    tok, width = partial.shape
    depth = weights[0].shape[0]
    count = len(kinds)
    in_vmem = pl.BlockSpec(memory_space=pltpu.VMEM)
    in_hbm = pl.BlockSpec(memory_space=pltpu.HBM)
    return pl.pallas_call(
        functools.partial(close_kernel, kinds, len(sources)),
        in_specs=[pl.BlockSpec(memory_space=pltpu.SMEM)] + [in_hbm] * len(sources) + [in_vmem] * (count + 4),
        out_specs=[in_vmem] * 2,
        out_shape=[
            jax.ShapeDtypeStruct((tok, width), jnp.float32),
            jax.ShapeDtypeStruct((tok + 8, 2 * RANK), jnp.float32),
        ],
        scratch_shapes=[pltpu.VMEM((tok, count * depth), jnp.bfloat16), pltpu.SemaphoreType.DMA((count,))],
        input_output_aliases={1 + len(sources) + count: 0},
        compiler_params=pltpu.CompilerParams(vmem_limit_bytes=VMEM_LIMIT),
        cost_estimate=pl.CostEstimate(
            flops=2 * tok * count * depth * width, bytes_accessed=2 * count * depth * width, transcendentals=0
        ),
    )(where, *sources, *weights, partial, gain, erase_in, mean)


def finish_kernel(model_width, own_ref, other_ref, gain_ref, out_ref, hidden_ref, erased_ref, tiles, sems):
    tok, width = hidden_ref.shape
    stat = own_ref[:tok, :] + other_ref[:tok, :]
    mean_code = own_ref[tok : tok + 1, :] + other_ref[tok : tok + 1, :]
    inv_rms = lax.rsqrt(stat[:, RANK : RANK + 1] / model_width + norm_eps)
    lane = lax.broadcasted_iota(jnp.int32, stat.shape, 1)
    code = jnp.where(lane < RANK, stat * inv_rms - mean_code, 0.0)
    high = code.astype(jnp.bfloat16).astype(jnp.float32)
    low = code - high
    packed = jnp.concatenate([high + pltpu.roll(low, RANK, 1), high], 1).astype(jnp.bfloat16)
    copies = []
    for n, at in enumerate(range(0, width, TILE)):
        here = slice(at, at + TILE)
        out_high = out_ref[:, here].astype(jnp.bfloat16)
        out_low = (out_ref[:, here] - out_high.astype(jnp.float32)).astype(jnp.bfloat16)
        out_parts = jnp.concatenate([out_high, out_high, out_low, jnp.zeros_like(out_low)], 0)
        removed = jnp.dot(packed, out_parts, preferred_element_type=jnp.float32)
        normed = hidden_ref[:, here] * inv_rms * gain_ref[:, here]
        tiles[:, here] = (normed - removed).astype(jnp.bfloat16)
        copies.append(pltpu.make_async_copy(tiles.at[:, here], erased_ref.at[:, here], sems.at[n]))
        copies[-1].start()
    for copy in copies:
        copy.wait()


def finish(model_width, stat, stat_other, gain, erase_out, hidden):
    tok, width = hidden.shape
    in_vmem = pl.BlockSpec(memory_space=pltpu.VMEM)
    return pl.pallas_call(
        functools.partial(finish_kernel, model_width),
        in_specs=[in_vmem] * 5,
        out_specs=pl.BlockSpec(memory_space=pltpu.HBM),
        out_shape=jax.ShapeDtypeStruct((tok, width), jnp.bfloat16),
        scratch_shapes=[pltpu.VMEM((tok, width), jnp.bfloat16), pltpu.SemaphoreType.DMA((width // TILE,))],
        compiler_params=pltpu.CompilerParams(vmem_limit_bytes=VMEM_LIMIT),
        cost_estimate=pl.CostEstimate(
            flops=2 * tok * 256 * width, bytes_accessed=6 * tok * width, transcendentals=0
        ),
    )(stat, stat_other, gain, erase_out, hidden)


def swapped(block, axis):
    return lax.ppermute(block, axis, [(0, 1), (1, 0)])


def ring_order(size):
    return list(range(0, 1)) + list(range(1, size, 2)) + [i for i in range(size - 1, 0, -1) if i % 2 == 0]


def on_device(queries, keys, values, out_proj, post_gain, mean_vec, erase_in, erase_out):
    tok = queries.shape[0]
    outer, inner = lax.axis_size("far"), lax.axis_size("near")
    grp, far, near, col = (lax.axis_index(a) for a in ("grp", "far", "near", "col"))
    row = far * inner + near
    depth, model_width = out_proj.shape
    width = model_width // 2
    kv_local = keys.shape[1] // HD
    heads = queries.shape[1] // HD
    direct = depth == HD and outer * inner == heads and outer == 4

    ahead = [(i, i + 1) for i in range(outer - 1)]
    from_behind = lambda block: lax.ppermute(block, "far", ahead)
    hold = lax.optimization_barrier

    def for_next(own, second):
        return swapped(jnp.where(near == 0, own, second), "near")

    def after(block, *earlier):
        return hold((block, earlier))[0]

    theirs = swapped(lax.dynamic_slice_in_dim(out_proj, (1 - col) * width, width, 1), "col")
    mine = lax.dynamic_slice_in_dim(out_proj, col * width, width, 1)
    gain, mean = post_gain[None, :], mean_vec[None, :]
    erase_in, erase_out = erase_in.T, erase_out.T
    is_mine = grp == col
    where = jnp.stack([is_mine.astype(jnp.int32), far, near, jnp.int32(outer)])

    if direct:
        order = ring_order(outer)
        hops = [(order[i], order[(i + 1) % outer]) for i in range(outer)]
        ring = lambda block: lax.ppermute(block, "far", hops)
        beyond = lambda block: swapped(block, "near")
        facing = lambda block: swapped(block, "grp")
        main, beside, across, corner = ({} for _ in range(4))
        main[0] = jnp.where(is_mine, mine, theirs)
        across[0] = jnp.where(is_mine, theirs, mine)
        beside[0] = beyond(main[0])
        second_keys, second_values = from_behind(keys), from_behind(values)
        corner[0] = facing(beside[0])
        cos, sin = rope_tables((after(row, beside[0]) - 2) * tok, 3 * tok)
        main[1] = ring(after(main[0], second_keys, second_values))
        own_both = jnp.concatenate([keys, values], 1)
        old_both = jnp.concatenate(after((second_keys, second_values), beside[0]), 1)
        first_both = for_next(own_both, old_both)
        main[1], corner[0], cos, sin = hold((main[1], corner[0], cos, sin))
        main[2], across[1] = ring(main[1]), facing(main[1])
        beside[1] = beyond(main[1])
        attended = attend(
            row[None], queries, (second_keys, first_both, keys), (second_values, first_both, values), cos, sin, True
        )
        main[2], beside[1], across[1], attended = hold((main[2], beside[1], across[1], attended))
        main[3], beside[2], corner[1] = ring(main[2]), beyond(main[2]), facing(beside[1])
        att_other = swapped(attended, "col")
        main[3], beside[2], corner[1], att_other, across[1] = hold((main[3], beside[2], corner[1], att_other, across[1]))
        across[2], beside[3], corner[2] = ring(across[1]), beyond(main[3]), facing(beside[2])
        across[2], beside[3], corner[2] = hold((across[2], beside[3], corner[2]))
        across[3], corner[3] = ring(across[2]), facing(beside[3])
        attended, att_other = [attended], [att_other]
        weights, kinds, late, late_kinds = [], [], [], []
        for name, pieces in (("main", main), ("beside", beside), ("across", across), ("corner", corner)):
            for k in range(outer):
                is_late = k == 3 and name in ("across", "corner")
                (late if is_late else weights).append(pieces[k])
                (late_kinds if is_late else kinds).append((name, k))
        partial = project(where, kinds, attended + att_other, weights)
    else:
        second_keys, second_values = from_behind(keys), from_behind(values)
        first_keys, first_values = for_next(keys, second_keys), for_next(values, second_values)
        cos, sin = rope_tables((row - 2) * tok, 3 * tok)
        attended = attend(
            row[None], queries, (second_keys, first_keys, keys), (second_values, first_values, values), cos, sin, False
        )
        attended = [attended[None]]
        att_other = [swapped(attended[0], "col")]
        weights, late = ([lax.all_gather(w, ("far", "near"), axis=0, tiled=True)] for w in (mine, theirs))
        kinds, late_kinds = [(None, 0)], [(None, 1)]
        partial = project(where, kinds, attended + att_other, weights)

    hidden, stat = close(where, late_kinds, attended + att_other, late, partial, gain, erase_in, mean)
    return finish(model_width, stat, swapped(stat, "col"), gain, erase_out, hidden)


def solution(mesh):
    grp, row, col = (mesh.shape[a] for a in ("grp", "row", "col"))
    fine = Mesh(mesh.devices.reshape(grp, row // 2, 2, col), ("grp", "far", "near", "col"))
    tokens = P(("grp", "far", "near"), "col")
    placed = (tokens, tokens, tokens, P(("col", "far", "near"), None), P("col"), P("col"), P("col", None), P("col", None))
    return jax.shard_map(on_device, mesh=fine, in_specs=placed, out_specs=tokens, check_vma=False)
```

```python
import functools

import jax
import jax.numpy as jnp
from jax import lax
from jax.experimental import pallas as pl
from jax.experimental.pallas import tpu as pltpu
from jax.sharding import Mesh
from jax.sharding import PartitionSpec as P

HD = 128
WINDOW = 1024
RANK = 64

query_scale = 168.0 ** (-0.5)
norm_eps = 1e-06
rope_base = 10000.0
log2_e = 1.4426950408889634

TILE = 896
VMEM_LIMIT = 32 * 2**20

NT = (((1,), (1,)), ((), ()))


def rope_tables(first_position, count):
    half_dim = HD // 2
    inverse = jnp.exp(
        -(2.0 * jnp.arange(half_dim, dtype=jnp.float32) / HD) * jnp.log(jnp.float32(rope_base))
    )
    positions = (first_position + jnp.arange(count, dtype=jnp.int32)).astype(jnp.float32)
    angles = positions[:, None] * inverse[None, :]
    cosine, sine = jnp.cos(angles), jnp.sin(angles)
    return jnp.concatenate([cosine, cosine], 1), jnp.concatenate([-sine, sine], 1)


def attend_kernel(tok, group, direct, row_ref, q_ref, k0, k1, k2, v0, v1, v2, cos_ref, sin_ref, out_ref):
    tile = 256

    def turned(field, at):
        wide = field.astype(jnp.float32)
        cos, sin = cos_ref[at : at + tok, :], sin_ref[at : at + tok, :]
        return (wide * cos + pltpu.roll(wide, HD // 2, 1) * sin).astype(jnp.bfloat16)

    row = row_ref[0]
    bias0 = jnp.where(row >= 2, 0.0, -1e30).astype(jnp.float32)
    bias1 = jnp.where(row >= 1, 0.0, -1e30).astype(jnp.float32)
    key0, key1, key2 = turned(k0[...], 0), turned(k1[...], tok), turned(k2[...], 2 * tok)
    heads = [turned(q_ref[:, h * HD : (h + 1) * HD], 2 * tok) for h in range(group)]
    scale = query_scale * log2_e
    stacked = group * tile
    inner = lax.rem(lax.broadcasted_iota(jnp.int32, (stacked, tile), 0), tile)
    newer = lax.broadcasted_iota(jnp.int32, (stacked, tile), 1) > inner

    def dot_nt(a, b):
        return lax.dot_general(a, b, NT, preferred_element_type=jnp.float32)

    def dot(a, b):
        return jnp.dot(a, b, preferred_element_type=jnp.float32)

    for t in range(tok // tile):
        lo, hi = t * tile, (t + 1) * tile
        query = jnp.concatenate([h[lo:hi] for h in heads], 0)
        parts = [(dot_nt(query, key1) + bias1, v1[...])]
        if hi < tok:
            parts.append((dot_nt(query, key0[hi:]) + bias0, v0[hi:, :]))
        if lo > 0:
            parts.append((dot_nt(query, key2[:lo]), v2[:lo, :]))
        mixed = jnp.where(newer, dot_nt(query, key0[lo:hi]) + bias0, dot_nt(query, key2[lo:hi]))
        top = jnp.max(mixed, axis=1, keepdims=True)
        for part, _ in parts:
            top = jnp.maximum(top, jnp.max(part, axis=1, keepdims=True))
        top = top * scale
        weights = jnp.exp2(mixed * scale - top)
        total = jnp.sum(weights, axis=1, keepdims=True)
        older = jnp.where(newer, weights, 0.0)
        result = dot(older.astype(jnp.bfloat16), v0[lo:hi, :])
        result += dot((weights - older).astype(jnp.bfloat16), v2[lo:hi, :])
        for part, value in parts:
            weights = jnp.exp2(part * scale - top)
            total += jnp.sum(weights, axis=1, keepdims=True)
            result += dot(weights.astype(jnp.bfloat16), value)
        result = (result / total).astype(jnp.bfloat16)
        for h in range(group):
            block = result[h * tile : (h + 1) * tile]
            if direct:
                out_ref[h, lo:hi, :] = block
            else:
                out_ref[lo:hi, h * HD : (h + 1) * HD] = block


def attend(row, queries, key_blocks, val_blocks, cos, sin, direct, first=0, count=None):
    tok, kv_local = queries.shape[0], key_blocks[-1].shape[1] // HD
    group = queries.shape[1] // HD // kv_local
    count = kv_local if count is None else count
    head_block = pl.BlockSpec((tok, HD), lambda g, r: (0, g + first))
    table = pl.BlockSpec((3 * tok, HD), lambda g, r: (0, 0))
    if direct:
        out_shape = (count * group, tok, HD)
        out_spec = pl.BlockSpec((group, tok, HD), lambda g, r: (g, 0, 0))
    else:
        out_shape = queries.shape
        out_spec = pl.BlockSpec((tok, group * HD), lambda g, r: (0, g))
    heads = count * group
    return pl.pallas_call(
        functools.partial(attend_kernel, tok, group, direct),
        grid_spec=pltpu.PrefetchScalarGridSpec(
            num_scalar_prefetch=1,
            grid=(count,),
            in_specs=[pl.BlockSpec((tok, group * HD), lambda g, r: (0, g + first))] + [head_block] * 3
            + [
                pl.BlockSpec((tok, HD), lambda g, r, skip=v.shape[1] // HD - kv_local: (0, g + first + skip))
                for v in val_blocks
            ]
            + [table] * 2,
            out_specs=out_spec,
        ),
        out_shape=jax.ShapeDtypeStruct(out_shape, jnp.bfloat16),
        compiler_params=pltpu.CompilerParams(vmem_limit_bytes=VMEM_LIMIT),
        cost_estimate=pl.CostEstimate(
            flops=4 * heads * tok * 10 * tok * HD, bytes_accessed=6 * 2**20, transcendentals=heads * tok * 2 * tok
        ),
    )(row, queries, *key_blocks, *val_blocks, cos, sin)


def ring_place(position, size):
    return jnp.where(position <= size // 2, jnp.maximum(2 * position - 1, 0), 2 * (size - position))


def ring_position(place, size):
    return jnp.where(place % 2 == 1, (place + 1) // 2, (size - place // 2) % size)


def slot_of(kind, step, where_ref, slots):
    if kind is None:
        return step * slots
    is_mine, far, near, outer = where_ref[0], where_ref[1], where_ref[2], where_ref[3]
    from_far = ring_place((ring_position(far, outer) - step + outer) % outer, outer)
    side = near if kind in ("main", "across") else 1 - near
    other = 1 - is_mine if kind in ("main", "beside") else is_mine
    return other * slots + from_far * 2 + side


def gather_heads(kinds, where_ref, sources, heads, sems):
    slots = sources[0].shape[0]
    depth = sources[0].shape[2]
    places = [heads.at[:, n * depth : (n + 1) * depth] for n in range(len(kinds))]
    for n, (kind, k) in enumerate(kinds):
        slot = slot_of(kind, k, where_ref, slots * len(sources) // 2)
        for i, source in enumerate(sources):

            @pl.when((slot >= i * slots) & (slot < (i + 1) * slots))
            def _():
                pltpu.make_async_copy(source.at[slot - i * slots], places[n], sems.at[n]).start()

    for n, place in enumerate(places):
        pltpu.make_async_copy(sources[0].at[0], place, sems.at[n]).wait()


def split_in(in_ref):
    high = in_ref[...].astype(jnp.bfloat16)
    low = (in_ref[...] - high.astype(jnp.float32)).astype(jnp.bfloat16)
    return jnp.concatenate([high, low], 0)


def coded(field, in_parts):
    code = lax.dot_general(field.astype(jnp.bfloat16), in_parts, NT, preferred_element_type=jnp.float32)
    return code + pltpu.roll(code, RANK, 1)


def project_kernel(kinds, late_kinds, sources, where_ref, *refs):
    sources, refs = refs[:sources], refs[sources:]
    weights, refs = refs[: len(kinds)], refs[len(kinds) :]
    in_ref, mean_ref, partial_ref, late_ref, code_ref, heads, sems, late_sems, blocks, block_sems = refs
    step = pl.program_id(0)
    steps = pl.num_programs(0)
    depth = weights[0].shape[0]

    def columns_of(at, act):
        slot = lax.rem(at, 2)
        for n, piece in enumerate(weights):
            source = piece.at[:, pl.ds(pl.multiple_of(at * TILE, TILE), TILE)]
            act(pltpu.make_async_copy(source, blocks.at[slot, n * depth : (n + 1) * depth], block_sems.at[slot, n]))

    @pl.when(step == 0)
    def _():
        columns_of(step, lambda copy: copy.start())

    @pl.when(step + 1 < steps)
    def _():
        columns_of(step + 1, lambda copy: copy.start())

    @pl.when(step == 0)
    def _():
        gather_heads(kinds, where_ref, sources, heads, sems)
        gather_heads(late_kinds, where_ref, sources, late_ref, late_sems)

    mean = jnp.broadcast_to(mean_ref[...], (8, mean_ref.shape[1]))
    mean_high = mean.astype(jnp.bfloat16).astype(jnp.float32)
    in_parts = split_in(in_ref)
    code = coded(mean_high, in_parts) + coded(mean - mean_high, in_parts)

    @pl.when(step == 0)
    def _():
        code_ref[...] = code

    @pl.when(step > 0)
    def _():
        code_ref[...] += code

    columns_of(step, lambda copy: copy.wait())
    partial_ref[...] = jnp.dot(heads[...], blocks[lax.rem(step, 2)], preferred_element_type=jnp.float32)


def project(where, kinds, late_kinds, sources, weights, erase_in, mean):
    tok = sources[0].shape[1]
    depth, width = weights[0].shape
    count, late = len(kinds), len(late_kinds)
    in_hbm = pl.BlockSpec(memory_space=pltpu.HBM)
    columns = lambda rows: pl.BlockSpec((rows, TILE), lambda j, r: (0, j))
    whole = lambda *shape: pl.BlockSpec(shape, lambda j, r: (0, 0))
    return pl.pallas_call(
        functools.partial(project_kernel, kinds, late_kinds, len(sources)),
        grid_spec=pltpu.PrefetchScalarGridSpec(
            num_scalar_prefetch=1,
            grid=(width // TILE,),
            in_specs=[in_hbm] * (len(sources) + count) + [columns(RANK), columns(1)],
            out_specs=[columns(tok), whole(tok, late * depth), whole(8, 2 * RANK)],
            scratch_shapes=[
                pltpu.VMEM((tok, count * depth), jnp.bfloat16),
                pltpu.SemaphoreType.DMA((count,)),
                pltpu.SemaphoreType.DMA((late,)),
                pltpu.VMEM((2, count * depth, TILE), jnp.bfloat16),
                pltpu.SemaphoreType.DMA((2, count)),
            ],
        ),
        out_shape=[
            jax.ShapeDtypeStruct((tok, width), jnp.float32),
            jax.ShapeDtypeStruct((tok, late * depth), jnp.bfloat16),
            jax.ShapeDtypeStruct((8, 2 * RANK), jnp.float32),
        ],
        compiler_params=pltpu.CompilerParams(vmem_limit_bytes=VMEM_LIMIT),
        cost_estimate=pl.CostEstimate(
            flops=2 * tok * count * depth * width, bytes_accessed=2 * count * depth * width, transcendentals=0
        ),
    )(where, *sources, *weights, erase_in, mean)


def close_kernel(heads_ref, *refs):
    weights, (partial_ref, mean_code_ref, gain_ref, in_ref, hidden_ref, stat_ref) = refs[:-6], refs[-6:]
    step = pl.program_id(0)
    tok = hidden_ref.shape[0]
    weight = jnp.concatenate([w[...] for w in weights], 0)
    total = partial_ref[...] + jnp.dot(heads_ref[...], weight, preferred_element_type=jnp.float32)
    hidden_ref[...] = total
    code = coded(total * gain_ref[...], split_in(in_ref))
    square = jnp.sum(total * total, axis=1, keepdims=True)
    lane = lax.broadcasted_iota(jnp.int32, code.shape, 1)
    stat = jnp.where(lane < RANK, code, square)

    @pl.when(step == 0)
    def _():
        stat_ref[:tok, :] = stat
        stat_ref[tok:, :] = mean_code_ref[...]

    @pl.when(step > 0)
    def _():
        stat_ref[:tok, :] += stat


def close(heads, weights, partial, mean_code, gain, erase_in):
    tok, width = partial.shape
    depth = weights[0].shape[0]
    count = len(weights)
    columns = lambda rows: pl.BlockSpec((rows, TILE), lambda j: (0, j))
    whole = lambda *shape: pl.BlockSpec(shape, lambda j: (0, 0))
    return pl.pallas_call(
        close_kernel,
        grid=(width // TILE,),
        in_specs=[whole(*heads.shape)]
        + [columns(depth)] * count
        + [columns(tok), whole(*mean_code.shape), columns(1), columns(RANK)],
        out_specs=[columns(tok), whole(tok + 8, 2 * RANK)],
        out_shape=[
            jax.ShapeDtypeStruct((tok, width), jnp.float32),
            jax.ShapeDtypeStruct((tok + 8, 2 * RANK), jnp.float32),
        ],
        compiler_params=pltpu.CompilerParams(vmem_limit_bytes=VMEM_LIMIT),
        cost_estimate=pl.CostEstimate(
            flops=2 * tok * count * depth * width, bytes_accessed=2 * count * depth * width, transcendentals=0
        ),
    )(heads, *weights, partial, mean_code, gain, erase_in)


def finish_kernel(model_width, own_ref, other_ref, gain_ref, out_ref, hidden_ref, erased_ref, tiles, sems):
    tok, width = hidden_ref.shape
    stat = own_ref[:tok, :] + other_ref[:tok, :]
    mean_code = own_ref[tok : tok + 1, :] + other_ref[tok : tok + 1, :]
    inv_rms = lax.rsqrt(stat[:, RANK : RANK + 1] / model_width + norm_eps)
    lane = lax.broadcasted_iota(jnp.int32, stat.shape, 1)
    code = jnp.where(lane < RANK, stat * inv_rms - mean_code, 0.0)
    high = code.astype(jnp.bfloat16).astype(jnp.float32)
    low = code - high
    packed = jnp.concatenate([high + pltpu.roll(low, RANK, 1), high], 1).astype(jnp.bfloat16)
    copies = []
    for n, at in enumerate(range(0, width, TILE)):
        here = slice(at, at + TILE)
        out_high = out_ref[:, here].astype(jnp.bfloat16)
        out_low = (out_ref[:, here] - out_high.astype(jnp.float32)).astype(jnp.bfloat16)
        out_parts = jnp.concatenate([out_high, out_high, out_low, jnp.zeros_like(out_low)], 0)
        removed = jnp.dot(packed, out_parts, preferred_element_type=jnp.float32)
        normed = hidden_ref[:, here] * inv_rms * gain_ref[:, here]
        tiles[:, here] = (normed - removed).astype(jnp.bfloat16)
        copies.append(pltpu.make_async_copy(tiles.at[:, here], erased_ref.at[:, here], sems.at[n]))
        copies[-1].start()
    for copy in copies:
        copy.wait()


def finish(model_width, stat, stat_other, gain, erase_out, hidden):
    tok, width = hidden.shape
    in_vmem = pl.BlockSpec(memory_space=pltpu.VMEM)
    return pl.pallas_call(
        functools.partial(finish_kernel, model_width),
        in_specs=[in_vmem] * 5,
        out_specs=pl.BlockSpec(memory_space=pltpu.HBM),
        out_shape=jax.ShapeDtypeStruct((tok, width), jnp.bfloat16),
        scratch_shapes=[pltpu.VMEM((tok, width), jnp.bfloat16), pltpu.SemaphoreType.DMA((width // TILE,))],
        compiler_params=pltpu.CompilerParams(vmem_limit_bytes=VMEM_LIMIT),
        cost_estimate=pl.CostEstimate(
            flops=2 * tok * 256 * width, bytes_accessed=6 * tok * width, transcendentals=0
        ),
    )(stat, stat_other, gain, erase_out, hidden)


def swapped(block, axis):
    return lax.ppermute(block, axis, [(0, 1), (1, 0)])


def ring_order(size):
    return list(range(0, 1)) + list(range(1, size, 2)) + [i for i in range(size - 1, 0, -1) if i % 2 == 0]


def on_device(queries, keys, values, out_proj, post_gain, mean_vec, erase_in, erase_out):
    tok = queries.shape[0]
    outer, inner = lax.axis_size("far"), lax.axis_size("near")
    grp, far, near, col = (lax.axis_index(a) for a in ("grp", "far", "near", "col"))
    row = far * inner + near
    depth, model_width = out_proj.shape
    width = model_width // 2
    kv_local = keys.shape[1] // HD
    heads = queries.shape[1] // HD
    direct = depth == HD and outer * inner == heads and outer == 4

    ahead = [(i, i + 1) for i in range(outer - 1)]
    from_behind = lambda block: lax.ppermute(block, "far", ahead)
    hold = lax.optimization_barrier

    def for_next(own, second):
        return swapped(jnp.where(near == 0, own, second), "near")

    def after(block, *earlier):
        return hold((block, earlier))[0]

    theirs = swapped(lax.dynamic_slice_in_dim(out_proj, (1 - col) * width, width, 1), "col")
    mine = lax.dynamic_slice_in_dim(out_proj, col * width, width, 1)
    gain, mean = post_gain[None, :], mean_vec[None, :]
    erase_in, erase_out = erase_in.T, erase_out.T
    is_mine = grp == col
    where = jnp.stack([is_mine.astype(jnp.int32), far, near, jnp.int32(outer)])

    if direct:
        order = ring_order(outer)
        hops = [(order[i], order[(i + 1) % outer]) for i in range(outer)]
        ring = lambda block: lax.ppermute(block, "far", hops)
        beyond = lambda block: swapped(block, "near")
        facing = lambda block: swapped(block, "grp")
        main, beside, across, corner = ({} for _ in range(4))
        main[0] = jnp.where(is_mine, mine, theirs)
        across[0] = jnp.where(is_mine, theirs, mine)
        beside[0] = beyond(main[0])
        second_keys = from_behind(after(keys, main[0]))
        second_values = from_behind(after(values, second_keys))
        first_keys = for_next(keys, after(second_keys, beside[0]))
        corner[0] = facing(beside[0])
        main[1] = ring(after(main[0], second_values))
        first_values = for_next(values, after(second_values, first_keys))
        cos, sin = rope_tables((after(row, beside[0]) - 2) * tok, 3 * tok)
        main[1], first_keys, first_values, corner[0], cos, sin, where = hold(
            (main[1], first_keys, first_values, corner[0], cos, sin, where)
        )
        main[2], beside[1], across[1] = ring(main[1]), beyond(main[1]), facing(main[1])
        attended = attend(
            row[None], queries, (second_keys, first_keys, keys), (second_values, first_values, values), cos, sin, True
        )
        main[2], beside[1], across[1], attended = hold((main[2], beside[1], across[1], attended))
        main[3], beside[2], corner[1] = ring(main[2]), beyond(main[2]), facing(beside[1])
        main[3], beside[2], corner[1], across[1], attended = hold((main[3], beside[2], corner[1], across[1], attended))
        across[2], beside[3], corner[2] = ring(across[1]), beyond(main[3]), facing(beside[2])
        across[2], beside[3], corner[2], attended = hold((across[2], beside[3], corner[2], attended))
        across[3], corner[3] = ring(across[2]), facing(beside[3])
        attended, att_other = [attended], [swapped(attended, "col")]
        weights, kinds, late, late_kinds = [], [], [], []
        for name, pieces in (("main", main), ("beside", beside), ("across", across), ("corner", corner)):
            for k in range(outer):
                is_late = k == 3 and name in ("across", "corner")
                (late if is_late else weights).append(pieces[k])
                (late_kinds if is_late else kinds).append((name, k))
    else:
        second_keys, second_values = from_behind(keys), from_behind(values)
        first_keys, first_values = for_next(keys, second_keys), for_next(values, second_values)
        cos, sin = rope_tables((row - 2) * tok, 3 * tok)
        attended = attend(
            row[None], queries, (second_keys, first_keys, keys), (second_values, first_values, values), cos, sin, False
        )
        attended = [attended[None]]
        att_other = [swapped(attended[0], "col")]
        weights, late = ([lax.all_gather(w, ("far", "near"), axis=0, tiled=True)] for w in (mine, theirs))
        kinds, late_kinds = [(None, 0)], [(None, 1)]

    partial, late_heads, mean_code = project(where, kinds, late_kinds, attended + att_other, weights, erase_in, mean)
    hidden, stat = close(late_heads, late, partial, mean_code, gain, erase_in)
    return finish(model_width, stat, swapped(stat, "col"), gain, erase_out, hidden)


def solution(mesh):
    grp, row, col = (mesh.shape[a] for a in ("grp", "row", "col"))
    fine = Mesh(mesh.devices.reshape(grp, row // 2, 2, col), ("grp", "far", "near", "col"))
    tokens = P(("grp", "far", "near"), "col")
    placed = (tokens, tokens, tokens, P(("col", "far", "near"), None), P("col"), P("col"), P("col", None), P("col", None))
    return jax.shard_map(on_device, mesh=fine, in_specs=placed, out_specs=tokens, check_vma=False)
```

```python
import functools

import jax
import jax.numpy as jnp
from jax import lax
from jax.experimental import pallas as pl
from jax.experimental.pallas import tpu as pltpu
from jax.sharding import Mesh
from jax.sharding import PartitionSpec as P

HD = 128
WINDOW = 1024
RANK = 64

query_scale = 168.0 ** (-0.5)
norm_eps = 1e-06
rope_base = 10000.0
log2_e = 1.4426950408889634

TILE = 896
VMEM_LIMIT = 32 * 2**20

NT = (((1,), (1,)), ((), ()))


def rope_tables(first_position, count):
    half_dim = HD // 2
    inverse = jnp.exp(
        -(2.0 * jnp.arange(half_dim, dtype=jnp.float32) / HD) * jnp.log(jnp.float32(rope_base))
    )
    positions = (first_position + jnp.arange(count, dtype=jnp.int32)).astype(jnp.float32)
    angles = positions[:, None] * inverse[None, :]
    cosine, sine = jnp.cos(angles), jnp.sin(angles)
    return jnp.concatenate([cosine, cosine], 1), jnp.concatenate([-sine, sine], 1)


def attend_kernel(tok, group, direct, row_ref, q_ref, k0, k1, k2, v0, v1, v2, cos_ref, sin_ref, out_ref):
    tile = 256

    def turned(field, at):
        wide = field.astype(jnp.float32)
        cos, sin = cos_ref[at : at + tok, :], sin_ref[at : at + tok, :]
        return (wide * cos + pltpu.roll(wide, HD // 2, 1) * sin).astype(jnp.bfloat16)

    row = row_ref[0]
    bias0 = jnp.where(row >= 2, 0.0, -1e30).astype(jnp.float32)
    bias1 = jnp.where(row >= 1, 0.0, -1e30).astype(jnp.float32)
    key0, key1, key2 = turned(k0[...], 0), turned(k1[...], tok), turned(k2[...], 2 * tok)
    heads = [turned(q_ref[:, h * HD : (h + 1) * HD], 2 * tok) for h in range(group)]
    scale = query_scale * log2_e
    stacked = group * tile
    inner = lax.rem(lax.broadcasted_iota(jnp.int32, (stacked, tile), 0), tile)
    newer = lax.broadcasted_iota(jnp.int32, (stacked, tile), 1) > inner

    def dot_nt(a, b):
        return lax.dot_general(a, b, NT, preferred_element_type=jnp.float32)

    def dot(a, b):
        return jnp.dot(a, b, preferred_element_type=jnp.float32)

    for t in range(tok // tile):
        lo, hi = t * tile, (t + 1) * tile
        query = jnp.concatenate([h[lo:hi] for h in heads], 0)
        parts = [(dot_nt(query, key1) + bias1, v1[...])]
        if hi < tok:
            parts.append((dot_nt(query, key0[hi:]) + bias0, v0[hi:, :]))
        if lo > 0:
            parts.append((dot_nt(query, key2[:lo]), v2[:lo, :]))
        mixed = jnp.where(newer, dot_nt(query, key0[lo:hi]) + bias0, dot_nt(query, key2[lo:hi]))
        top = jnp.max(mixed, axis=1, keepdims=True)
        for part, _ in parts:
            top = jnp.maximum(top, jnp.max(part, axis=1, keepdims=True))
        top = top * scale
        weights = jnp.exp2(mixed * scale - top)
        total = jnp.sum(weights, axis=1, keepdims=True)
        older = jnp.where(newer, weights, 0.0)
        result = dot(older.astype(jnp.bfloat16), v0[lo:hi, :])
        result += dot((weights - older).astype(jnp.bfloat16), v2[lo:hi, :])
        for part, value in parts:
            weights = jnp.exp2(part * scale - top)
            total += jnp.sum(weights, axis=1, keepdims=True)
            result += dot(weights.astype(jnp.bfloat16), value)
        result = (result / total).astype(jnp.bfloat16)
        for h in range(group):
            block = result[h * tile : (h + 1) * tile]
            if direct:
                out_ref[h, lo:hi, :] = block
            else:
                out_ref[lo:hi, h * HD : (h + 1) * HD] = block


def attend(row, queries, key_blocks, val_blocks, cos, sin, direct, first=0, count=None):
    tok, kv_local = queries.shape[0], key_blocks[-1].shape[1] // HD
    group = queries.shape[1] // HD // kv_local
    count = kv_local if count is None else count
    head_block = pl.BlockSpec((tok, HD), lambda g, r: (0, g + first))
    table = pl.BlockSpec((3 * tok, HD), lambda g, r: (0, 0))
    if direct:
        out_shape = (count * group, tok, HD)
        out_spec = pl.BlockSpec((group, tok, HD), lambda g, r: (g, 0, 0))
    else:
        out_shape = queries.shape
        out_spec = pl.BlockSpec((tok, group * HD), lambda g, r: (0, g))
    heads = count * group
    return pl.pallas_call(
        functools.partial(attend_kernel, tok, group, direct),
        grid_spec=pltpu.PrefetchScalarGridSpec(
            num_scalar_prefetch=1,
            grid=(count,),
            in_specs=[pl.BlockSpec((tok, group * HD), lambda g, r: (0, g + first))] + [head_block] * 3
            + [
                pl.BlockSpec((tok, HD), lambda g, r, skip=v.shape[1] // HD - kv_local: (0, g + first + skip))
                for v in val_blocks
            ]
            + [table] * 2,
            out_specs=out_spec,
        ),
        out_shape=jax.ShapeDtypeStruct(out_shape, jnp.bfloat16),
        compiler_params=pltpu.CompilerParams(vmem_limit_bytes=VMEM_LIMIT),
        cost_estimate=pl.CostEstimate(
            flops=4 * heads * tok * 10 * tok * HD, bytes_accessed=6 * 2**20, transcendentals=heads * tok * 2 * tok
        ),
    )(row, queries, *key_blocks, *val_blocks, cos, sin)


def ring_place(position, size):
    return jnp.where(position <= size // 2, jnp.maximum(2 * position - 1, 0), 2 * (size - position))


def ring_position(place, size):
    return jnp.where(place % 2 == 1, (place + 1) // 2, (size - place // 2) % size)


def slot_of(kind, step, where_ref, slots):
    if kind is None:
        return step * slots
    is_mine, far, near, outer = where_ref[0], where_ref[1], where_ref[2], where_ref[3]
    from_far = ring_place((ring_position(far, outer) - step + outer) % outer, outer)
    side = near if kind in ("main", "across") else 1 - near
    other = 1 - is_mine if kind in ("main", "beside") else is_mine
    return other * slots + from_far * 2 + side


def gather_heads(kinds, where_ref, sources, heads, sems):
    slots = sources[0].shape[0]
    depth = sources[0].shape[2]
    places = [heads.at[:, n * depth : (n + 1) * depth] for n in range(len(kinds))]
    for n, (kind, k) in enumerate(kinds):
        slot = slot_of(kind, k, where_ref, slots * len(sources) // 2)
        for i, source in enumerate(sources):

            @pl.when((slot >= i * slots) & (slot < (i + 1) * slots))
            def _():
                pltpu.make_async_copy(source.at[slot - i * slots], places[n], sems.at[n]).start()

    for n, place in enumerate(places):
        pltpu.make_async_copy(sources[0].at[0], place, sems.at[n]).wait()


def split_in(in_ref):
    high = in_ref[...].astype(jnp.bfloat16)
    low = (in_ref[...] - high.astype(jnp.float32)).astype(jnp.bfloat16)
    return jnp.concatenate([high, low], 0)


def coded(field, in_parts):
    code = lax.dot_general(field.astype(jnp.bfloat16), in_parts, NT, preferred_element_type=jnp.float32)
    return code + pltpu.roll(code, RANK, 1)


def project_kernel(kinds, late_kinds, sources, where_ref, *refs):
    sources, refs = refs[:sources], refs[sources:]
    weights, refs = refs[: len(kinds)], refs[len(kinds) :]
    in_ref, mean_ref, partial_ref, late_ref, code_ref, heads, sems, late_sems, blocks, block_sems = refs
    step = pl.program_id(0)
    steps = pl.num_programs(0)
    depth = weights[0].shape[0]

    def columns_of(at, act):
        slot = lax.rem(at, 2)
        for n, piece in enumerate(weights):
            source = piece.at[:, pl.ds(pl.multiple_of(at * TILE, TILE), TILE)]
            act(pltpu.make_async_copy(source, blocks.at[slot, n * depth : (n + 1) * depth], block_sems.at[slot, n]))

    @pl.when(step == 0)
    def _():
        columns_of(step, lambda copy: copy.start())

    @pl.when(step + 1 < steps)
    def _():
        columns_of(step + 1, lambda copy: copy.start())

    @pl.when(step == 0)
    def _():
        gather_heads(kinds, where_ref, sources, heads, sems)
        gather_heads(late_kinds, where_ref, sources, late_ref, late_sems)

    mean = jnp.broadcast_to(mean_ref[...], (8, mean_ref.shape[1]))
    mean_high = mean.astype(jnp.bfloat16).astype(jnp.float32)
    in_parts = split_in(in_ref)
    code = coded(mean_high, in_parts) + coded(mean - mean_high, in_parts)

    @pl.when(step == 0)
    def _():
        code_ref[...] = code

    @pl.when(step > 0)
    def _():
        code_ref[...] += code

    columns_of(step, lambda copy: copy.wait())
    partial_ref[...] = jnp.dot(heads[...], blocks[lax.rem(step, 2)], preferred_element_type=jnp.float32)


def project(where, kinds, late_kinds, sources, weights, erase_in, mean):
    tok = sources[0].shape[1]
    depth, width = weights[0].shape
    count, late = len(kinds), len(late_kinds)
    in_hbm = pl.BlockSpec(memory_space=pltpu.HBM)
    columns = lambda rows: pl.BlockSpec((rows, TILE), lambda j, r: (0, j))
    whole = lambda *shape: pl.BlockSpec(shape, lambda j, r: (0, 0))
    return pl.pallas_call(
        functools.partial(project_kernel, kinds, late_kinds, len(sources)),
        grid_spec=pltpu.PrefetchScalarGridSpec(
            num_scalar_prefetch=1,
            grid=(width // TILE,),
            in_specs=[in_hbm] * (len(sources) + count) + [columns(RANK), columns(1)],
            out_specs=[columns(tok), whole(tok, late * depth), whole(8, 2 * RANK)],
            scratch_shapes=[
                pltpu.VMEM((tok, count * depth), jnp.bfloat16),
                pltpu.SemaphoreType.DMA((count,)),
                pltpu.SemaphoreType.DMA((late,)),
                pltpu.VMEM((2, count * depth, TILE), jnp.bfloat16),
                pltpu.SemaphoreType.DMA((2, count)),
            ],
        ),
        out_shape=[
            jax.ShapeDtypeStruct((tok, width), jnp.float32),
            jax.ShapeDtypeStruct((tok, late * depth), jnp.bfloat16),
            jax.ShapeDtypeStruct((8, 2 * RANK), jnp.float32),
        ],
        compiler_params=pltpu.CompilerParams(vmem_limit_bytes=VMEM_LIMIT),
        cost_estimate=pl.CostEstimate(
            flops=2 * tok * count * depth * width, bytes_accessed=2 * count * depth * width, transcendentals=0
        ),
    )(where, *sources, *weights, erase_in, mean)


def close_kernel(heads_ref, *refs):
    weights, (partial_ref, mean_code_ref, gain_ref, in_ref, hidden_ref, stat_ref) = refs[:-6], refs[-6:]
    step = pl.program_id(0)
    tok = hidden_ref.shape[0]
    weight = jnp.concatenate([w[...] for w in weights], 0)
    total = partial_ref[...] + jnp.dot(heads_ref[...], weight, preferred_element_type=jnp.float32)
    hidden_ref[...] = total
    code = coded(total * gain_ref[...], split_in(in_ref))
    square = jnp.sum(total * total, axis=1, keepdims=True)
    lane = lax.broadcasted_iota(jnp.int32, code.shape, 1)
    stat = jnp.where(lane < RANK, code, square)

    @pl.when(step == 0)
    def _():
        stat_ref[:tok, :] = stat
        stat_ref[tok:, :] = mean_code_ref[...]

    @pl.when(step > 0)
    def _():
        stat_ref[:tok, :] += stat


def close(heads, weights, partial, mean_code, gain, erase_in):
    tok, width = partial.shape
    depth = weights[0].shape[0]
    count = len(weights)
    columns = lambda rows: pl.BlockSpec((rows, TILE), lambda j: (0, j))
    whole = lambda *shape: pl.BlockSpec(shape, lambda j: (0, 0))
    return pl.pallas_call(
        close_kernel,
        grid=(width // TILE,),
        in_specs=[whole(*heads.shape)]
        + [columns(depth)] * count
        + [columns(tok), whole(*mean_code.shape), columns(1), columns(RANK)],
        out_specs=[columns(tok), whole(tok + 8, 2 * RANK)],
        out_shape=[
            jax.ShapeDtypeStruct((tok, width), jnp.float32),
            jax.ShapeDtypeStruct((tok + 8, 2 * RANK), jnp.float32),
        ],
        compiler_params=pltpu.CompilerParams(vmem_limit_bytes=VMEM_LIMIT),
        cost_estimate=pl.CostEstimate(
            flops=2 * tok * count * depth * width, bytes_accessed=2 * count * depth * width, transcendentals=0
        ),
    )(heads, *weights, partial, mean_code, gain, erase_in)


def finish_kernel(model_width, own_ref, other_ref, gain_ref, out_ref, hidden_ref, erased_ref, tiles, sems):
    tok, width = hidden_ref.shape
    stat = own_ref[:tok, :] + other_ref[:tok, :]
    mean_code = own_ref[tok : tok + 1, :] + other_ref[tok : tok + 1, :]
    inv_rms = lax.rsqrt(stat[:, RANK : RANK + 1] / model_width + norm_eps)
    lane = lax.broadcasted_iota(jnp.int32, stat.shape, 1)
    code = jnp.where(lane < RANK, stat * inv_rms - mean_code, 0.0)
    high = code.astype(jnp.bfloat16).astype(jnp.float32)
    low = code - high
    packed = jnp.concatenate([high + pltpu.roll(low, RANK, 1), high], 1).astype(jnp.bfloat16)
    copies = []
    for n, at in enumerate(range(0, width, TILE)):
        here = slice(at, at + TILE)
        out_high = out_ref[:, here].astype(jnp.bfloat16)
        out_low = (out_ref[:, here] - out_high.astype(jnp.float32)).astype(jnp.bfloat16)
        out_parts = jnp.concatenate([out_high, out_high, out_low, jnp.zeros_like(out_low)], 0)
        removed = jnp.dot(packed, out_parts, preferred_element_type=jnp.float32)
        normed = hidden_ref[:, here] * inv_rms * gain_ref[:, here]
        tiles[:, here] = (normed - removed).astype(jnp.bfloat16)
        copies.append(pltpu.make_async_copy(tiles.at[:, here], erased_ref.at[:, here], sems.at[n]))
        copies[-1].start()
    for copy in copies:
        copy.wait()


def finish(model_width, stat, stat_other, gain, erase_out, hidden):
    tok, width = hidden.shape
    in_vmem = pl.BlockSpec(memory_space=pltpu.VMEM)
    return pl.pallas_call(
        functools.partial(finish_kernel, model_width),
        in_specs=[in_vmem] * 5,
        out_specs=pl.BlockSpec(memory_space=pltpu.HBM),
        out_shape=jax.ShapeDtypeStruct((tok, width), jnp.bfloat16),
        scratch_shapes=[pltpu.VMEM((tok, width), jnp.bfloat16), pltpu.SemaphoreType.DMA((width // TILE,))],
        compiler_params=pltpu.CompilerParams(vmem_limit_bytes=VMEM_LIMIT),
        cost_estimate=pl.CostEstimate(
            flops=2 * tok * 256 * width, bytes_accessed=6 * tok * width, transcendentals=0
        ),
    )(stat, stat_other, gain, erase_out, hidden)


def swapped(block, axis):
    return lax.ppermute(block, axis, [(0, 1), (1, 0)])


def ring_order(size):
    return list(range(0, 1)) + list(range(1, size, 2)) + [i for i in range(size - 1, 0, -1) if i % 2 == 0]


def on_device(queries, keys, values, out_proj, post_gain, mean_vec, erase_in, erase_out):
    tok = queries.shape[0]
    outer, inner = lax.axis_size("far"), lax.axis_size("near")
    grp, far, near, col = (lax.axis_index(a) for a in ("grp", "far", "near", "col"))
    row = far * inner + near
    depth, model_width = out_proj.shape
    width = model_width // 2
    kv_local = keys.shape[1] // HD
    heads = queries.shape[1] // HD
    direct = depth == HD and outer * inner == heads and outer == 4

    ahead = [(i, i + 1) for i in range(outer - 1)]
    from_behind = lambda block: lax.ppermute(block, "far", ahead)
    hold = lax.optimization_barrier

    def for_next(own, second):
        return swapped(jnp.where(near == 0, own, second), "near")

    def after(block, *earlier):
        return hold((block, earlier))[0]

    theirs = swapped(lax.dynamic_slice_in_dim(out_proj, (1 - col) * width, width, 1), "col")
    mine = lax.dynamic_slice_in_dim(out_proj, col * width, width, 1)
    gain, mean = post_gain[None, :], mean_vec[None, :]
    erase_in, erase_out = erase_in.T, erase_out.T
    is_mine = grp == col
    where = jnp.stack([is_mine.astype(jnp.int32), far, near, jnp.int32(outer)])

    if direct:
        order = ring_order(outer)
        hops = [(order[i], order[(i + 1) % outer]) for i in range(outer)]
        ring = lambda block: lax.ppermute(block, "far", hops)
        beyond = lambda block: swapped(block, "near")
        facing = lambda block: swapped(block, "grp")
        main, beside, across, corner = ({} for _ in range(4))
        main[0] = jnp.where(is_mine, mine, theirs)
        across[0] = jnp.where(is_mine, theirs, mine)
        beside[0] = beyond(main[0])
        second_keys = from_behind(after(keys, main[0]))
        second_values = from_behind(after(values, main[0]))
        first_keys = for_next(keys, after(second_keys, beside[0]))
        corner[0] = facing(beside[0])
        main[1] = ring(after(main[0], second_values))
        first_values = for_next(values, after(second_values, first_keys))
        cos, sin = rope_tables((after(row, beside[0]) - 2) * tok, 3 * tok)
        main[1], first_keys, first_values, corner[0], cos, sin, where = hold(
            (main[1], first_keys, first_values, corner[0], cos, sin, where)
        )
        main[2], beside[1], across[1] = ring(main[1]), beyond(main[1]), facing(main[1])
        attended = attend(
            row[None], queries, (second_keys, first_keys, keys), (second_values, first_values, values), cos, sin, True
        )
        main[2], beside[1], across[1], attended = hold((main[2], beside[1], across[1], attended))
        main[3], beside[2], corner[1] = ring(main[2]), beyond(main[2]), facing(beside[1])
        main[3], beside[2], corner[1], across[1], attended = hold((main[3], beside[2], corner[1], across[1], attended))
        across[2], beside[3], corner[2] = ring(across[1]), beyond(main[3]), facing(beside[2])
        across[2], beside[3], corner[2], attended = hold((across[2], beside[3], corner[2], attended))
        across[3], corner[3] = ring(across[2]), facing(beside[3])
        attended, att_other = [attended], [swapped(attended, "col")]
        weights, kinds, late, late_kinds = [], [], [], []
        for name, pieces in (("main", main), ("beside", beside), ("across", across), ("corner", corner)):
            for k in range(outer):
                is_late = k == 3 and name in ("across", "corner")
                (late if is_late else weights).append(pieces[k])
                (late_kinds if is_late else kinds).append((name, k))
    else:
        second_keys, second_values = from_behind(keys), from_behind(values)
        first_keys, first_values = for_next(keys, second_keys), for_next(values, second_values)
        cos, sin = rope_tables((row - 2) * tok, 3 * tok)
        attended = attend(
            row[None], queries, (second_keys, first_keys, keys), (second_values, first_values, values), cos, sin, False
        )
        attended = [attended[None]]
        att_other = [swapped(attended[0], "col")]
        weights, late = ([lax.all_gather(w, ("far", "near"), axis=0, tiled=True)] for w in (mine, theirs))
        kinds, late_kinds = [(None, 0)], [(None, 1)]

    partial, late_heads, mean_code = project(where, kinds, late_kinds, attended + att_other, weights, erase_in, mean)
    hidden, stat = close(late_heads, late, partial, mean_code, gain, erase_in)
    return finish(model_width, stat, swapped(stat, "col"), gain, erase_out, hidden)


def solution(mesh):
    grp, row, col = (mesh.shape[a] for a in ("grp", "row", "col"))
    fine = Mesh(mesh.devices.reshape(grp, row // 2, 2, col), ("grp", "far", "near", "col"))
    tokens = P(("grp", "far", "near"), "col")
    placed = (tokens, tokens, tokens, P(("col", "far", "near"), None), P("col"), P("col"), P("col", None), P("col", None))
    return jax.shard_map(on_device, mesh=fine, in_specs=placed, out_specs=tokens, check_vma=False)
```

```python
import functools

import jax
import jax.numpy as jnp
from jax import lax
from jax.experimental import pallas as pl
from jax.experimental.pallas import tpu as pltpu
from jax.sharding import Mesh
from jax.sharding import PartitionSpec as P

HD = 128
WINDOW = 1024
RANK = 64

query_scale = 168.0 ** (-0.5)
norm_eps = 1e-06
rope_base = 10000.0
log2_e = 1.4426950408889634

TILE = 896
VMEM_LIMIT = 32 * 2**20

NT = (((1,), (1,)), ((), ()))


def rope_tables(first_position, count):
    half_dim = HD // 2
    inverse = jnp.exp(
        -(2.0 * jnp.arange(half_dim, dtype=jnp.float32) / HD) * jnp.log(jnp.float32(rope_base))
    )
    positions = (first_position + jnp.arange(count, dtype=jnp.int32)).astype(jnp.float32)
    angles = positions[:, None] * inverse[None, :]
    cosine, sine = jnp.cos(angles), jnp.sin(angles)
    return jnp.concatenate([cosine, cosine], 1), jnp.concatenate([-sine, sine], 1)


def attend_kernel(tok, group, direct, row_ref, q_ref, k0, k1, k2, v0, v1, v2, cos_ref, sin_ref, out_ref):
    tile = 256

    def turned(field, at):
        wide = field.astype(jnp.float32)
        cos, sin = cos_ref[at : at + tok, :], sin_ref[at : at + tok, :]
        return (wide * cos + pltpu.roll(wide, HD // 2, 1) * sin).astype(jnp.bfloat16)

    row = row_ref[0]
    bias0 = jnp.where(row >= 2, 0.0, -1e30).astype(jnp.float32)
    bias1 = jnp.where(row >= 1, 0.0, -1e30).astype(jnp.float32)
    key0, key1, key2 = turned(k0[...], 0), turned(k1[...], tok), turned(k2[...], 2 * tok)
    heads = [turned(q_ref[:, h * HD : (h + 1) * HD], 2 * tok) for h in range(group)]
    scale = query_scale * log2_e
    stacked = group * tile
    inner = lax.rem(lax.broadcasted_iota(jnp.int32, (stacked, tile), 0), tile)
    newer = lax.broadcasted_iota(jnp.int32, (stacked, tile), 1) > inner

    def dot_nt(a, b):
        return lax.dot_general(a, b, NT, preferred_element_type=jnp.float32)

    def dot(a, b):
        return jnp.dot(a, b, preferred_element_type=jnp.float32)

    for t in range(tok // tile):
        lo, hi = t * tile, (t + 1) * tile
        query = jnp.concatenate([h[lo:hi] for h in heads], 0)
        parts = [(dot_nt(query, key1) + bias1, v1[...])]
        if hi < tok:
            parts.append((dot_nt(query, key0[hi:]) + bias0, v0[hi:, :]))
        if lo > 0:
            parts.append((dot_nt(query, key2[:lo]), v2[:lo, :]))
        mixed = jnp.where(newer, dot_nt(query, key0[lo:hi]) + bias0, dot_nt(query, key2[lo:hi]))
        top = jnp.max(mixed, axis=1, keepdims=True)
        for part, _ in parts:
            top = jnp.maximum(top, jnp.max(part, axis=1, keepdims=True))
        top = top * scale
        weights = jnp.exp2(mixed * scale - top)
        total = jnp.sum(weights, axis=1, keepdims=True)
        older = jnp.where(newer, weights, 0.0)
        result = dot(older.astype(jnp.bfloat16), v0[lo:hi, :])
        result += dot((weights - older).astype(jnp.bfloat16), v2[lo:hi, :])
        for part, value in parts:
            weights = jnp.exp2(part * scale - top)
            total += jnp.sum(weights, axis=1, keepdims=True)
            result += dot(weights.astype(jnp.bfloat16), value)
        result = (result / total).astype(jnp.bfloat16)
        for h in range(group):
            block = result[h * tile : (h + 1) * tile]
            if direct:
                out_ref[h, lo:hi, :] = block
            else:
                out_ref[lo:hi, h * HD : (h + 1) * HD] = block


def attend(row, queries, key_blocks, val_blocks, cos, sin, direct, first=0, count=None):
    tok, kv_local = queries.shape[0], key_blocks[-1].shape[1] // HD
    group = queries.shape[1] // HD // kv_local
    count = kv_local if count is None else count
    head_block = pl.BlockSpec((tok, HD), lambda g, r: (0, g + first))
    table = pl.BlockSpec((3 * tok, HD), lambda g, r: (0, 0))
    if direct:
        out_shape = (count * group, tok, HD)
        out_spec = pl.BlockSpec((group, tok, HD), lambda g, r: (g, 0, 0))
    else:
        out_shape = queries.shape
        out_spec = pl.BlockSpec((tok, group * HD), lambda g, r: (0, g))
    heads = count * group
    return pl.pallas_call(
        functools.partial(attend_kernel, tok, group, direct),
        grid_spec=pltpu.PrefetchScalarGridSpec(
            num_scalar_prefetch=1,
            grid=(count,),
            in_specs=[pl.BlockSpec((tok, group * HD), lambda g, r: (0, g + first))] + [head_block] * 3
            + [
                pl.BlockSpec((tok, HD), lambda g, r, skip=v.shape[1] // HD - kv_local: (0, g + first + skip))
                for v in val_blocks
            ]
            + [table] * 2,
            out_specs=out_spec,
        ),
        out_shape=jax.ShapeDtypeStruct(out_shape, jnp.bfloat16),
        compiler_params=pltpu.CompilerParams(vmem_limit_bytes=VMEM_LIMIT),
        cost_estimate=pl.CostEstimate(
            flops=4 * heads * tok * 10 * tok * HD, bytes_accessed=6 * 2**20, transcendentals=heads * tok * 2 * tok
        ),
    )(row, queries, *key_blocks, *val_blocks, cos, sin)


def ring_place(position, size):
    return jnp.where(position <= size // 2, jnp.maximum(2 * position - 1, 0), 2 * (size - position))


def ring_position(place, size):
    return jnp.where(place % 2 == 1, (place + 1) // 2, (size - place // 2) % size)


def slot_of(kind, step, where_ref, slots):
    if kind is None:
        return step * slots
    is_mine, far, near, outer = where_ref[0], where_ref[1], where_ref[2], where_ref[3]
    from_far = ring_place((ring_position(far, outer) - step + outer) % outer, outer)
    side = near if kind in ("main", "across") else 1 - near
    other = 1 - is_mine if kind in ("main", "beside") else is_mine
    return other * slots + from_far * 2 + side


def gather_heads(kinds, where_ref, sources, heads, sems):
    slots = sources[0].shape[0]
    depth = sources[0].shape[2]
    ends = [sum(source.shape[0] for source in sources[: i + 1]) for i in range(len(sources))]
    places = [heads.at[:, n * depth : (n + 1) * depth] for n in range(len(kinds))]
    for n, (kind, k) in enumerate(kinds):
        slot = slot_of(kind, k, where_ref, slots)
        for source, end in zip(sources, ends):
            begin = end - source.shape[0]

            @pl.when((slot >= begin) & (slot < end))
            def _():
                pltpu.make_async_copy(source.at[slot - begin], places[n], sems.at[n]).start()

    for n, place in enumerate(places):
        pltpu.make_async_copy(sources[0].at[0], place, sems.at[n]).wait()


def split_in(in_ref):
    high = in_ref[...].astype(jnp.bfloat16)
    low = (in_ref[...] - high.astype(jnp.float32)).astype(jnp.bfloat16)
    return jnp.concatenate([high, low], 0)


def coded(field, in_parts):
    code = lax.dot_general(field.astype(jnp.bfloat16), in_parts, NT, preferred_element_type=jnp.float32)
    return code + pltpu.roll(code, RANK, 1)


def project_kernel(kinds, late_kinds, sources, where_ref, *refs):
    sources, refs = refs[:sources], refs[sources:]
    weights, refs = refs[: len(kinds)], refs[len(kinds) :]
    in_ref, mean_ref, partial_ref, late_ref, code_ref, heads, sems, late_sems, blocks, block_sems = refs
    step = pl.program_id(0)
    steps = pl.num_programs(0)
    depth = weights[0].shape[0]

    def columns_of(at, act):
        slot = lax.rem(at, 2)
        for n, piece in enumerate(weights):
            source = piece.at[:, pl.ds(pl.multiple_of(at * TILE, TILE), TILE)]
            act(pltpu.make_async_copy(source, blocks.at[slot, n * depth : (n + 1) * depth], block_sems.at[slot, n]))

    @pl.when(step == 0)
    def _():
        columns_of(step, lambda copy: copy.start())

    @pl.when(step + 1 < steps)
    def _():
        columns_of(step + 1, lambda copy: copy.start())

    @pl.when(step == 0)
    def _():
        gather_heads(kinds, where_ref, sources, heads, sems)
        gather_heads(late_kinds, where_ref, sources, late_ref, late_sems)

    mean = jnp.broadcast_to(mean_ref[...], (8, mean_ref.shape[1]))
    mean_high = mean.astype(jnp.bfloat16).astype(jnp.float32)
    in_parts = split_in(in_ref)
    code = coded(mean_high, in_parts) + coded(mean - mean_high, in_parts)

    @pl.when(step == 0)
    def _():
        code_ref[...] = code

    @pl.when(step > 0)
    def _():
        code_ref[...] += code

    columns_of(step, lambda copy: copy.wait())
    partial_ref[...] = jnp.dot(heads[...], blocks[lax.rem(step, 2)], preferred_element_type=jnp.float32)


def project(where, kinds, late_kinds, sources, weights, erase_in, mean):
    tok = sources[0].shape[1]
    depth, width = weights[0].shape
    count, late = len(kinds), len(late_kinds)
    in_hbm = pl.BlockSpec(memory_space=pltpu.HBM)
    columns = lambda rows: pl.BlockSpec((rows, TILE), lambda j, r: (0, j))
    whole = lambda *shape: pl.BlockSpec(shape, lambda j, r: (0, 0))
    return pl.pallas_call(
        functools.partial(project_kernel, kinds, late_kinds, len(sources)),
        grid_spec=pltpu.PrefetchScalarGridSpec(
            num_scalar_prefetch=1,
            grid=(width // TILE,),
            in_specs=[in_hbm] * (len(sources) + count) + [columns(RANK), columns(1)],
            out_specs=[columns(tok), whole(tok, late * depth), whole(8, 2 * RANK)],
            scratch_shapes=[
                pltpu.VMEM((tok, count * depth), jnp.bfloat16),
                pltpu.SemaphoreType.DMA((count,)),
                pltpu.SemaphoreType.DMA((late,)),
                pltpu.VMEM((2, count * depth, TILE), jnp.bfloat16),
                pltpu.SemaphoreType.DMA((2, count)),
            ],
        ),
        out_shape=[
            jax.ShapeDtypeStruct((tok, width), jnp.float32),
            jax.ShapeDtypeStruct((tok, late * depth), jnp.bfloat16),
            jax.ShapeDtypeStruct((8, 2 * RANK), jnp.float32),
        ],
        compiler_params=pltpu.CompilerParams(vmem_limit_bytes=VMEM_LIMIT),
        cost_estimate=pl.CostEstimate(
            flops=tok * depth * width, bytes_accessed=depth * width, transcendentals=0
        ),
    )(where, *sources, *weights, erase_in, mean)


def close_kernel(heads_ref, *refs):
    weights, (partial_ref, mean_code_ref, gain_ref, in_ref, hidden_ref, stat_ref) = refs[:-6], refs[-6:]
    step = pl.program_id(0)
    tok = hidden_ref.shape[0]
    weight = jnp.concatenate([w[...] for w in weights], 0)
    total = partial_ref[...] + jnp.dot(heads_ref[...], weight, preferred_element_type=jnp.float32)
    hidden_ref[...] = total
    code = coded(total * gain_ref[...], split_in(in_ref))
    square = jnp.sum(total * total, axis=1, keepdims=True)
    lane = lax.broadcasted_iota(jnp.int32, code.shape, 1)
    stat = jnp.where(lane < RANK, code, square)

    @pl.when(step == 0)
    def _():
        stat_ref[:tok, :] = stat
        stat_ref[tok:, :] = mean_code_ref[...]

    @pl.when(step > 0)
    def _():
        stat_ref[:tok, :] += stat


def close(heads, weights, partial, mean_code, gain, erase_in):
    tok, width = partial.shape
    depth = weights[0].shape[0]
    count = len(weights)
    columns = lambda rows: pl.BlockSpec((rows, TILE), lambda j: (0, j))
    whole = lambda *shape: pl.BlockSpec(shape, lambda j: (0, 0))
    return pl.pallas_call(
        close_kernel,
        grid=(width // TILE,),
        in_specs=[whole(*heads.shape)]
        + [columns(depth)] * count
        + [columns(tok), whole(*mean_code.shape), columns(1), columns(RANK)],
        out_specs=[columns(tok), whole(tok + 8, 2 * RANK)],
        out_shape=[
            jax.ShapeDtypeStruct((tok, width), jnp.float32),
            jax.ShapeDtypeStruct((tok + 8, 2 * RANK), jnp.float32),
        ],
        compiler_params=pltpu.CompilerParams(vmem_limit_bytes=VMEM_LIMIT),
        cost_estimate=pl.CostEstimate(
            flops=2 * tok * count * depth * width, bytes_accessed=2 * count * depth * width, transcendentals=0
        ),
    )(heads, *weights, partial, mean_code, gain, erase_in)


def finish_kernel(model_width, own_ref, other_ref, gain_ref, out_ref, hidden_ref, erased_ref, tiles, sems):
    tok, width = hidden_ref.shape
    stat = own_ref[:tok, :] + other_ref[:tok, :]
    mean_code = own_ref[tok : tok + 1, :] + other_ref[tok : tok + 1, :]
    inv_rms = lax.rsqrt(stat[:, RANK : RANK + 1] / model_width + norm_eps)
    lane = lax.broadcasted_iota(jnp.int32, stat.shape, 1)
    code = jnp.where(lane < RANK, stat * inv_rms - mean_code, 0.0)
    high = code.astype(jnp.bfloat16).astype(jnp.float32)
    low = code - high
    packed = jnp.concatenate([high + pltpu.roll(low, RANK, 1), high], 1).astype(jnp.bfloat16)
    copies = []
    for n, at in enumerate(range(0, width, TILE)):
        here = slice(at, at + TILE)
        out_high = out_ref[:, here].astype(jnp.bfloat16)
        out_low = (out_ref[:, here] - out_high.astype(jnp.float32)).astype(jnp.bfloat16)
        out_parts = jnp.concatenate([out_high, out_high, out_low, jnp.zeros_like(out_low)], 0)
        removed = jnp.dot(packed, out_parts, preferred_element_type=jnp.float32)
        normed = hidden_ref[:, here] * inv_rms * gain_ref[:, here]
        tiles[:, here] = (normed - removed).astype(jnp.bfloat16)
        copies.append(pltpu.make_async_copy(tiles.at[:, here], erased_ref.at[:, here], sems.at[n]))
        copies[-1].start()
    for copy in copies:
        copy.wait()


def finish(model_width, stat, stat_other, gain, erase_out, hidden):
    tok, width = hidden.shape
    in_vmem = pl.BlockSpec(memory_space=pltpu.VMEM)
    return pl.pallas_call(
        functools.partial(finish_kernel, model_width),
        in_specs=[in_vmem] * 5,
        out_specs=pl.BlockSpec(memory_space=pltpu.HBM),
        out_shape=jax.ShapeDtypeStruct((tok, width), jnp.bfloat16),
        scratch_shapes=[pltpu.VMEM((tok, width), jnp.bfloat16), pltpu.SemaphoreType.DMA((width // TILE,))],
        compiler_params=pltpu.CompilerParams(vmem_limit_bytes=VMEM_LIMIT),
        cost_estimate=pl.CostEstimate(
            flops=2 * tok * 256 * width, bytes_accessed=6 * tok * width, transcendentals=0
        ),
    )(stat, stat_other, gain, erase_out, hidden)


def swapped(block, axis):
    return lax.ppermute(block, axis, [(0, 1), (1, 0)])


def ring_order(size):
    return list(range(0, 1)) + list(range(1, size, 2)) + [i for i in range(size - 1, 0, -1) if i % 2 == 0]


def on_device(queries, keys, values, out_proj, post_gain, mean_vec, erase_in, erase_out):
    tok = queries.shape[0]
    outer, inner = lax.axis_size("far"), lax.axis_size("near")
    grp, far, near, col = (lax.axis_index(a) for a in ("grp", "far", "near", "col"))
    row = far * inner + near
    depth, model_width = out_proj.shape
    width = model_width // 2
    kv_local = keys.shape[1] // HD
    heads = queries.shape[1] // HD
    direct = depth == HD and outer * inner == heads and outer == 4

    ahead = [(i, i + 1) for i in range(outer - 1)]
    from_behind = lambda block: lax.ppermute(block, "far", ahead)
    hold = lax.optimization_barrier

    def for_next(own, second):
        return swapped(jnp.where(near == 0, own, second), "near")

    def after(block, *earlier):
        return hold((block, earlier))[0]

    theirs = swapped(lax.dynamic_slice_in_dim(out_proj, (1 - col) * width, width, 1), "col")
    mine = lax.dynamic_slice_in_dim(out_proj, col * width, width, 1)
    gain, mean = post_gain[None, :], mean_vec[None, :]
    erase_in, erase_out = erase_in.T, erase_out.T
    is_mine = grp == col
    where = jnp.stack([is_mine.astype(jnp.int32), far, near, jnp.int32(outer)])

    if direct:
        order = ring_order(outer)
        hops = [(order[i], order[(i + 1) % outer]) for i in range(outer)]
        ring = lambda block: lax.ppermute(block, "far", hops)
        beyond = lambda block: swapped(block, "near")
        facing = lambda block: swapped(block, "grp")
        main, beside, across, corner = ({} for _ in range(4))
        main[0] = jnp.where(is_mine, mine, theirs)
        across[0] = jnp.where(is_mine, theirs, mine)
        beside[0] = beyond(main[0])
        second_keys = from_behind(after(keys, main[0]))
        second_values = from_behind(after(values, main[0]))
        first_keys = for_next(keys, after(second_keys, beside[0]))
        corner[0] = facing(beside[0])
        main[1] = ring(after(main[0], second_values))
        first_values = for_next(values, after(second_values, first_keys))
        cos, sin = rope_tables((after(row, beside[0]) - 2) * tok, 3 * tok)
        main[1], first_keys, first_values, corner[0], cos, sin, where = hold(
            (main[1], first_keys, first_values, corner[0], cos, sin, where)
        )
        main[2], beside[1], across[1] = ring(main[1]), beyond(main[1]), facing(main[1])
        attended = attend(
            row[None], queries, (second_keys, first_keys, keys), (second_values, first_values, values), cos, sin, True
        )
        main[2], beside[1], across[1], attended = hold((main[2], beside[1], across[1], attended))
        main[3], beside[2], corner[1] = ring(main[2]), beyond(main[2]), facing(beside[1])
        main[3], beside[2], corner[1], across[1], attended = hold((main[3], beside[2], corner[1], across[1], attended))
        across[2], beside[3], corner[2] = ring(across[1]), beyond(main[3]), facing(beside[2])
        across[2], beside[3], corner[2], attended = hold((across[2], beside[3], corner[2], attended))
        across[3], corner[3] = ring(across[2]), facing(beside[3])
        some = heads // 2
        attended, att_other = [attended], [swapped(part, "col") for part in (attended[:some], attended[some:])]
        weights, kinds, late, late_kinds = [], [], [], []
        for name, pieces in (("main", main), ("beside", beside), ("across", across), ("corner", corner)):
            for k in range(outer):
                is_late = k == 3 and name in ("across", "corner")
                (late if is_late else weights).append(pieces[k])
                (late_kinds if is_late else kinds).append((name, k))
    else:
        second_keys, second_values = from_behind(keys), from_behind(values)
        first_keys, first_values = for_next(keys, second_keys), for_next(values, second_values)
        cos, sin = rope_tables((row - 2) * tok, 3 * tok)
        attended = attend(
            row[None], queries, (second_keys, first_keys, keys), (second_values, first_values, values), cos, sin, False
        )
        attended = [attended[None]]
        att_other = [swapped(attended[0], "col")]
        weights, late = ([lax.all_gather(w, ("far", "near"), axis=0, tiled=True)] for w in (mine, theirs))
        kinds, late_kinds = [(None, 0)], [(None, 1)]

    partial, late_heads, mean_code = project(where, kinds, late_kinds, attended + att_other, weights, erase_in, mean)
    hidden, stat = close(late_heads, late, partial, mean_code, gain, erase_in)
    return finish(model_width, stat, swapped(stat, "col"), gain, erase_out, hidden)


def solution(mesh):
    grp, row, col = (mesh.shape[a] for a in ("grp", "row", "col"))
    fine = Mesh(mesh.devices.reshape(grp, row // 2, 2, col), ("grp", "far", "near", "col"))
    tokens = P(("grp", "far", "near"), "col")
    placed = (tokens, tokens, tokens, P(("col", "far", "near"), None), P("col"), P("col"), P("col", None), P("col", None))
    return jax.shard_map(on_device, mesh=fine, in_specs=placed, out_specs=tokens, check_vma=False)
```
